32 devices in a mesh: win: 8 (over z, x), ffn: 4 (over y, core).
Axes of the slice: x: 2, y: 2, z: 4, core: 2. Of those that a mesh axis runs over, the one named last changes fastest.
Arguments:
- pillar_feats: float32 [27648, 128], P(('win', 'ffn')), may hold values from -40 to 40
- occupied: int32 [27648], P(('win', 'ffn')), may hold values from 0 to 1, as said below
- shifted_source_rows: int32 [27648], P(('win', 'ffn')), may hold values from 0 to 27647, as said below
- w_vfe: float32 [128, 128], replicated, may hold values from -0.5 to 0.5
- bn_gain: float32 [2, 128], replicated, may hold values from 0.5 to 1.5
- bn_shift: float32 [2, 128], replicated, may hold values from -3 to 3
- query_key_value_weight: float32 [2, 128, 384], replicated, may hold values from -0.75 to 0.75
- attention_output_weight: float32 [2, 128, 128], replicated, may hold values from -1 to 1
- up_weight_matrix: float32 [2, 128, 256], P(None, None, 'ffn'), may hold values from -0.5 to 0.5
- up_bias_rows: float32 [2, 256], P(None, 'ffn'), may hold values from -3 to 3
- down_weight_matrix: float32 [2, 256, 128], P(None, 'ffn'), may hold values from -0.375 to 0.375
- down_bias_rows: float32 [2, 128], replicated, may hold values from -3 to 3
- layernorm_gains: float32 [4, 128], replicated, may hold values from 0.5 to 1.5
- layernorm_offsets: float32 [4, 128], replicated, may hold values from -3 to 3
- cotangent: float32 [27648, 128], P(('win', 'ffn')), may hold values from -6 to 6
Outputs:
- pillars_out: float32 [27648, 128], P(('win', 'ffn'))
- grad_pillar_feats: float32 [27648, 128], P(('win', 'ffn'))
- grad_w_vfe: float32 [128, 128], replicated
- grad_bn_gain: float32 [2, 128], replicated
- grad_bn_shift: float32 [2, 128], replicated
- grad_w_qkv: float32 [2, 128, 384], replicated
- grad_w_out: float32 [2, 128, 128], replicated
- grad_w_in: float32 [2, 128, 256], P(None, None, 'ffn')
- grad_b_in: float32 [2, 256], P(None, 'ffn')
- grad_w_back: float32 [2, 256, 128], P(None, 'ffn')
- grad_b_back: float32 [2, 128], replicated
- grad_ln_gain: float32 [4, 128], replicated
- grad_ln_shift: float32 [4, 128], replicated
The draws below stay inside these ranges and needn't reach their ends.
Inputs may be any that keep to these rules, and one draw needn't show every extreme that they name: Every window of 144 consecutive rows has from 36 to 144 occupied slots; both counts occur in every draw. `shifted_source_rows`: A permutation of the 27648 rows. With g = t // 864, row t takes a regular row from g * 864 + 72 to g * 864 + 935, counted modulo 27648; which of these rows fall into which shifted window is arbitrary.
All inputs are finite; a program needn't handle non-finite values.
Results may differ from the reference program's by a relative error of at most 0.0003.
Values sent between devices are 32-bit elements; how exact they have to be, the bound alone decides.
No kernel may reach another device: no remote copies, remote signals or barrier semaphores. Data moves between devices by JAX's collectives and lax.ppermute only.
A program may use at most 128 MiB of HBM per device.

```python
import math
import jax
import jax.numpy as jnp
from jax import lax

D = 128
HEADS = 8
HID = 256
C_IN = 128
CELLS = 144
WIN_DEV = 6
TOKENS = 27648


def draw_pillar_feats(key, part):
    key = jax.random.fold_in(key, 5)
    first_key, second_key = jax.random.split(key)
    position = jnp.arange(TOKENS, dtype=jnp.float32)[:, None] / TOKENS
    base = jax.random.normal(first_key, (TOKENS, C_IN), jnp.float32)
    offset = 0.5 * jax.random.normal(second_key, (1, C_IN), jnp.float32)
    growth = jnp.exp(1.4 * position)
    return (growth * (base + offset)).astype(jnp.float32)


def draw_occupied(key, part):
    key = jax.random.fold_in(key, 29)
    count_key, order_key, full_key, sparse_key = jax.random.split(key, 4)
    windows = TOKENS // CELLS
    counts = jax.random.randint(count_key, (windows,), CELLS // 4, CELLS + 1)
    full_pick = jax.random.randint(full_key, (), 0, windows)
    sparse_pick = (full_pick + 1 + jax.random.randint(sparse_key, (), 0, windows - 1)) % windows
    window_ids = jnp.arange(windows, dtype=jnp.int32)
    counts = jnp.where(window_ids == full_pick, CELLS, counts)
    counts = jnp.where(window_ids == sparse_pick, CELLS // 4, counts)
    orders = jax.vmap(lambda subkey: jax.random.permutation(subkey, CELLS))(jax.random.split(order_key, windows))
    return (orders < counts[:, None]).astype(jnp.int32).reshape(TOKENS)


def draw_shifted_source_rows(key, part):
    key = jax.random.fold_in(key, 17)
    span = WIN_DEV * CELLS
    groups = TOKENS // span
    orders = jax.vmap(lambda subkey: jax.random.permutation(subkey, span))(jax.random.split(key, groups))
    starts = jnp.arange(groups, dtype=jnp.int32)[:, None] * span + CELLS // 2
    return ((starts + orders.astype(jnp.int32)) % TOKENS).reshape(TOKENS).astype(jnp.int32)


def block_scale(stream_key, extent, pieces, smallest, high):
    def one(dim, blocks):
        steps = jax.random.uniform(jax.random.fold_in(jax.random.fold_in(stream_key, 6), dim), (blocks,), jnp.float32, smallest / len(pieces), high / len(pieces))
        return jnp.repeat(jnp.exp(steps), extent[dim] // blocks).reshape((-1,) + (1,) * (len(extent) - dim - 1))

    gain = one(*pieces[0])
    for cut in pieces[1:]:
        gain = gain * one(*cut)
    return gain


def normal_values(key, dims, scale, limit, pieces=(), held_as=jnp.bfloat16):
    values = jax.random.normal(key, dims, jnp.float32) * scale
    if len(pieces) > 0:
        values = block_scale(key, dims, pieces, -0.22, 0.18) * values
    return jnp.clip(values, min=-limit, max=limit).astype(held_as)


def setup_inputs(seed: int = 0) -> dict:
    splits = jax.random.split(jax.random.key(seed), 16)
    pillar_feats = draw_pillar_feats(jax.random.fold_in(splits[15], 71), 0)
    occupied = draw_occupied(jax.random.fold_in(splits[15], 71), 0)
    shifted_source_rows = draw_shifted_source_rows(jax.random.fold_in(splits[15], 71), 0)
    w_vfe = normal_values(splits[3], (C_IN, D), C_IN ** -0.5, 0.5, (), jnp.float32)
    bn_gain = jnp.clip(1.0 + 0.1 * jax.random.normal(splits[4], (2, D), jnp.float32), 0.5, 1.5)
    bn_shift = normal_values(splits[5], (2, D), 0.5, 3.0, (), jnp.float32)
    query_key_value_weight = normal_values(splits[6], (2, D, 3 * D), (D // 2) ** -0.5, 0.75, (), jnp.float32)
    attention_output_weight = normal_values(splits[7], (2, D, D), (D // 4) ** -0.5, 1.0, (), jnp.float32)
    up_weight_matrix = normal_values(splits[8], (2, D, HID), D ** -0.5, 0.5, ((2, 4),), jnp.float32)
    up_bias_rows = normal_values(splits[9], (2, HID), 0.5, 3.0, ((1, 4),), jnp.float32)
    down_weight_matrix = normal_values(splits[10], (2, HID, D), HID ** -0.5, 0.375, ((1, 4),), jnp.float32)
    down_bias_rows = normal_values(splits[11], (2, D), 0.5, 3.0, (), jnp.float32)
    layernorm_gains = jnp.clip(1.0 + 0.1 * jax.random.normal(splits[12], (4, D), jnp.float32), 0.5, 1.5)
    layernorm_offsets = normal_values(splits[13], (4, D), 0.5, 3.0, (), jnp.float32)
    cotangent = normal_values(splits[14], (TOKENS, D), 1.0, 6.0, ((0, 32),), jnp.float32)
    return {"pillar_feats": pillar_feats, "occupied": occupied, "shifted_source_rows": shifted_source_rows, "w_vfe": w_vfe, "bn_gain": bn_gain, "bn_shift": bn_shift, "query_key_value_weight": query_key_value_weight, "attention_output_weight": attention_output_weight, "up_weight_matrix": up_weight_matrix, "up_bias_rows": up_bias_rows, "down_weight_matrix": down_weight_matrix, "down_bias_rows": down_bias_rows, "layernorm_gains": layernorm_gains, "layernorm_offsets": layernorm_offsets, "cotangent": cotangent}


EPS_NORM = 1e-05
NEG_FILL = -1000000000.0

@jax.custom_vjp
def low(v):
    return lax.optimization_barrier(v.astype(jnp.bfloat16)).astype(jnp.float32)

@jax.custom_vjp
def low_back(v):
    return v

def low_keep(v):
    return (low(v), None)

def low_pass(kept, grad):
    return (grad,)

def back_keep(v):
    return (v, None)

def back_low(kept, grad):
    return (low(grad),)
low.defvjp(low_keep, low_pass)
low_back.defvjp(back_keep, back_low)

def matmul(former, latter):
    return jnp.dot(former, latter, precision=lax.Precision.HIGHEST)

def gelu_exact(values):
    return jax.nn.gelu(values, approximate=False)

def layer_norm(values, norm_gain, norm_shift):
    center = lax.optimization_barrier(jnp.mean(values, axis=-1, keepdims=True))
    spread = lax.optimization_barrier(jnp.mean((values - center) ** 2, axis=-1, keepdims=True))
    return (values - center) * lax.rsqrt(spread + EPS_NORM) * norm_gain + norm_shift

def batch_norm(values, live_rows, norm_gain, norm_shift):
    row_total = jnp.sum(live_rows)
    center = lax.optimization_barrier(jnp.sum(live_rows * values, axis=0)) / row_total
    spread = lax.optimization_barrier(jnp.sum(live_rows * (values - center) ** 2, axis=0)) / row_total
    return (values - center) * lax.rsqrt(spread + EPS_NORM) * norm_gain + norm_shift

def window_core(window_rows, key_live, w_qkv_one):
    windows, window_cells, model_width = window_rows.shape
    head_width = model_width // HEADS
    packed = jnp.einsum('wcd,de->wce', window_rows, w_qkv_one, precision=lax.Precision.HIGHEST)
    queries = packed[..., :model_width].reshape(windows, window_cells, HEADS, head_width)
    key_rows = packed[..., model_width:2 * model_width].reshape(windows, window_cells, HEADS, head_width)
    value_rows = packed[..., 2 * model_width:].reshape(windows, window_cells, HEADS, head_width)
    scores = jnp.einsum('wqhe,wkhe->whqk', queries, key_rows, precision=lax.Precision.HIGHEST) / math.sqrt(head_width)
    scores = jnp.where(key_live[:, None, None, :] > 0, scores, NEG_FILL)
    scores = scores - lax.optimization_barrier(jnp.max(scores, axis=-1, keepdims=True))
    weights = jnp.exp(scores)
    weights = weights / lax.optimization_barrier(jnp.sum(weights, axis=-1, keepdims=True))
    mixture = jnp.einsum('whqk,wkhe->wqhe', weights, value_rows, precision=lax.Precision.HIGHEST)
    return mixture.reshape(windows, window_cells, model_width)

def attention(carried_state, live_flat_rows, w_qkv_one, w_out_one):
    model_width = carried_state.shape[-1]
    groups = carried_state.reshape(-1, WIN_DEV, CELLS, model_width)
    live_groups = live_flat_rows.reshape(-1, WIN_DEV, CELLS)
    window_fn = jax.checkpoint(window_core)
    mixture = lax.map(lambda paired: window_fn(paired[0], paired[1], w_qkv_one), (groups, live_groups))
    return matmul(mixture.reshape(-1, model_width), w_out_one)

def sparse_window_layer(carried_state, live_flat_rows, layer_picker, query_key_value_weight, attention_output_weight, up_weight_matrix, up_bias_rows, down_weight_matrix, down_bias_rows, layernorm_gains, layernorm_offsets):
    first_norm = layer_norm(carried_state + attention(carried_state, live_flat_rows, query_key_value_weight[layer_picker], attention_output_weight[layer_picker]), layernorm_gains[2 * layer_picker], layernorm_offsets[2 * layer_picker])
    hidden = gelu_exact(matmul(first_norm, up_weight_matrix[layer_picker]) + up_bias_rows[layer_picker])
    summed = first_norm + matmul(hidden, down_weight_matrix[layer_picker]) + down_bias_rows[layer_picker]
    return layer_norm(summed, layernorm_gains[2 * layer_picker + 1], layernorm_offsets[2 * layer_picker + 1])

def reference(pillar_feats, occupied, shifted_source_rows, w_vfe, bn_gain, bn_shift, query_key_value_weight, attention_output_weight, up_weight_matrix, up_bias_rows, down_weight_matrix, down_bias_rows, layernorm_gains, layernorm_offsets, cotangent):
    live_flat_rows = occupied.astype(jnp.float32)
    live_rows = live_flat_rows[:, None]
    shifted_live_mask = live_flat_rows[shifted_source_rows]

    def forward(pillar_feats, w_vfe, bn_gain, bn_shift, query_key_value_weight, attention_output_weight, up_weight_matrix, up_bias_rows, down_weight_matrix, down_bias_rows, layernorm_gains, layernorm_offsets):
        carried_state = gelu_exact(batch_norm(matmul(pillar_feats, w_vfe), live_rows, bn_gain[0], bn_shift[0]))
        carried_state = sparse_window_layer(carried_state, live_flat_rows, 0, query_key_value_weight, attention_output_weight, up_weight_matrix, up_bias_rows, down_weight_matrix, down_bias_rows, layernorm_gains, layernorm_offsets)
        shifted_tokens = sparse_window_layer(carried_state[shifted_source_rows], shifted_live_mask, 1, query_key_value_weight, attention_output_weight, up_weight_matrix, up_bias_rows, down_weight_matrix, down_bias_rows, layernorm_gains, layernorm_offsets)
        returned = jnp.zeros_like(carried_state).at[shifted_source_rows].set(shifted_tokens)
        return live_rows * batch_norm(returned, live_rows, bn_gain[1], bn_shift[1])
    result, pull_back = jax.vjp(forward, pillar_feats, w_vfe, bn_gain, bn_shift, query_key_value_weight, attention_output_weight, up_weight_matrix, up_bias_rows, down_weight_matrix, down_bias_rows, layernorm_gains, layernorm_offsets)
    gradients = pull_back(cotangent)
    return (result, gradients[0], gradients[1], gradients[2], gradients[3], gradients[4], gradients[5], gradients[6], gradients[7], gradients[8], gradients[9], gradients[10], gradients[11])
```

```python
import math

import jax
import jax.numpy as jnp
from jax import lax
from jax.sharding import PartitionSpec as P

HEADS = 8
CELLS = 144


EPS_NORM = 1e-05
NEG_FILL = -1000000000.0


def passed_along(shard, axis, by):
    peers = lax.axis_size(axis)
    return lax.ppermute(shard, axis, [(i, (i + by) % peers) for i in range(peers)])


def matmul(former, latter):
    return jnp.dot(former, latter, precision=lax.Precision.HIGHEST)


def outer_sum(former, latter):
    return lax.dot_general(
        former, latter, (((0,), (0,)), ((), ())), precision=lax.Precision.HIGHEST
    )


def back_product(former, latter):
    return lax.dot_general(
        former, latter, (((1,), (1,)), ((), ())), precision=lax.Precision.HIGHEST
    )


def gelu_exact(values):
    return jax.nn.gelu(values, approximate=False)


def layer_norm(values, norm_gain, norm_shift):
    center = jnp.mean(values, axis=-1, keepdims=True)
    spread = jnp.mean((values - center) ** 2, axis=-1, keepdims=True)
    return (values - center) * lax.rsqrt(spread + EPS_NORM) * norm_gain + norm_shift


def window_core(window_rows, key_live, w_qkv_one):
    windows, window_cells, model_width = window_rows.shape
    head_width = model_width // HEADS
    packed = jnp.einsum("wcd,de->wce", window_rows, w_qkv_one, precision=lax.Precision.HIGHEST)
    queries = packed[..., :model_width].reshape(windows, window_cells, HEADS, head_width)
    key_rows = packed[..., model_width : 2 * model_width].reshape(
        windows, window_cells, HEADS, head_width
    )
    value_rows = packed[..., 2 * model_width :].reshape(windows, window_cells, HEADS, head_width)
    scores = jnp.einsum(
        "wqhe,wkhe->whqk", queries, key_rows, precision=lax.Precision.HIGHEST
    ) / math.sqrt(head_width)
    scores = jnp.where(key_live[:, None, None, :] > 0, scores, NEG_FILL)
    scores = scores - jnp.max(scores, axis=-1, keepdims=True)
    weights = jnp.exp(scores)
    weights = weights / jnp.sum(weights, axis=-1, keepdims=True)
    mixture = jnp.einsum("whqk,wkhe->wqhe", weights, value_rows, precision=lax.Precision.HIGHEST)
    return mixture.reshape(windows, window_cells, model_width)


AXES = ("win", "ffn")
WIDTH = 128


def spread_rows(rows, axes):
    peers = lax.axis_size(axes)
    return lax.all_to_all(jnp.broadcast_to(rows[None], (peers,) + rows.shape), axes, 0, 0)


def stack_rows(rows, multiple):
    count = sum(part.shape[0] for part in rows)
    short = -count % multiple
    if short:
        rows = list(rows) + [jnp.zeros((short, WIDTH), jnp.float32)]
    return jnp.concatenate(rows)


def local_places(source, row_count):
    devices = lax.axis_size(AXES)
    return (source - lax.axis_index(AXES) * row_count) % (row_count * devices)


def column_stats(values, live_rows):
    count = jnp.sum(live_rows)
    total = jnp.sum(live_rows * values, axis=0)
    mean = total / jnp.maximum(count, 1.0)
    deviations = values - mean
    return count, total, mean, deviations, jnp.sum(live_rows * deviations**2, axis=0)


def joined_stats(counts, totals, squares):
    count = jnp.sum(counts, axis=0)
    center = jnp.sum(totals, axis=0) / count
    means = totals / jnp.maximum(counts, 1.0)
    shifts = means - center
    spread = jnp.sum(squares + counts * shifts**2, axis=0) / count
    return count, center, lax.rsqrt(spread + EPS_NORM), shifts


def sum_everywhere(shared, split):
    wins, ffns = lax.axis_size("win"), lax.axis_size("ffn")
    devices = wins * ffns
    first = shared.reshape(wins, ffns, -1, WIDTH)
    second = split.reshape(ffns, wins, -1, WIDTH).transpose(1, 0, 2, 3)
    part = first.shape[2]
    pieces = jnp.concatenate([first, second], axis=2).reshape(devices, -1, WIDTH)
    mine = jnp.sum(lax.all_to_all(pieces, AXES, 0, 0), axis=0)
    return (
        spread_rows(mine[:part], AXES).reshape(-1, WIDTH),
        spread_rows(mine[part:], "win").reshape(-1, WIDTH),
    )


def layer_rows(
    values, key_live, qkv_one, out_one, in_one, bias_one, back_one, back_bias, norm_gains, norm_shifts
):
    window_rows = values.reshape(-1, CELLS, values.shape[-1])
    mixture = window_core(window_rows, key_live, qkv_one).reshape(values.shape)
    first = layer_norm(values + matmul(mixture, out_one), norm_gains[0], norm_shifts[0])
    hidden = gelu_exact(back_product(first, in_one) + bias_one)
    return layer_norm(
        first + matmul(hidden, back_one) + back_bias, norm_gains[1], norm_shifts[1]
    )


def on_device(
    pillar_feats,
    occupied,
    shifted_source_rows,
    w_vfe,
    bn_gain,
    bn_shift,
    query_key_value_weight,
    attention_output_weight,
    up_weight_matrix,
    up_bias_rows,
    down_weight_matrix,
    down_bias_rows,
    layernorm_gains,
    layernorm_offsets,
    cotangent,
):
    row_count = pillar_feats.shape[0]
    half = CELLS // 2
    units = up_weight_matrix.shape[2]
    ffns = lax.axis_size("ffn")
    live_rows = occupied.astype(jnp.float32)[:, None]
    places = local_places(shifted_source_rows, row_count)

    packed = stack_rows(
        [
            up_weight_matrix.transpose(0, 2, 1).reshape(2 * units, WIDTH),
            down_weight_matrix.reshape(2 * units, WIDTH),
            jnp.pad(up_bias_rows, ((0, 0), (0, WIDTH - units))),
        ],
        8,
    )
    gathered = lax.all_gather(packed, "ffn", axis=0, tiled=False)
    weights = gathered[:, : 4 * units].reshape(ffns, 2, 2, units, WIDTH)
    weights = weights.transpose(1, 2, 0, 3, 4).reshape(2, 2, ffns * units, WIDTH)
    biases = gathered[:, 4 * units : 4 * units + 2, :units].transpose(1, 0, 2).reshape(2, -1)

    edge = stack_rows(
        [
            cotangent[:half],
            jnp.pad(live_rows[:half, 0], (0, WIDTH - half))[None],
        ],
        8,
    )
    edge = passed_along(edge, AXES, -1)
    shifted_cotangent = jnp.concatenate([cotangent, edge[:half]])[places]
    shifted_live = jnp.concatenate([live_rows, edge[half, :half][:, None]])[places]

    lifted = matmul(pillar_feats, w_vfe)
    count, total, _, _, square = column_stats(lifted, live_rows)
    sent = jnp.stack([jnp.full((WIDTH,), count), total, square])
    seen = spread_rows(jnp.pad(sent, ((0, 5), (0, 0))), AXES)
    rows_live, vfe_center, vfe_rate, _ = joined_stats(seen[:, 0], seen[:, 1], seen[:, 2])
    vfe_hat = (lifted - vfe_center) * vfe_rate
    live_hat = live_rows * vfe_hat
    hat_sums = lax.psum(
        stack_rows([outer_sum(pillar_feats, live_hat), outer_sum(live_rows, pillar_feats)], 8), AXES
    )

    carried_state, pull_gelu = jax.vjp(gelu_exact, vfe_hat * bn_gain[0] + bn_shift[0])

    def layer(values, live, one):
        key_live = live[:, 0].reshape(-1, CELLS)

        def run(values, *held):
            return layer_rows(values, key_live, *held)

        return jax.vjp(
            run,
            values,
            query_key_value_weight[one],
            attention_output_weight[one],
            weights[0, one],
            biases[one],
            weights[1, one],
            down_bias_rows[one],
            layernorm_gains[2 * one : 2 * one + 2],
            layernorm_offsets[2 * one : 2 * one + 2],
        )

    first_out, pull_first = layer(carried_state, live_rows, 0)
    incoming = passed_along(first_out[:half], AXES, -1)
    second_out, pull_second = layer(
        jnp.concatenate([first_out, incoming])[places], shifted_live, 1
    )

    def back_to_rows(values):
        placed = jnp.zeros((row_count + half, WIDTH), values.dtype).at[places].set(values)
        arrived = passed_along(placed[row_count:], AXES, 1)
        return jnp.concatenate([arrived, placed[half:row_count]])

    live_cotangent = shifted_live * shifted_cotangent
    count, total, _, deviations, square = column_stats(second_out, shifted_live)
    cot_sum = jnp.sum(live_cotangent, axis=0)
    cot_product = jnp.sum(live_cotangent * deviations, axis=0)
    sent = jnp.stack([jnp.full((WIDTH,), count), total, square, cot_sum, cot_product])
    seen = spread_rows(jnp.pad(sent, ((0, 3), (0, 0))), AXES)
    _, neck_center, neck_rate, shifts = joined_stats(seen[:, 0], seen[:, 1], seen[:, 2])
    neck_shift_grad = jnp.sum(seen[:, 3], axis=0)
    neck_gain_grad = neck_rate * jnp.sum(seen[:, 4] + shifts * seen[:, 3], axis=0)
    neck_hat = (second_out - neck_center) * neck_rate
    pillars_out = back_to_rows(shifted_live * (neck_hat * bn_gain[1] + bn_shift[1]))
    grad_second = (
        neck_rate
        * bn_gain[1]
        * (
            live_cotangent
            - shifted_live * (neck_hat * neck_gain_grad + neck_shift_grad) / rows_live
        )
    )
    grad_shifted, *second_grads = pull_second(grad_second)
    grad_carried, *first_grads = pull_first(back_to_rows(grad_shifted))
    grad_affine = pull_gelu(grad_carried)[0]

    both = [jnp.stack(pair) for pair in zip(first_grads, second_grads)]
    qkv, out, up, up_bias, down, down_bias, gains, offsets = both
    shared = stack_rows(
        [
            jnp.sum(grad_affine * vfe_hat, axis=0)[None],
            jnp.sum(grad_affine, axis=0)[None],
            down_bias,
            gains.reshape(4, WIDTH),
            offsets.reshape(4, WIDTH),
            up_bias.reshape(-1, WIDTH),
            outer_sum(pillar_feats, grad_affine),
            out.reshape(-1, WIDTH),
            qkv.reshape(-1, WIDTH),
        ],
        8 * lax.axis_size(AXES),
    )
    split = jnp.stack([up, down]).reshape(4, ffns, units, WIDTH).transpose(1, 0, 2, 3)
    shared, split = sum_everywhere(shared, split.reshape(ffns, 4 * units, WIDTH))
    vfe_gain_grad, vfe_shift_grad = shared[0], shared[1]
    grad_b_back = shared[2:4]
    grad_ln_gain = shared[4:8]
    grad_ln_shift = shared[8:12]
    at = 12 + up_bias.size // WIDTH
    grad_b_in = lax.dynamic_slice_in_dim(
        shared[12:at].reshape(2, -1), lax.axis_index("ffn") * units, units, 1
    )
    affine_sums = shared[at : at + WIDTH]
    at += WIDTH
    grad_w_out = shared[at : at + 2 * WIDTH].reshape(2, WIDTH, WIDTH)
    at += 2 * WIDTH
    grad_w_qkv = shared[at : at + 6 * WIDTH].reshape(2, WIDTH, 3 * WIDTH)
    split = split.reshape(2, 2, units, WIDTH)
    grad_w_in, grad_w_back = split[0].transpose(0, 2, 1), split[1]

    scale = vfe_rate * bn_gain[0]
    grad_w_vfe = scale * (
        affine_sums
        - (
            hat_sums[:WIDTH] * vfe_gain_grad
            + hat_sums[WIDTH][:, None] * vfe_shift_grad
        )
        / rows_live
    )
    grad_lifted = scale * (
        grad_affine - live_rows * (vfe_hat * vfe_gain_grad + vfe_shift_grad) / rows_live
    )
    return (
        pillars_out,
        back_product(grad_lifted, w_vfe),
        grad_w_vfe,
        jnp.stack([vfe_gain_grad, neck_gain_grad]),
        jnp.stack([vfe_shift_grad, neck_shift_grad]),
        grad_w_qkv,
        grad_w_out,
        grad_w_in,
        grad_b_in,
        grad_w_back,
        grad_b_back,
        grad_ln_gain,
        grad_ln_shift,
    )


def solution(mesh):
    return jax.shard_map(
        on_device,
        mesh=mesh,
        in_specs=(
            P(("win", "ffn"), None),
            P(("win", "ffn")),
            P(("win", "ffn")),
            P(),
            P(),
            P(),
            P(),
            P(),
            P(None, None, "ffn"),
            P(None, "ffn"),
            P(None, "ffn", None),
            P(),
            P(),
            P(),
            P(("win", "ffn"), None),
        ),
        out_specs=(
            P(("win", "ffn"), None),
            P(("win", "ffn"), None),
            P(),
            P(),
            P(),
            P(),
            P(),
            P(None, None, "ffn"),
            P(None, "ffn"),
            P(None, "ffn", None),
            P(),
            P(),
            P(),
        ),
        check_vma=False,
    )
```

```python
import functools

import jax
import jax.numpy as jnp
from jax import lax
from jax.experimental import pallas as pl
from jax.experimental.pallas import tpu as pltpu
from jax.sharding import PartitionSpec as P

HEADS = 8
CELLS = 144
HALF = CELLS // 2
WIDTH = 128
EPS_NORM = 1e-05
NEG_FILL = -1000000000.0
AXES = ("win", "ffn")
STEP = 2 * CELLS
TILE_ROWS = WIDTH // HEADS
TILES = CELLS // TILE_ROWS
CHUNKS = ((0, 2), (2, 4), (4, 6), (6, 8), (8, 9))
F32 = jnp.float32
BF16 = jnp.bfloat16
VMEM_LIMIT = 56 * 1024 * 1024


def shape(*dims, dtype=F32):
    return jax.ShapeDtypeStruct(dims, dtype)


def whole(*dims):
    return pl.BlockSpec(dims, lambda i: (0,) * len(dims))


def rows_of(*dims):
    return pl.BlockSpec(dims, lambda i: (i,) + (0,) * (len(dims) - 1))


def share_of(rows, devices):
    return -(-rows // devices)


def halves(values):
    high = values.astype(BF16)
    return high, (values - high.astype(F32)).astype(BF16)


def nn(former, latter):
    return lax.dot_general(former, latter, (((1,), (0,)), ((), ())), preferred_element_type=F32)


def nt(former, latter):
    return lax.dot_general(former, latter, (((1,), (1,)), ((), ())), preferred_element_type=F32)


def tn(former, latter):
    return lax.dot_general(former, latter, (((0,), (0,)), ((), ())), preferred_element_type=F32)


def product(kind, former, latter):
    return kind(former[0], latter[0]) + (kind(former[0], latter[1]) + kind(former[1], latter[0]))


def gelu_parts(values):
    below = 0.5 * (1.0 + lax.erf(values * 0.7071067811865476))
    density = 0.3989422804014327 * jnp.exp(-0.5 * values * values)
    return values * below, below + values * density


def normed_rows(values):
    center = jnp.mean(values, axis=-1, keepdims=True)
    moved = values - center
    rate = lax.rsqrt(jnp.mean(moved * moved, axis=-1, keepdims=True) + EPS_NORM)
    return moved * rate, rate


def normed_back(grad, hat, rate, gain):
    scaled = grad * gain
    first = jnp.mean(scaled, axis=-1, keepdims=True)
    second = jnp.mean(scaled * hat, axis=-1, keepdims=True)
    return rate * (scaled - first - hat * second)


def column_sum(values):
    return jnp.sum(values, axis=0, keepdims=True)


def head_mask():
    dims = (HEADS, TILE_ROWS, WIDTH)
    lane_head = lax.broadcasted_iota(jnp.int32, dims, 2) // TILE_ROWS
    return (lane_head == lax.broadcasted_iota(jnp.int32, dims, 0)).astype(F32)


def per_head(rows, mask):
    count = rows.shape[0] // TILE_ROWS
    return (rows.reshape(count, 1, TILE_ROWS, WIDTH) * mask[None]).reshape(count * WIDTH, WIDTH)


def from_heads(table, mask):
    parts = []
    for at in range(0, table.shape[1], WIDTH):
        turned = table[:, at : at + WIDTH].T.reshape(HEADS, TILE_ROWS, WIDTH)
        parts.append(jnp.sum(turned * mask, axis=0))
    return parts


def window_mix(query, key, value, live, mask, mask_low, keep_high, keep_low):
    query_high, query_low = halves(query)
    key_high, key_low = halves(key)
    key_stack = jnp.concatenate([key_high, key_low, key_high], axis=1)
    turned = halves(value.T)
    mixed = []
    for first, last in CHUNKS:
        rows = slice(first * TILE_ROWS, last * TILE_ROWS)
        lanes = slice(first * WIDTH, last * WIDTH)
        high = per_head(query_high[rows], mask_low)
        low = per_head(query_low[rows], mask_low)
        scores = nt(key_stack, jnp.concatenate([high, high, low], axis=1))
        scores = jnp.where(live > 0, scores, NEG_FILL)
        weights = jnp.exp(scores - jnp.max(scores, axis=0, keepdims=True))
        weights = weights * (1.0 / column_sum(weights))
        weights = halves(weights)
        keep_high[:, lanes] = weights[0]
        keep_low[:, lanes] = weights[1]
        mixed += from_heads(product(nn, turned, weights), mask)
    return jnp.concatenate(mixed, axis=0)


def window_back(query, key, value, grad_mixed, live, mask, mask_low, kept_high, kept_low):
    query_halves = halves(query)
    grad_halves = halves(grad_mixed)
    value_high, value_low = halves(value)
    value_stack = jnp.concatenate([value_high, value_low, value_high], axis=1)
    turned = halves(key.T)
    grad_key = jnp.zeros((CELLS, 2 * WIDTH), F32)
    grad_value = jnp.zeros((CELLS, 2 * WIDTH), F32)
    key_rest = jnp.zeros((CELLS, WIDTH), F32)
    value_rest = jnp.zeros((CELLS, WIDTH), F32)
    grad_query = []
    for first, last in CHUNKS:
        rows = slice(first * TILE_ROWS, last * TILE_ROWS)
        lanes = slice(first * WIDTH, last * WIDTH)
        query_high, query_low = (per_head(part[rows], mask_low) for part in query_halves)
        grad_high, grad_low = (per_head(part[rows], mask_low) for part in grad_halves)
        grad_weights = nt(value_stack, jnp.concatenate([grad_high, grad_high, grad_low], axis=1))
        high, low = kept_high[:, lanes], kept_low[:, lanes]
        weights = high.astype(F32) + low.astype(F32)
        grad_scores = weights * grad_weights
        grad_scores = live * (grad_scores - weights * column_sum(grad_scores))
        scores_high, scores_low = halves(grad_scores)
        grad_value += nn(high, jnp.concatenate([grad_high, grad_low], axis=1))
        value_rest += nn(low, grad_high)
        grad_key += nn(scores_high, jnp.concatenate([query_high, query_low], axis=1))
        key_rest += nn(scores_low, query_high)
        grad_query += from_heads(product(nn, turned, (scores_high, scores_low)), mask)
    return (
        0.25 * jnp.concatenate(grad_query, axis=0),
        grad_key[:, :WIDTH] + (grad_key[:, WIDTH:] + key_rest),
        grad_value[:, :WIDTH] + (grad_value[:, WIDTH:] + value_rest),
    )


def unpack_weights(packed, one, up_high, up_low, down_high, down_low, bias):
    ffns = packed.shape[0]
    units = bias.shape[1] // ffns
    for at in range(ffns):
        rows = slice(at * units, (at + 1) * units)
        high, low = halves(packed[at, one * units : (one + 1) * units])
        up_high[rows], up_low[rows] = high, low
        high, low = halves(packed[at, (2 + one) * units : (3 + one) * units])
        down_high[rows], down_low[rows] = high, low
    bias[...] = jnp.concatenate(
        [packed[at, 4 * units + one : 4 * units + one + 1, :units] for at in range(ffns)], axis=1
    )


def layer_rows(one, values, live, weights, saved):
    qkv_high, qkv_low, out_high, out_low, up, down, bias, back_bias, gains, offsets = weights
    packed_keep, high_keep, low_keep, mixed_keep, hat_one, rate_one, hidden_keep, slope, hat_two, rate_two = saved
    mask = head_mask()
    mask_low = mask.astype(BF16)
    qkv = product(nn, halves(values), (qkv_high[one], qkv_low[one]))
    query = 0.25 * qkv[:, :WIDTH]
    packed_keep[:, :WIDTH] = query
    packed_keep[:, WIDTH:] = qkv[:, WIDTH:]
    for at in range(STEP // CELLS):
        rows = slice(at * CELLS, (at + 1) * CELLS)
        mixed_keep[rows] = window_mix(
            query[rows],
            qkv[rows, WIDTH : 2 * WIDTH],
            qkv[rows, 2 * WIDTH :],
            live[rows],
            mask,
            mask_low,
            high_keep.at[at],
            low_keep.at[at],
        )
    mixed = mixed_keep[...]
    hat, rate = normed_rows(
        values + product(nn, halves(mixed), (out_high[one], out_low[one]))
    )
    hat_one[...] = hat
    rate_one[...] = jnp.broadcast_to(rate, hat.shape)
    first = hat * gains[2 * one : 2 * one + 1] + offsets[2 * one : 2 * one + 1]
    hidden, steep = gelu_parts(product(nt, halves(first), up) + bias)
    hidden_keep[...] = hidden
    slope[...] = steep
    summed = first + product(nn, halves(hidden), down) + back_bias[one : one + 1]
    hat, rate = normed_rows(summed)
    hat_two[...] = hat
    rate_two[...] = jnp.broadcast_to(rate, hat.shape)
    return hat * gains[2 * one + 1 : 2 * one + 2] + offsets[2 * one + 1 : 2 * one + 2]


def ffn_rows_back(one, grad, saved, weights, sums):
    mixed_keep, hat_one, rate_one, hidden_keep, slope, hat_two, rate_two = saved
    out, up, down, gains, offsets = weights
    small, sum_out, sum_up, sum_down = sums
    hat = hat_two[...]
    grad_summed = normed_back(grad, hat, rate_two[...], gains[2 * one + 1 : 2 * one + 2])
    small[3:4] += column_sum(grad * hat)
    small[4:5] += column_sum(grad)
    small[0:1] += column_sum(grad_summed)
    summed_halves = halves(grad_summed)
    grad_pre = product(nt, summed_halves, down) * slope[...]
    pre_halves = halves(grad_pre)
    hidden_halves = halves(hidden_keep[...])
    sum_down[...] += product(tn, hidden_halves, summed_halves)
    hat = hat_one[...]
    first = hat * gains[2 * one : 2 * one + 1] + offsets[2 * one : 2 * one + 1]
    sum_up[...] += product(tn, pre_halves, halves(first))
    bias_sum = column_sum(grad_pre)
    for at in range(bias_sum.shape[1] // WIDTH):
        small[5 + at : 6 + at] += bias_sum[:, at * WIDTH : (at + 1) * WIDTH]
    grad_first = grad_summed + product(nn, pre_halves, up)
    small[1:2] += column_sum(grad_first * hat)
    small[2:3] += column_sum(grad_first)
    grad_joined = normed_back(grad_first, hat, rate_one[...], gains[2 * one : 2 * one + 1])
    joined_halves = halves(grad_joined)
    sum_out[...] += product(tn, halves(mixed_keep[...]), joined_halves)
    return grad_joined, product(nt, joined_halves, out)


def attention_rows_back(one, values, live, grad_joined, grad_mixed, saved, qkv_weights, sum_qkv):
    packed_keep, high_keep, low_keep = saved
    mask = head_mask()
    mask_low = mask.astype(BF16)
    parts = []
    for at in range(STEP // CELLS):
        rows = slice(at * CELLS, (at + 1) * CELLS)
        parts.append(
            window_back(
                packed_keep[rows, :WIDTH],
                packed_keep[rows, WIDTH : 2 * WIDTH],
                packed_keep[rows, 2 * WIDTH :],
                grad_mixed[rows],
                live[rows],
                mask,
                mask_low,
                high_keep.at[at],
                low_keep.at[at],
            )
        )
    grad_packed = halves(
        jnp.concatenate([jnp.concatenate(part, axis=1) for part in parts], axis=0)
    )
    sum_qkv[...] += product(tn, halves(values), grad_packed)
    return grad_joined + product(nt, grad_packed, (qkv_weights[0][one], qkv_weights[1][one]))


def share_rows(target, at, values, devices):
    count = values.shape[0]
    share = share_of(count, devices)
    for device in range(devices):
        begin = device * share
        if begin < count:
            held = min(share, count - begin)
            target[device, at : at + held] = values[begin : begin + held]
    return at + share


def share_units(target, at, sum_up, sum_down, wins, ffns):
    units = sum_up.shape[0] // ffns
    part = 2 * units // wins
    for f in range(ffns):
        rows = slice(f * units, (f + 1) * units)
        joined = jnp.concatenate([sum_up[rows], sum_down[rows]], axis=0)
        for w in range(wins):
            target[w * ffns + f, at : at + part] = joined[w * part : (w + 1) * part]
    return at + part


def joined_rows(table, at, count):
    devices = table.shape[0]
    share = share_of(count, devices)
    if share % 8 == 0 and share * devices == count:
        return table[:, at : at + share].reshape(count, WIDTH)
    pieces = []
    for device in range(devices):
        begin = device * share
        if begin < count:
            pieces.append(table[device, at : at + min(share, count - begin)])
    return jnp.concatenate(pieces, axis=0)


def vfe_kernel(
    feats_ref, weight_ref, occupied_ref, up_ref, down_ref, bias_ref, lifted_ref, live_ref, sent_ref, packed_ref
):
    devices = sent_ref.shape[0]
    units = up_ref.shape[2]
    feats = feats_ref[...]
    row_count = feats.shape[0]
    feats_halves = halves(feats)
    lifted = product(nn, feats_halves, halves(weight_ref[...]))
    lifted_ref[...] = lifted
    live = jnp.broadcast_to(occupied_ref[...].astype(F32), (8, row_count)).T[:, :1]
    live_ref[...] = live
    count = jnp.sum(live, axis=0, keepdims=True)
    total = column_sum(live * lifted)
    moved = live * (lifted - total / jnp.maximum(count, 1.0))
    sent_ref[...] = jnp.zeros(sent_ref.shape, F32)
    stats = jnp.concatenate(
        [
            jnp.broadcast_to(count, (1, WIDTH)),
            total,
            column_sum(moved * moved),
            column_sum(live * feats),
        ],
        axis=0,
    )
    sent_ref[:, 0:4] = jnp.broadcast_to(stats[None], (devices, 4, WIDTH))
    share_rows(sent_ref, 4, product(tn, feats_halves, halves(moved)), devices)
    turned = (up_ref[0].T, up_ref[1].T)
    for to in range(packed_ref.shape[0]):
        for one in range(2):
            packed_ref[to, one * units : (one + 1) * units] = turned[one]
            packed_ref[to, (2 + one) * units : (3 + one) * units] = down_ref[one]
        packed_ref[to, 4 * units :] = jnp.zeros((8, WIDTH), F32)
        packed_ref[to, 4 * units : 4 * units + 2, :units] = bias_ref[...]


def maps_kernel(source_ref, qkv_ref, out_ref, gather_ref, scatter_ref, qkv_high, qkv_low, out_high, out_low):
    row_count = source_ref.shape[1]
    held = gather_ref.shape[1]
    devices = lax.axis_size(AXES)
    places = source_ref[...] - lax.axis_index(AXES) * row_count
    places = jnp.where(places < 0, places + row_count * devices, places)
    column = jnp.broadcast_to(places.astype(F32), (8, row_count)).T[:, :1].astype(jnp.int32)
    for at in range(row_count // STEP):
        rows = slice(at * STEP, (at + 1) * STEP)
        lanes = lax.broadcasted_iota(jnp.int32, (STEP, held), 1)
        gather_ref[rows] = (lanes == column[rows]).astype(F32).astype(BF16)
        down = lax.broadcasted_iota(jnp.int32, (held, STEP), 0)
        scatter_ref[at] = (down == places[:, rows]).astype(F32).astype(BF16)
    qkv_high[...], qkv_low[...] = halves(qkv_ref[...])
    out_high[...], out_low[...] = halves(out_ref[...])


def vfe_stats(seen_ref, gain_ref, shift_ref, stats_ref, product_ref):
    counts, totals, squares, lives = (seen_ref[:, at] for at in range(4))
    count = column_sum(counts)
    center = column_sum(totals) / count
    moves = totals / jnp.maximum(counts, 1.0) - center
    rate = lax.rsqrt(column_sum(squares + counts * moves * moves) / count + EPS_NORM)
    stats_ref[...] = jnp.zeros(stats_ref.shape, F32)
    stats_ref[0:1] = count
    stats_ref[1:2] = center
    stats_ref[2:3] = rate
    stats_ref[3:4] = column_sum(lives)
    devices = seen_ref.shape[0]
    share = share_of(WIDTH, devices)
    mine = lax.axis_index(AXES) * share
    lanes = lax.broadcasted_iota(jnp.int32, lives.shape, 1)
    product_ref[...] = jnp.zeros(product_ref.shape, F32)
    for at in range(share):
        picked = jnp.sum(jnp.where(lanes == mine + at, lives, 0.0), axis=1, keepdims=True)
        product_ref[at : at + 1] = rate * column_sum(seen_ref[:, 4 + at] + picked * moves)


def first_kernel(
    lifted_ref,
    live_ref,
    cotangent_ref,
    seen_ref,
    bn_gain,
    bn_shift,
    qkv_high,
    qkv_low,
    out_high,
    out_low,
    packed,
    back_bias,
    gains,
    offsets,
    result,
    edge,
    stats,
    hat_product,
    vfe_hat,
    vfe_slope,
    carried,
    packed_keep,
    high_keep,
    low_keep,
    mixed_keep,
    hat_one,
    rate_one,
    hidden_keep,
    slope,
    hat_two,
    rate_two,
    up_high,
    up_low,
    down_high,
    down_low,
    bias,
):
    at = pl.program_id(0)

    @pl.when(at == 0)
    def _():
        unpack_weights(packed, 0, up_high, up_low, down_high, down_low, bias)
        vfe_stats(seen_ref, bn_gain, bn_shift, stats, hat_product)

    hat = (lifted_ref[...] - stats[1:2]) * stats[2:3]
    values, steep = gelu_parts(hat * bn_gain[0:1] + bn_shift[0:1])
    vfe_hat[...] = hat
    vfe_slope[...] = steep
    carried[...] = values
    live = live_ref[...]
    rows = layer_rows(
        0,
        values,
        live,
        (
            qkv_high,
            qkv_low,
            out_high,
            out_low,
            (up_high[...], up_low[...]),
            (down_high[...], down_low[...]),
            bias[...],
            back_bias,
            gains,
            offsets,
        ),
        (packed_keep, high_keep, low_keep, mixed_keep, hat_one, rate_one, hidden_keep, slope, hat_two, rate_two),
    )
    result[...] = rows

    @pl.when(at == 0)
    def _():
        edge[:, :WIDTH] = rows[:HALF]
        edge[:, WIDTH : 2 * WIDTH] = cotangent_ref[:HALF]
        edge[:, 2 * WIDTH :] = jnp.broadcast_to(live[:HALF], (HALF, WIDTH))


def second_kernel(
    first_ref,
    cotangent_ref,
    live_ref,
    edge,
    gather_ref,
    qkv_high,
    qkv_low,
    out_high,
    out_low,
    packed,
    back_bias,
    gains,
    offsets,
    result,
    sent,
    live_keep,
    cotangent_keep,
    carried,
    packed_keep,
    high_keep,
    low_keep,
    mixed_keep,
    hat_one,
    rate_one,
    hidden_keep,
    slope,
    hat_two,
    rate_two,
    up_high,
    up_low,
    down_high,
    down_low,
    bias,
    table,
    sums,
):
    at = pl.program_id(0)
    row_count = first_ref.shape[0]

    @pl.when(at == 0)
    def _():
        unpack_weights(packed, 1, up_high, up_low, down_high, down_low, bias)
        high, low = halves(first_ref[...])
        table[:row_count, :WIDTH] = high
        table[:row_count, WIDTH : 2 * WIDTH] = low
        high, low = halves(cotangent_ref[...])
        table[:row_count, 2 * WIDTH : 3 * WIDTH] = high
        table[:row_count, 3 * WIDTH : 4 * WIDTH] = low
        table[:row_count, 4 * WIDTH :] = jnp.broadcast_to(live_ref[...], (row_count, WIDTH)).astype(BF16)
        spare = table.shape[0] - row_count
        tail = jnp.concatenate([edge[...], jnp.zeros((spare - HALF, 3 * WIDTH), F32)], axis=0)
        high, low = halves(tail)
        table[row_count:, :WIDTH] = high[:, :WIDTH]
        table[row_count:, WIDTH : 2 * WIDTH] = low[:, :WIDTH]
        table[row_count:, 2 * WIDTH : 3 * WIDTH] = high[:, WIDTH : 2 * WIDTH]
        table[row_count:, 3 * WIDTH : 4 * WIDTH] = low[:, WIDTH : 2 * WIDTH]
        table[row_count:, 4 * WIDTH :] = high[:, 2 * WIDTH :]
        sums[...] = jnp.zeros(sums.shape, F32)

    gathered = nn(gather_ref[...], table[...])
    values = gathered[:, :WIDTH] + gathered[:, WIDTH : 2 * WIDTH]
    live = gathered[:, 4 * WIDTH :]
    grad = live * (gathered[:, 2 * WIDTH : 3 * WIDTH] + gathered[:, 3 * WIDTH : 4 * WIDTH])
    carried[...] = values
    cotangent_keep[...] = grad
    live_keep[...] = live[:, :1]
    rows = layer_rows(
        1,
        values,
        live[:, :1],
        (
            qkv_high,
            qkv_low,
            out_high,
            out_low,
            (up_high[...], up_low[...]),
            (down_high[...], down_low[...]),
            bias[...],
            back_bias,
            gains,
            offsets,
        ),
        (packed_keep, high_keep, low_keep, mixed_keep, hat_one, rate_one, hidden_keep, slope, hat_two, rate_two),
    )
    result[...] = rows
    count = column_sum(live)

    @pl.when(at == 0)
    def _():
        sums[5:6] = column_sum(live * rows) / jnp.maximum(count, 1.0)

    moved = rows - sums[5:6]
    sums[0:1] += count
    sums[1:2] += column_sum(live * moved)
    sums[2:3] += column_sum(live * moved * moved)
    sums[3:4] += column_sum(grad)
    sums[4:5] += column_sum(grad * moved)

    @pl.when(at == pl.num_programs(0) - 1)
    def _():
        count = sums[0:1]
        move = sums[1:2] / jnp.maximum(count, 1.0)
        stats = jnp.concatenate(
            [
                count,
                sums[5:6] + move,
                sums[2:3] - count * move * move,
                sums[3:4],
                sums[4:5] - move * sums[3:4],
                jnp.zeros((3, WIDTH), F32),
            ],
            axis=0,
        )
        sent[...] = jnp.broadcast_to(stats[None], sent.shape)


def second_back_kernel(
    result,
    seen_ref,
    bn_gain,
    bn_shift,
    scatter_ref,
    qkv_high,
    qkv_low,
    out_high,
    out_low,
    packed,
    gains,
    offsets,
    live_keep,
    cotangent_keep,
    carried,
    packed_keep,
    high_keep,
    low_keep,
    mixed_keep,
    hat_one,
    rate_one,
    hidden_keep,
    slope,
    hat_two,
    rate_two,
    shared,
    edge,
    grad_rows,
    out_rows,
    neck,
    up_high,
    up_low,
    down_high,
    down_low,
    bias,
    stats,
    small,
    sum_qkv,
    sum_out,
    sum_up,
    sum_down,
    placed,
    *,
    wins,
    ffns,
):
    at = pl.program_id(0)
    row_count = grad_rows.shape[0]

    @pl.when(at == 0)
    def _():
        unpack_weights(packed, 1, up_high, up_low, down_high, down_low, bias)
        counts, means, squares, grads, products = (seen_ref[:, row] for row in range(5))
        count = column_sum(counts)
        center = column_sum(counts * means) / count
        moves = means - center
        rate = lax.rsqrt(column_sum(squares + counts * moves * moves) / count + EPS_NORM)
        stats[0:1] = count
        stats[1:2] = center
        stats[2:3] = rate
        stats[3:4] = rate * column_sum(products + moves * grads)
        stats[4:5] = column_sum(grads)
        neck[...] = jnp.zeros(neck.shape, F32)
        neck[0:2] = stats[3:5]
        for held in (small, sum_qkv, sum_out, sum_up, sum_down, placed):
            held[...] = jnp.zeros(held.shape, F32)

    live = live_keep[...]
    rate = stats[2:3]
    hat = (result[...] - stats[1:2]) * rate
    neck_rows = live * (hat * bn_gain[1:2] + bn_shift[1:2])
    grad = rate * bn_gain[1:2] * (
        cotangent_keep[...] - live * (hat * stats[3:4] + stats[4:5]) / stats[0:1]
    )
    grad_joined, grad_mixed = ffn_rows_back(
        1,
        grad,
        (mixed_keep, hat_one, rate_one, hidden_keep, slope, hat_two, rate_two),
        (
            (out_high[1], out_low[1]),
            (up_high[...], up_low[...]),
            (down_high[...], down_low[...]),
            gains,
            offsets,
        ),
        (small, sum_out, sum_up, sum_down),
    )
    grad_values = attention_rows_back(
        1,
        carried[...],
        live,
        grad_joined,
        grad_mixed,
        (packed_keep, high_keep, low_keep),
        (qkv_high, qkv_low),
        sum_qkv,
    )
    pieces = halves(grad_values) + halves(neck_rows)
    moved = nn(scatter_ref[0], jnp.concatenate(pieces, axis=1))
    placed[:, :WIDTH] += moved[:, :WIDTH] + moved[:, WIDTH : 2 * WIDTH]
    placed[:, WIDTH:] += moved[:, 2 * WIDTH : 3 * WIDTH] + moved[:, 3 * WIDTH :]

    @pl.when(at == pl.num_programs(0) - 1)
    def _():
        grad_rows[...] = placed[:row_count, :WIDTH]
        out_rows[...] = placed[:row_count, WIDTH:]
        edge[...] = placed[row_count : row_count + HALF]
        devices = wins * ffns
        shared[...] = jnp.zeros(shared.shape, F32)
        row = share_units(shared, 0, sum_up, sum_down, wins, ffns)
        for block in range(3):
            row = share_rows(shared, row, sum_qkv[:, block * WIDTH : (block + 1) * WIDTH], devices)
        row = share_rows(shared, row, sum_out, devices)
        share_rows(shared, row, small, devices)


def first_ffn_back_kernel(
    grad_rows,
    edge,
    out_rows,
    out_high,
    out_low,
    packed,
    gains,
    offsets,
    mixed_keep,
    hat_one,
    rate_one,
    hidden_keep,
    slope,
    hat_two,
    rate_two,
    grad_joined,
    grad_mixed,
    pillars,
    shared,
    up_high,
    up_low,
    down_high,
    down_low,
    bias,
    small,
    sum_out,
    sum_up,
    sum_down,
    grad_step,
    *,
    wins,
    ffns,
):
    at = pl.program_id(0)

    @pl.when(at == 0)
    def _():
        unpack_weights(packed, 0, up_high, up_low, down_high, down_low, bias)
        for held in (small, sum_out, sum_up, sum_down):
            held[...] = jnp.zeros(held.shape, F32)

    grad_step[...] = grad_rows[...]
    pillars[...] = out_rows[...]

    @pl.when(at == 0)
    def _():
        grad_step[:HALF] = edge[:, :WIDTH]
        pillars[:HALF] = edge[:, WIDTH:]

    joined, mixed = ffn_rows_back(
        0,
        grad_step[...],
        (mixed_keep, hat_one, rate_one, hidden_keep, slope, hat_two, rate_two),
        (
            (out_high[0], out_low[0]),
            (up_high[...], up_low[...]),
            (down_high[...], down_low[...]),
            gains,
            offsets,
        ),
        (small, sum_out, sum_up, sum_down),
    )
    grad_joined[...] = joined
    grad_mixed[...] = mixed

    @pl.when(at == pl.num_programs(0) - 1)
    def _():
        shared[...] = jnp.zeros(shared.shape, F32)
        row = share_units(shared, 0, sum_up, sum_down, wins, ffns)
        row = share_rows(shared, row, sum_out, wins * ffns)
        share_rows(shared, row, small, wins * ffns)


def first_attention_back_kernel(
    grad_joined,
    grad_mixed,
    feats_ref,
    live_ref,
    carried,
    vfe_hat,
    vfe_slope,
    qkv_high,
    qkv_low,
    packed_keep,
    high_keep,
    low_keep,
    grad_affine,
    shared,
    sent,
    sum_qkv,
    sum_feats,
    small,
):
    at = pl.program_id(0)

    @pl.when(at == 0)
    def _():
        for held in (small, sum_qkv, sum_feats):
            held[...] = jnp.zeros(held.shape, F32)

    grad = attention_rows_back(
        0,
        carried[...],
        live_ref[...],
        grad_joined[...],
        grad_mixed[...],
        (packed_keep, high_keep, low_keep),
        (qkv_high, qkv_low),
        sum_qkv,
    )
    grad = grad * vfe_slope[...]
    grad_affine[...] = grad
    small[0:1] += column_sum(grad * vfe_hat[...])
    small[1:2] += column_sum(grad)
    sum_feats[...] += product(tn, halves(feats_ref[...]), halves(grad))

    @pl.when(at == pl.num_programs(0) - 1)
    def _():
        devices = shared.shape[0]
        shared[...] = jnp.zeros(shared.shape, F32)
        row = 0
        for block in range(3):
            row = share_rows(shared, row, sum_qkv[:, block * WIDTH : (block + 1) * WIDTH], devices)
        share_rows(shared, row, sum_feats, devices)
        sent[...] = jnp.broadcast_to(small[...][None], sent.shape)


def relay_kernel(*refs, split, count, extra):
    arrived = refs[0]
    total = jnp.sum(arrived[...], axis=0)
    outs = refs[2:] if extra else refs[1:]
    if split:
        outs[1][...] = jnp.broadcast_to(total[:split][None], outs[1].shape)
    rows = total[split : split + count]
    if extra:
        rows = jnp.concatenate([rows, refs[1][:extra]], axis=0)
    room = outs[0].shape[1]
    if rows.shape[0] < room:
        rows = jnp.concatenate([rows, jnp.zeros((room - rows.shape[0], WIDTH), F32)], axis=0)
    outs[0][...] = jnp.broadcast_to(rows[:room][None], outs[0].shape)


def feats_back_kernel(grad_affine, vfe_hat, live_ref, stats, seen_ref, bn_gain, weight_ref, grad_feats, vfe_grads):
    sums = jnp.sum(seen_ref[...], axis=0)
    vfe_grads[...] = sums
    scale = stats[2:3] * bn_gain[0:1]
    grad = scale * (
        grad_affine[...]
        - live_ref[...] * (vfe_hat[...] * sums[0:1] + sums[1:2]) / stats[0:1]
    )
    grad_feats[...] = product(nt, halves(grad), halves(weight_ref[...]))


def last_kernel(
    late,
    middle,
    early,
    late_units,
    early_units,
    stats,
    vfe_grads,
    neck,
    bn_gain,
    grad_w_vfe,
    grad_bn_gain,
    grad_bn_shift,
    grad_w_qkv,
    grad_w_out,
    grad_w_in,
    grad_b_in,
    grad_w_back,
    grad_b_back,
    grad_ln_gain,
    grad_ln_shift,
    *,
    ffns,
):
    devices = late.shape[0]
    part = share_of(WIDTH, devices)
    units = grad_w_in.shape[2]
    wins = late_units.shape[0]
    piece = 2 * units // wins
    for block in range(3):
        lanes = slice(block * WIDTH, (block + 1) * WIDTH)
        grad_w_qkv[0, :, lanes] = joined_rows(late, block * part, WIDTH)
        grad_w_qkv[1, :, lanes] = joined_rows(early, block * part, WIDTH)
    feats_sum = joined_rows(late, 3 * part, WIDTH)
    grad_w_out[0] = joined_rows(middle, 0, WIDTH)
    grad_w_out[1] = joined_rows(early, 3 * part, WIDTH)
    small_rows = 8
    one = share_of(small_rows, devices)
    smalls = (
        joined_rows(middle, part, small_rows),
        joined_rows(early, 4 * part, small_rows),
    )
    hat_sum = joined_rows(early, 4 * part + one, WIDTH)
    mine = lax.rem(lax.axis_index(AXES), ffns)
    for layer in range(2):
        small = smalls[layer]
        grad_b_back[layer : layer + 1] = small[0:1]
        grad_ln_gain[2 * layer : 2 * layer + 1] = small[1:2]
        grad_ln_shift[2 * layer : 2 * layer + 1] = small[2:3]
        grad_ln_gain[2 * layer + 1 : 2 * layer + 2] = small[3:4]
        grad_ln_shift[2 * layer + 1 : 2 * layer + 2] = small[4:5]
        held = jnp.zeros((1, units), F32)
        for f in range(ffns):
            row, lane = divmod(f * units, WIDTH)
            held = jnp.where(mine == f, small[5 + row : 6 + row, lane : lane + units], held)
        grad_b_in[layer : layer + 1] = held
        table = (late_units, early_units)[layer]
        joined = joined_rows(table, 0, 2 * units)
        grad_w_in[layer] = joined[:units].T
        grad_w_back[layer] = joined[units:]
    gain, shift = vfe_grads[0:1], vfe_grads[1:2]
    grad_bn_gain[0:1] = gain
    grad_bn_gain[1:2] = neck[0:1]
    grad_bn_shift[0:1] = shift
    grad_bn_shift[1:2] = neck[1:2]
    live_sum = jnp.broadcast_to(stats[3:4], (8, WIDTH)).T[:, :1]
    grad_w_vfe[...] = stats[2:3] * bn_gain[0:1] * (
        feats_sum - (hat_sum * gain + live_sum * shift) / stats[0:1]
    )


def spread_rows(pieces, axes):
    return lax.all_to_all(pieces, axes, 0, 0)


def passed_along(rows, by):
    peers = lax.axis_size(AXES)
    return lax.ppermute(rows, AXES, [(i, (i + by) % peers) for i in range(peers)])


def params():
    return pltpu.CompilerParams(vmem_limit_bytes=VMEM_LIMIT)


def cost(flops, size):
    return pl.CostEstimate(flops=int(flops), bytes_accessed=int(size), transcendentals=0)


def on_device(
    pillar_feats,
    occupied,
    shifted_source_rows,
    w_vfe,
    bn_gain,
    bn_shift,
    query_key_value_weight,
    attention_output_weight,
    up_weight_matrix,
    up_bias_rows,
    down_weight_matrix,
    down_bias_rows,
    layernorm_gains,
    layernorm_offsets,
    cotangent,
):
    row_count = pillar_feats.shape[0]
    steps = row_count // STEP
    held = row_count + -(-HALF // 16) * 16
    wins, ffns = lax.axis_size("win"), lax.axis_size("ffn")
    devices = wins * ffns
    units = up_weight_matrix.shape[2]
    hidden = units * ffns
    part = share_of(WIDTH, devices)
    stats_rows = -(-(4 + part) // 8) * 8

    lifted, live, sent, packed = pl.pallas_call(
        vfe_kernel,
        out_shape=(
            shape(row_count, WIDTH),
            shape(row_count, 1),
            shape(devices, stats_rows, WIDTH),
            shape(ffns, 4 * units + 8, WIDTH),
        ),
        compiler_params=params(),
        name="vfe",
    )(
        pillar_feats,
        w_vfe,
        occupied.reshape(1, row_count),
        up_weight_matrix,
        down_weight_matrix,
        up_bias_rows,
    )
    seen = spread_rows(sent, AXES)
    packed = spread_rows(packed, "ffn")
    gather, scatter, qkv_high, qkv_low, out_high, out_low = pl.pallas_call(
        maps_kernel,
        out_shape=(
            shape(row_count, held, dtype=BF16),
            shape(steps, held, STEP, dtype=BF16),
            shape(2, WIDTH, 3 * WIDTH, dtype=BF16),
            shape(2, WIDTH, 3 * WIDTH, dtype=BF16),
            shape(2, WIDTH, WIDTH, dtype=BF16),
            shape(2, WIDTH, WIDTH, dtype=BF16),
        ),
        compiler_params=params(),
        cost_estimate=cost(1e8, 4e6),
        name="maps",
    )(shifted_source_rows.reshape(1, row_count), query_key_value_weight, attention_output_weight)

    rows_spec = rows_of(STEP, WIDTH)
    column_spec = rows_of(STEP, 1)
    qkv_specs = [whole(2, WIDTH, 3 * WIDTH)] * 2
    out_specs = [whole(2, WIDTH, WIDTH)] * 2
    packed_spec = whole(*packed.shape)
    norm_specs = [whole(4, WIDTH)] * 2
    pair_spec = whole(2, WIDTH)
    seen_spec = whole(devices, stats_rows, WIDTH)
    eight_spec = whole(8, WIDTH)
    unit_scratch = [pltpu.VMEM((hidden, WIDTH), BF16)] * 4 + [pltpu.VMEM((1, hidden), F32)]
    keep_specs = [
        rows_spec,
        rows_of(STEP, 3 * WIDTH),
        rows_of(STEP // CELLS, CELLS, HEADS * CELLS),
        rows_of(STEP // CELLS, CELLS, HEADS * CELLS),
        rows_spec,
        rows_spec,
        rows_spec,
        rows_of(STEP, hidden),
        rows_of(STEP, hidden),
        rows_spec,
        rows_spec,
    ]
    windows = row_count // CELLS
    row_shape = shape(row_count, WIDTH)
    keep_shapes = [
        row_shape,
        shape(row_count, 3 * WIDTH),
        shape(windows, CELLS, HEADS * CELLS, dtype=BF16),
        shape(windows, CELLS, HEADS * CELLS, dtype=BF16),
        row_shape,
        row_shape,
        row_shape,
        shape(row_count, hidden),
        shape(row_count, hidden),
        row_shape,
        row_shape,
    ]

    first_out, edge, stats, hat_product, vfe_hat, vfe_slope, *first_keep = pl.pallas_call(
        first_kernel,
        grid=(steps,),
        in_specs=[rows_spec, column_spec, rows_spec, seen_spec, pair_spec, pair_spec]
        + qkv_specs
        + out_specs
        + [packed_spec, pair_spec]
        + norm_specs,
        out_specs=[rows_spec, whole(HALF, 3 * WIDTH), eight_spec, eight_spec, rows_spec, rows_spec] + keep_specs,
        out_shape=[row_shape, shape(HALF, 3 * WIDTH), shape(8, WIDTH), shape(8, WIDTH), row_shape, row_shape]
        + keep_shapes,
        scratch_shapes=unit_scratch,
        compiler_params=params(),
        cost_estimate=cost(4e9, 12e6),
        name="first",
    )(
        lifted,
        live,
        cotangent,
        seen,
        bn_gain,
        bn_shift,
        qkv_high,
        qkv_low,
        out_high,
        out_low,
        packed,
        down_bias_rows,
        layernorm_gains,
        layernorm_offsets,
    )
    edge = passed_along(edge, -1)
    second_out, sent, live_keep, cotangent_keep, *second_keep = pl.pallas_call(
        second_kernel,
        grid=(steps,),
        in_specs=[
            whole(row_count, WIDTH),
            whole(row_count, WIDTH),
            whole(row_count, 1),
            whole(HALF, 3 * WIDTH),
            rows_of(STEP, held),
        ]
        + qkv_specs
        + out_specs
        + [packed_spec, pair_spec]
        + norm_specs,
        out_specs=[rows_spec, whole(devices, 8, WIDTH), column_spec, rows_spec] + keep_specs,
        out_shape=[row_shape, shape(devices, 8, WIDTH), shape(row_count, 1), row_shape] + keep_shapes,
        scratch_shapes=unit_scratch
        + [pltpu.VMEM((held, 5 * WIDTH), BF16), pltpu.VMEM((8, WIDTH), F32)],
        compiler_params=params(),
        cost_estimate=cost(4e9, 12e6),
        name="second",
    )(
        first_out,
        cotangent,
        live,
        edge,
        gather,
        qkv_high,
        qkv_low,
        out_high,
        out_low,
        packed,
        down_bias_rows,
        layernorm_gains,
        layernorm_offsets,
    )
    seen = spread_rows(sent, AXES)
    piece = 2 * units // wins
    early_rows = -(-(piece + 4 * part + share_of(8, devices)) // 8) * 8
    sum_scratch = [
        pltpu.VMEM((8, WIDTH), F32),
        pltpu.VMEM((WIDTH, 3 * WIDTH), F32),
        pltpu.VMEM((WIDTH, WIDTH), F32),
        pltpu.VMEM((hidden, WIDTH), F32),
        pltpu.VMEM((hidden, WIDTH), F32),
    ]
    shared, edge, grad_rows, out_rows, neck = pl.pallas_call(
        functools.partial(second_back_kernel, wins=wins, ffns=ffns),
        grid=(steps,),
        in_specs=[rows_spec, whole(devices, 8, WIDTH), pair_spec, pair_spec, rows_of(1, held, STEP)]
        + qkv_specs
        + out_specs
        + [packed_spec]
        + norm_specs
        + [column_spec, rows_spec]
        + keep_specs,
        out_specs=[
            whole(devices, early_rows, WIDTH),
            whole(HALF, 2 * WIDTH),
            whole(row_count, WIDTH),
            whole(row_count, WIDTH),
            eight_spec,
        ],
        out_shape=[
            shape(devices, early_rows, WIDTH),
            shape(HALF, 2 * WIDTH),
            row_shape,
            row_shape,
            shape(8, WIDTH),
        ],
        scratch_shapes=unit_scratch
        + [pltpu.VMEM((8, WIDTH), F32)]
        + sum_scratch
        + [pltpu.VMEM((held, 2 * WIDTH), F32)],
        compiler_params=params(),
        cost_estimate=cost(8e9, 12e6),
        name="second_back",
    )(
        second_out,
        seen,
        bn_gain,
        bn_shift,
        scatter,
        qkv_high,
        qkv_low,
        out_high,
        out_low,
        packed,
        layernorm_gains,
        layernorm_offsets,
        live_keep,
        cotangent_keep,
        *second_keep,
    )
    edge = passed_along(edge, 1)
    early = spread_rows(shared, AXES)
    middle_rows = -(-(piece + part + share_of(8, devices)) // 8) * 8
    carried, packed_keep, high_keep, low_keep, *ffn_keep = first_keep
    grad_joined, grad_mixed, pillars_out, shared = pl.pallas_call(
        functools.partial(first_ffn_back_kernel, wins=wins, ffns=ffns),
        grid=(steps,),
        in_specs=[rows_spec, whole(HALF, 2 * WIDTH), rows_spec]
        + out_specs
        + [packed_spec]
        + norm_specs
        + keep_specs[4:],
        out_specs=[rows_spec, rows_spec, rows_spec, whole(devices, middle_rows, WIDTH)],
        out_shape=[row_shape, row_shape, row_shape, shape(devices, middle_rows, WIDTH)],
        scratch_shapes=unit_scratch + [sum_scratch[0]] + sum_scratch[2:] + [pltpu.VMEM((STEP, WIDTH), F32)],
        compiler_params=params(),
        cost_estimate=cost(4e9, 6e6),
        name="first_ffn_back",
    )(
        grad_rows,
        edge,
        out_rows,
        out_high,
        out_low,
        packed,
        layernorm_gains,
        layernorm_offsets,
        *ffn_keep,
    )

    def relay(arrived, split, count, *extra):
        extra_rows = part if extra else 0
        rows = -(-(count + extra_rows) // 8) * 8
        outs = [shape(devices, rows, WIDTH)]
        if split:
            outs.append(shape(wins, split, WIDTH))
        return pl.pallas_call(
            functools.partial(relay_kernel, split=split, count=count, extra=extra_rows),
            out_shape=outs,
            compiler_params=params(),
            name="relay",
        )(arrived, *extra)

    one = share_of(8, devices)
    early, early_units = relay(early, piece, 4 * part + one, hat_product)
    early = spread_rows(early, AXES)
    early_units = spread_rows(early_units, "win")
    middle = spread_rows(shared, AXES)
    late_rows = -(-(4 * part) // 8) * 8
    grad_affine, shared, sent = pl.pallas_call(
        first_attention_back_kernel,
        grid=(steps,),
        in_specs=[rows_spec, rows_spec, rows_spec, column_spec, rows_spec, rows_spec, rows_spec]
        + qkv_specs
        + keep_specs[1:4],
        out_specs=[rows_spec, whole(devices, late_rows, WIDTH), whole(devices, 8, WIDTH)],
        out_shape=[row_shape, shape(devices, late_rows, WIDTH), shape(devices, 8, WIDTH)],
        scratch_shapes=[sum_scratch[1], sum_scratch[2], sum_scratch[0]],
        compiler_params=params(),
        cost_estimate=cost(6e9, 8e6),
        name="first_attention_back",
    )(
        grad_joined,
        grad_mixed,
        pillar_feats,
        live,
        carried,
        vfe_hat,
        vfe_slope,
        qkv_high,
        qkv_low,
        packed_keep,
        high_keep,
        low_keep,
    )
    seen = spread_rows(sent, AXES)
    late = spread_rows(shared, AXES)
    middle, late_units = relay(middle, piece, part + one)
    middle = spread_rows(middle, AXES)
    late_units = spread_rows(late_units, "win")
    late = relay(late, 0, 4 * part)[0]
    late = spread_rows(late, AXES)
    grad_feats, vfe_grads = pl.pallas_call(
        feats_back_kernel,
        out_shape=(row_shape, shape(8, WIDTH)),
        compiler_params=params(),
        cost_estimate=cost(1e8, 2e6),
        name="feats_back",
    )(grad_affine, vfe_hat, live, stats, seen, bn_gain, w_vfe)
    grads = pl.pallas_call(
        functools.partial(last_kernel, ffns=ffns),
        out_shape=(
            shape(WIDTH, WIDTH),
            shape(2, WIDTH),
            shape(2, WIDTH),
            shape(2, WIDTH, 3 * WIDTH),
            shape(2, WIDTH, WIDTH),
            shape(2, WIDTH, units),
            shape(2, units),
            shape(2, units, WIDTH),
            shape(2, WIDTH),
            shape(4, WIDTH),
            shape(4, WIDTH),
        ),
        compiler_params=params(),
        name="last",
    )(late, middle, early, late_units, early_units, stats, vfe_grads, neck, bn_gain)
    return (pillars_out, grad_feats, *grads)


def solution(mesh):
    return jax.shard_map(
        on_device,
        mesh=mesh,
        in_specs=(
            P(("win", "ffn"), None),
            P(("win", "ffn")),
            P(("win", "ffn")),
            P(),
            P(),
            P(),
            P(),
            P(),
            P(None, None, "ffn"),
            P(None, "ffn"),
            P(None, "ffn", None),
            P(),
            P(),
            P(),
            P(("win", "ffn"), None),
        ),
        out_specs=(
            P(("win", "ffn"), None),
            P(("win", "ffn"), None),
            P(),
            P(),
            P(),
            P(),
            P(),
            P(None, None, "ffn"),
            P(None, "ffn"),
            P(None, "ffn", None),
            P(),
            P(),
            P(),
        ),
        check_vma=False,
    )
```

```python
import functools

import jax
import jax.numpy as jnp
from jax import lax
from jax.experimental import pallas as pl
from jax.experimental.pallas import tpu as pltpu
from jax.sharding import PartitionSpec as P

HEADS = 8
CELLS = 144
HALF = CELLS // 2
WIDTH = 128
EPS_NORM = 1e-05
NEG_FILL = -1000000000.0
AXES = ("win", "ffn")
STEP = 2 * CELLS
TILE_ROWS = WIDTH // HEADS
TILES = CELLS // TILE_ROWS
CHUNKS = ((0, 2), (2, 4), (4, 6), (6, 8), (8, 9))
F32 = jnp.float32
BF16 = jnp.bfloat16
VMEM_LIMIT = 56 * 1024 * 1024


def shape(*dims, dtype=F32):
    return jax.ShapeDtypeStruct(dims, dtype)


def whole(*dims):
    return pl.BlockSpec(dims, lambda i: (0,) * len(dims))


def rows_of(*dims):
    return pl.BlockSpec(dims, lambda i: (i,) + (0,) * (len(dims) - 1))


def later(spec):
    return pl.BlockSpec(spec.block_shape, lambda i: spec.index_map(i + 1))


def share_of(rows, devices):
    return -(-rows // devices)


def halves(values):
    high = values.astype(BF16)
    return high, (values - high.astype(F32)).astype(BF16)


def nn(former, latter):
    return lax.dot_general(former, latter, (((1,), (0,)), ((), ())), preferred_element_type=F32)


def nt(former, latter):
    return lax.dot_general(former, latter, (((1,), (1,)), ((), ())), preferred_element_type=F32)


def tn(former, latter):
    return lax.dot_general(former, latter, (((0,), (0,)), ((), ())), preferred_element_type=F32)


def product(kind, former, latter):
    return kind(former[0], latter[0]) + (kind(former[0], latter[1]) + kind(former[1], latter[0]))


def gelu_parts(values):
    below = 0.5 * (1.0 + lax.erf(values * 0.7071067811865476))
    density = 0.3989422804014327 * jnp.exp(-0.5 * values * values)
    return values * below, below + values * density


def normed_rows(values):
    center = jnp.mean(values, axis=-1, keepdims=True)
    moved = values - center
    rate = lax.rsqrt(jnp.mean(moved * moved, axis=-1, keepdims=True) + EPS_NORM)
    return moved * rate, rate


def normed_back(grad, hat, rate, gain):
    scaled = grad * gain
    first = jnp.mean(scaled, axis=-1, keepdims=True)
    second = jnp.mean(scaled * hat, axis=-1, keepdims=True)
    return rate * (scaled - first - hat * second)


def column_sum(values):
    return jnp.sum(values, axis=0, keepdims=True)


def head_mask():
    dims = (HEADS, TILE_ROWS, WIDTH)
    lane_head = lax.broadcasted_iota(jnp.int32, dims, 2) // TILE_ROWS
    return (lane_head == lax.broadcasted_iota(jnp.int32, dims, 0)).astype(F32)


def per_head(rows, mask):
    count = rows.shape[0] // TILE_ROWS
    return (rows.reshape(count, 1, TILE_ROWS, WIDTH) * mask[None]).reshape(count * WIDTH, WIDTH)


def from_heads(table, mask):
    parts = []
    for at in range(0, table.shape[1], WIDTH):
        turned = table[:, at : at + WIDTH].T.reshape(HEADS, TILE_ROWS, WIDTH)
        parts.append(jnp.sum(turned * mask, axis=0))
    return parts


def window_mix(query, key, value, live, mask, mask_low, keep_high, keep_low):
    query_high, query_low = halves(query)
    key_high, key_low = halves(key)
    key_stack = jnp.concatenate([key_high, key_low, key_high], axis=1)
    turned = halves(value.T)
    mixed = []
    for first, last in CHUNKS:
        rows = slice(first * TILE_ROWS, last * TILE_ROWS)
        lanes = slice(first * WIDTH, last * WIDTH)
        high = per_head(query_high[rows], mask_low)
        low = per_head(query_low[rows], mask_low)
        scores = nt(key_stack, jnp.concatenate([high, high, low], axis=1))
        scores = jnp.where(live > 0, scores, NEG_FILL)
        weights = jnp.exp(scores - jnp.max(scores, axis=0, keepdims=True))
        weights = weights * (1.0 / column_sum(weights))
        weights = halves(weights)
        keep_high[:, lanes] = weights[0]
        keep_low[:, lanes] = weights[1]
        mixed += from_heads(product(nn, turned, weights), mask)
    return jnp.concatenate(mixed, axis=0)


def window_back(query, key, value, grad_mixed, live, mask, mask_low, kept_high, kept_low):
    query_halves = halves(query)
    grad_halves = halves(grad_mixed)
    value_high, value_low = halves(value)
    value_stack = jnp.concatenate([value_high, value_low, value_high], axis=1)
    turned = halves(key.T)
    grad_key = jnp.zeros((CELLS, 2 * WIDTH), F32)
    grad_value = jnp.zeros((CELLS, 2 * WIDTH), F32)
    key_rest = jnp.zeros((CELLS, WIDTH), F32)
    value_rest = jnp.zeros((CELLS, WIDTH), F32)
    grad_query = []
    for first, last in CHUNKS:
        rows = slice(first * TILE_ROWS, last * TILE_ROWS)
        lanes = slice(first * WIDTH, last * WIDTH)
        query_high, query_low = (per_head(part[rows], mask_low) for part in query_halves)
        grad_high, grad_low = (per_head(part[rows], mask_low) for part in grad_halves)
        grad_weights = nt(value_stack, jnp.concatenate([grad_high, grad_high, grad_low], axis=1))
        high, low = kept_high[:, lanes], kept_low[:, lanes]
        weights = high.astype(F32) + low.astype(F32)
        grad_scores = weights * grad_weights
        grad_scores = live * (grad_scores - weights * column_sum(grad_scores))
        scores_high, scores_low = halves(grad_scores)
        grad_value += nn(high, jnp.concatenate([grad_high, grad_low], axis=1))
        value_rest += nn(low, grad_high)
        grad_key += nn(scores_high, jnp.concatenate([query_high, query_low], axis=1))
        key_rest += nn(scores_low, query_high)
        grad_query += from_heads(product(nn, turned, (scores_high, scores_low)), mask)
    return (
        0.25 * jnp.concatenate(grad_query, axis=0),
        grad_key[:, :WIDTH] + (grad_key[:, WIDTH:] + key_rest),
        grad_value[:, :WIDTH] + (grad_value[:, WIDTH:] + value_rest),
    )


def unpack_weights(packed, one, up_high, up_low, down_high, down_low, bias):
    ffns = packed.shape[0]
    units = bias.shape[1] // ffns
    for at in range(ffns):
        rows = slice(at * units, (at + 1) * units)
        high, low = halves(packed[at, one * units : (one + 1) * units])
        up_high[rows], up_low[rows] = high, low
        high, low = halves(packed[at, (2 + one) * units : (3 + one) * units])
        down_high[rows], down_low[rows] = high, low
    bias[...] = jnp.concatenate(
        [packed[at, 4 * units + one : 4 * units + one + 1, :units] for at in range(ffns)], axis=1
    )


def layer_rows(one, values, live, weights, saved):
    qkv_high, qkv_low, out_high, out_low, up, down, bias, back_bias, gains, offsets = weights
    packed_keep, high_keep, low_keep, mixed_keep, hat_one, rate_one, hidden_keep, slope, hat_two, rate_two = saved
    mask = head_mask()
    mask_low = mask.astype(BF16)
    qkv = product(nn, halves(values), (qkv_high[one], qkv_low[one]))
    query = 0.25 * qkv[:, :WIDTH]
    packed_keep[:, :WIDTH] = query
    packed_keep[:, WIDTH:] = qkv[:, WIDTH:]
    for at in range(STEP // CELLS):
        rows = slice(at * CELLS, (at + 1) * CELLS)
        mixed_keep[rows] = window_mix(
            query[rows],
            qkv[rows, WIDTH : 2 * WIDTH],
            qkv[rows, 2 * WIDTH :],
            live[rows],
            mask,
            mask_low,
            high_keep.at[at],
            low_keep.at[at],
        )
    mixed = mixed_keep[...]
    hat, rate = normed_rows(
        values + product(nn, halves(mixed), (out_high[one], out_low[one]))
    )
    hat_one[...] = hat
    rate_one[...] = jnp.broadcast_to(rate, hat.shape)
    first = hat * gains[2 * one : 2 * one + 1] + offsets[2 * one : 2 * one + 1]
    hidden, steep = gelu_parts(product(nt, halves(first), up) + bias)
    hidden_keep[...] = hidden
    slope[...] = steep
    summed = first + product(nn, halves(hidden), down) + back_bias[one : one + 1]
    hat, rate = normed_rows(summed)
    hat_two[...] = hat
    rate_two[...] = jnp.broadcast_to(rate, hat.shape)
    return hat * gains[2 * one + 1 : 2 * one + 2] + offsets[2 * one + 1 : 2 * one + 2]


def ffn_rows_back(one, grad, saved, weights, sums):
    mixed_keep, hat_one, rate_one, hidden_keep, slope, hat_two, rate_two = saved
    out, up, down, gains, offsets = weights
    small, sum_out, sum_up, sum_down = sums
    hat = hat_two[...]
    grad_summed = normed_back(grad, hat, rate_two[...], gains[2 * one + 1 : 2 * one + 2])
    small[3:4] += column_sum(grad * hat)
    small[4:5] += column_sum(grad)
    small[0:1] += column_sum(grad_summed)
    summed_halves = halves(grad_summed)
    grad_pre = product(nt, summed_halves, down) * slope[...]
    pre_halves = halves(grad_pre)
    hidden_halves = halves(hidden_keep[...])
    sum_down[...] += product(tn, hidden_halves, summed_halves)
    hat = hat_one[...]
    first = hat * gains[2 * one : 2 * one + 1] + offsets[2 * one : 2 * one + 1]
    sum_up[...] += product(tn, pre_halves, halves(first))
    bias_sum = column_sum(grad_pre)
    for at in range(bias_sum.shape[1] // WIDTH):
        small[5 + at : 6 + at] += bias_sum[:, at * WIDTH : (at + 1) * WIDTH]
    grad_first = grad_summed + product(nn, pre_halves, up)
    small[1:2] += column_sum(grad_first * hat)
    small[2:3] += column_sum(grad_first)
    grad_joined = normed_back(grad_first, hat, rate_one[...], gains[2 * one : 2 * one + 1])
    joined_halves = halves(grad_joined)
    sum_out[...] += product(tn, halves(mixed_keep[...]), joined_halves)
    return grad_joined, product(nt, joined_halves, out)


def attention_rows_back(one, values, live, grad_joined, grad_mixed, saved, qkv_weights, sum_qkv):
    packed_keep, high_keep, low_keep = saved
    mask = head_mask()
    mask_low = mask.astype(BF16)
    parts = []
    for at in range(STEP // CELLS):
        rows = slice(at * CELLS, (at + 1) * CELLS)
        parts.append(
            window_back(
                packed_keep[rows, :WIDTH],
                packed_keep[rows, WIDTH : 2 * WIDTH],
                packed_keep[rows, 2 * WIDTH :],
                grad_mixed[rows],
                live[rows],
                mask,
                mask_low,
                high_keep.at[at],
                low_keep.at[at],
            )
        )
    grad_packed = halves(
        jnp.concatenate([jnp.concatenate(part, axis=1) for part in parts], axis=0)
    )
    sum_qkv[...] += product(tn, halves(values), grad_packed)
    return grad_joined + product(nt, grad_packed, (qkv_weights[0][one], qkv_weights[1][one]))


def share_rows(target, at, values, devices):
    count = values.shape[0]
    share = share_of(count, devices)
    for device in range(devices):
        begin = device * share
        if begin < count:
            held = min(share, count - begin)
            target[device, at : at + held] = values[begin : begin + held]
    return at + share


def share_units(target, at, sum_up, sum_down, ffns):
    units = sum_up.shape[0] // ffns
    for f in range(ffns):
        rows = slice(f * units, (f + 1) * units)
        joined = jnp.concatenate([sum_up[rows], sum_down[rows]], axis=0)
        at = share_rows(target, at, joined, target.shape[0])
    return at


def joined_rows(table, at, count):
    devices = table.shape[0]
    share = share_of(count, devices)
    if share % 8 == 0 and share * devices == count:
        return table[:, at : at + share].reshape(count, WIDTH)
    pieces = []
    for device in range(devices):
        begin = device * share
        if begin < count:
            pieces.append(table[device, at : at + min(share, count - begin)])
    return jnp.concatenate(pieces, axis=0)


def vfe_kernel(
    feats_ref, weight_ref, occupied_ref, up_ref, down_ref, bias_ref, lifted_ref, live_ref, sent_ref, packed_ref
):
    devices = sent_ref.shape[0]
    units = up_ref.shape[1]
    feats = feats_ref[...]
    row_count = feats.shape[0]
    feats_halves = halves(feats)
    lifted = product(nn, feats_halves, halves(weight_ref[...]))
    lifted_ref[...] = lifted
    live = jnp.broadcast_to(occupied_ref[...].astype(F32).reshape(1, row_count), (8, row_count)).T[:, :1]
    live_ref[...] = live
    count = jnp.sum(live, axis=0, keepdims=True)
    total = column_sum(live * lifted)
    moved = live * (lifted - total / jnp.maximum(count, 1.0))
    sent_ref[...] = jnp.zeros(sent_ref.shape, F32)
    stats = jnp.concatenate(
        [
            jnp.broadcast_to(count, (1, WIDTH)),
            total,
            column_sum(moved * moved),
            column_sum(live * feats),
        ],
        axis=0,
    )
    sent_ref[:, 0:4] = jnp.broadcast_to(stats[None], (devices, 4, WIDTH))
    share_rows(sent_ref, 4, product(tn, feats_halves, halves(moved)), devices)
    for one in range(2):
        packed_ref[one * units : (one + 1) * units] = up_ref[one]
        packed_ref[(2 + one) * units : (3 + one) * units] = down_ref[one]
    packed_ref[4 * units :] = jnp.zeros((8, WIDTH), F32)
    packed_ref[4 * units : 4 * units + 2, :units] = bias_ref[...]


def places_of(source_ref):
    row_count = source_ref.shape[0]
    places = source_ref[...].reshape(1, row_count) - lax.axis_index(AXES) * row_count
    return jnp.where(places < 0, places + row_count * lax.axis_size(AXES), places)


def one_hot(former, latter):
    return (former == latter).astype(F32).astype(BF16)


def split_kernel(qkv_ref, out_ref, qkv_high, qkv_low, out_high, out_low):
    qkv_high[...], qkv_low[...] = halves(qkv_ref[...])
    out_high[...], out_low[...] = halves(out_ref[...])


def vfe_stats(seen_ref, stats_ref, product_ref):
    counts, totals, squares, lives = (seen_ref[:, at] for at in range(4))
    count = column_sum(counts)
    center = column_sum(totals) / count
    moves = totals / jnp.maximum(counts, 1.0) - center
    rate = lax.rsqrt(column_sum(squares + counts * moves * moves) / count + EPS_NORM)
    stats_ref[...] = jnp.zeros(stats_ref.shape, F32)
    stats_ref[0:1] = count
    stats_ref[1:2] = center
    stats_ref[2:3] = rate
    stats_ref[3:4] = column_sum(lives)
    devices = seen_ref.shape[0]
    share = share_of(WIDTH, devices)
    mine = lax.axis_index(AXES) * share
    lanes = lax.broadcasted_iota(jnp.int32, lives.shape, 1)
    product_ref[...] = jnp.zeros(product_ref.shape, F32)
    for at in range(share):
        picked = jnp.sum(jnp.where(lanes == mine + at, lives, 0.0), axis=1, keepdims=True)
        product_ref[at : at + 1] = rate * column_sum(seen_ref[:, 4 + at] + picked * moves)


def first_kernel(*refs, tail):
    lifted_ref, live_ref = refs[:2]
    bn_gain, bn_shift, qkv_high, qkv_low, out_high, out_low, packed, back_bias, gains, offsets = refs[2:12]
    if tail:
        stats = refs[12]
        refs = refs[27:]
    else:
        cotangent_ref, seen_ref, edge, stats, hat_product = refs[12:17]
        refs = refs[17:]
    result, vfe_hat, vfe_slope, carried = refs[:4]
    saved = refs[4:14]
    up_high, up_low, down_high, down_low, bias = refs[14:]

    @pl.when(pl.program_id(0) == 0)
    def _():
        unpack_weights(packed, 0, up_high, up_low, down_high, down_low, bias)
        if not tail:
            vfe_stats(seen_ref, stats, hat_product)

    hat = (lifted_ref[...] - stats[1:2]) * stats[2:3]
    values, steep = gelu_parts(hat * bn_gain[0:1] + bn_shift[0:1])
    vfe_hat[...] = hat
    vfe_slope[...] = steep
    carried[...] = values
    live = live_ref[...]
    rows = layer_rows(
        0,
        values,
        live,
        (
            qkv_high,
            qkv_low,
            out_high,
            out_low,
            (up_high[...], up_low[...]),
            (down_high[...], down_low[...]),
            bias[...],
            back_bias,
            gains,
            offsets,
        ),
        saved,
    )
    result[...] = rows
    if not tail:
        edge[:, :WIDTH] = rows[:HALF]
        edge[:, WIDTH : 2 * WIDTH] = cotangent_ref[:HALF]
        edge[:, 2 * WIDTH :] = jnp.broadcast_to(live[:HALF], (HALF, WIDTH))


def second_kernel(
    first_ref,
    cotangent_ref,
    live_ref,
    edge,
    source_ref,
    qkv_high,
    qkv_low,
    out_high,
    out_low,
    packed,
    back_bias,
    gains,
    offsets,
    result,
    sent,
    live_keep,
    cotangent_keep,
    carried,
    packed_keep,
    high_keep,
    low_keep,
    mixed_keep,
    hat_one,
    rate_one,
    hidden_keep,
    slope,
    hat_two,
    rate_two,
    up_high,
    up_low,
    down_high,
    down_low,
    bias,
    table,
    sums,
    column,
):
    at = pl.program_id(0)
    row_count = first_ref.shape[0]

    @pl.when(at == 0)
    def _():
        unpack_weights(packed, 1, up_high, up_low, down_high, down_low, bias)
        high, low = halves(first_ref[...])
        table[:row_count, :WIDTH] = high
        table[:row_count, WIDTH : 2 * WIDTH] = low
        high, low = halves(cotangent_ref[...])
        table[:row_count, 2 * WIDTH : 3 * WIDTH] = high
        table[:row_count, 3 * WIDTH : 4 * WIDTH] = low
        table[:row_count, 4 * WIDTH :] = jnp.broadcast_to(live_ref[...], (row_count, WIDTH)).astype(BF16)
        spare = table.shape[0] - row_count
        tail = jnp.concatenate([edge[...], jnp.zeros((spare - HALF, 3 * WIDTH), F32)], axis=0)
        high, low = halves(tail)
        table[row_count:, :WIDTH] = high[:, :WIDTH]
        table[row_count:, WIDTH : 2 * WIDTH] = low[:, :WIDTH]
        table[row_count:, 2 * WIDTH : 3 * WIDTH] = high[:, WIDTH : 2 * WIDTH]
        table[row_count:, 3 * WIDTH : 4 * WIDTH] = low[:, WIDTH : 2 * WIDTH]
        table[row_count:, 4 * WIDTH :] = high[:, 2 * WIDTH :]
        sums[...] = jnp.zeros(sums.shape, F32)
        places = jnp.broadcast_to(places_of(source_ref).astype(F32), (8, row_count))
        column[...] = places.T[:, :1].astype(jnp.int32)

    lanes = lax.broadcasted_iota(jnp.int32, (STEP, table.shape[0]), 1)
    gathered = nn(one_hot(lanes, column[pl.ds(at * STEP, STEP)]), table[...])
    values = gathered[:, :WIDTH] + gathered[:, WIDTH : 2 * WIDTH]
    live = gathered[:, 4 * WIDTH :]
    grad = live * (gathered[:, 2 * WIDTH : 3 * WIDTH] + gathered[:, 3 * WIDTH : 4 * WIDTH])
    carried[...] = values
    cotangent_keep[...] = grad
    live_keep[...] = live[:, :1]
    rows = layer_rows(
        1,
        values,
        live[:, :1],
        (
            qkv_high,
            qkv_low,
            out_high,
            out_low,
            (up_high[...], up_low[...]),
            (down_high[...], down_low[...]),
            bias[...],
            back_bias,
            gains,
            offsets,
        ),
        (packed_keep, high_keep, low_keep, mixed_keep, hat_one, rate_one, hidden_keep, slope, hat_two, rate_two),
    )
    result[...] = rows
    count = column_sum(live)

    @pl.when(at == 0)
    def _():
        sums[5:6] = column_sum(live * rows) / jnp.maximum(count, 1.0)

    moved = rows - sums[5:6]
    sums[0:1] += count
    sums[1:2] += column_sum(live * moved)
    sums[2:3] += column_sum(live * moved * moved)
    sums[3:4] += column_sum(grad)
    sums[4:5] += column_sum(grad * moved)

    @pl.when(at == pl.num_programs(0) - 1)
    def _():
        count = sums[0:1]
        move = sums[1:2] / jnp.maximum(count, 1.0)
        stats = jnp.concatenate(
            [
                count,
                sums[5:6] + move,
                sums[2:3] - count * move * move,
                sums[3:4],
                sums[4:5] - move * sums[3:4],
                jnp.zeros((3, WIDTH), F32),
            ],
            axis=0,
        )
        sent[...] = jnp.broadcast_to(stats[None], sent.shape)


def second_back_kernel(
    result,
    seen_ref,
    bn_gain,
    bn_shift,
    source_ref,
    qkv_high,
    qkv_low,
    out_high,
    out_low,
    packed,
    gains,
    offsets,
    live_keep,
    cotangent_keep,
    carried,
    packed_keep,
    high_keep,
    low_keep,
    mixed_keep,
    hat_one,
    rate_one,
    hidden_keep,
    slope,
    hat_two,
    rate_two,
    shared,
    edge,
    grad_rows,
    out_rows,
    neck,
    small,
    up_high,
    up_low,
    down_high,
    down_low,
    bias,
    stats,
    sum_qkv,
    sum_out,
    sum_up,
    sum_down,
    placed,
    places_ref,
    *,
    ffns,
):
    at = pl.program_id(0)
    row_count = grad_rows.shape[0]

    @pl.when(at == 0)
    def _():
        unpack_weights(packed, 1, up_high, up_low, down_high, down_low, bias)
        counts, means, squares, grads, products = (seen_ref[:, row] for row in range(5))
        count = column_sum(counts)
        center = column_sum(counts * means) / count
        moves = means - center
        rate = lax.rsqrt(column_sum(squares + counts * moves * moves) / count + EPS_NORM)
        stats[0:1] = count
        stats[1:2] = center
        stats[2:3] = rate
        stats[3:4] = rate * column_sum(products + moves * grads)
        stats[4:5] = column_sum(grads)
        neck[...] = jnp.zeros(neck.shape, F32)
        neck[0:2] = stats[3:5]
        for held in (small, sum_qkv, sum_out, sum_up, sum_down, placed):
            held[...] = jnp.zeros(held.shape, F32)
        places = places_of(source_ref)
        for step in range(places_ref.shape[0]):
            places_ref[step] = places[:, step * STEP : (step + 1) * STEP]

    live = live_keep[...]
    rate = stats[2:3]
    hat = (result[...] - stats[1:2]) * rate
    neck_rows = live * (hat * bn_gain[1:2] + bn_shift[1:2])
    grad = rate * bn_gain[1:2] * (
        cotangent_keep[...] - live * (hat * stats[3:4] + stats[4:5]) / stats[0:1]
    )
    grad_joined, grad_mixed = ffn_rows_back(
        1,
        grad,
        (mixed_keep, hat_one, rate_one, hidden_keep, slope, hat_two, rate_two),
        (
            (out_high[1], out_low[1]),
            (up_high[...], up_low[...]),
            (down_high[...], down_low[...]),
            gains,
            offsets,
        ),
        (small, sum_out, sum_up, sum_down),
    )
    grad_values = attention_rows_back(
        1,
        carried[...],
        live,
        grad_joined,
        grad_mixed,
        (packed_keep, high_keep, low_keep),
        (qkv_high, qkv_low),
        sum_qkv,
    )
    pieces = halves(grad_values) + halves(neck_rows)
    down = lax.broadcasted_iota(jnp.int32, (placed.shape[0], STEP), 0)
    moved = nn(one_hot(down, places_ref[at]), jnp.concatenate(pieces, axis=1))
    placed[:, :WIDTH] += moved[:, :WIDTH] + moved[:, WIDTH : 2 * WIDTH]
    placed[:, WIDTH:] += moved[:, 2 * WIDTH : 3 * WIDTH] + moved[:, 3 * WIDTH :]

    @pl.when(at == pl.num_programs(0) - 1)
    def _():
        grad_rows[...] = placed[:row_count, :WIDTH]
        out_rows[...] = placed[:row_count, WIDTH:]
        edge[...] = placed[row_count : row_count + HALF]
        devices = shared.shape[0]
        shared[...] = jnp.zeros(shared.shape, F32)
        row = share_units(shared, 0, sum_up, sum_down, ffns)
        for block in range(3):
            row = share_rows(shared, row, sum_qkv[:, block * WIDTH : (block + 1) * WIDTH], devices)
        share_rows(shared, row, sum_out, devices)


def first_ffn_back_kernel(*refs, tail):
    grad_rows, out_high, out_low, packed, gains, offsets = refs[:6]
    keeps = refs[6:13]
    refs = refs[13:]
    if tail:
        edge, out_rows = refs[:2]
        held_sums = refs[2:6]
        grad_joined, grad_mixed, pillars = refs[8:11]
        sums = refs[11:15]
        refs = refs[15:]
    else:
        grad_joined, grad_mixed = refs[:2]
        sums = refs[2:6]
        refs = refs[6:]
    up_high, up_low, down_high, down_low, bias = refs[:5]
    grad = grad_rows

    @pl.when(pl.program_id(0) == 0)
    def _():
        unpack_weights(packed, 0, up_high, up_low, down_high, down_low, bias)
        for at, held in enumerate(sums):
            held[...] = held_sums[at][...] if tail else jnp.zeros(held.shape, F32)

    if tail:
        grad = refs[5]
        grad[...] = grad_rows[...]
        grad[:HALF] = edge[:, :WIDTH]
        pillars[...] = out_rows[...]
        pillars[:HALF] = edge[:, WIDTH:]
    joined, mixed = ffn_rows_back(
        0,
        grad[...],
        keeps,
        (
            (out_high[0], out_low[0]),
            (up_high[...], up_low[...]),
            (down_high[...], down_low[...]),
            gains,
            offsets,
        ),
        sums,
    )
    grad_joined[...] = joined
    grad_mixed[...] = mixed


def first_attention_back_kernel(
    grad_joined,
    grad_mixed,
    feats_ref,
    live_ref,
    carried,
    vfe_hat,
    vfe_slope,
    qkv_high,
    qkv_low,
    packed_keep,
    high_keep,
    low_keep,
    small_second,
    small_ffn,
    sum_out,
    sum_up,
    sum_down,
    grad_affine,
    shared,
    sum_qkv,
    sum_feats,
    small,
    *,
    ffns,
):
    at = pl.program_id(0)

    @pl.when(at == 0)
    def _():
        for held in (small, sum_qkv, sum_feats):
            held[...] = jnp.zeros(held.shape, F32)

    grad = attention_rows_back(
        0,
        carried[...],
        live_ref[...],
        grad_joined[...],
        grad_mixed[...],
        (packed_keep, high_keep, low_keep),
        (qkv_high, qkv_low),
        sum_qkv,
    )
    grad = grad * vfe_slope[...]
    grad_affine[...] = grad
    small[0:1] += column_sum(grad * vfe_hat[...])
    small[1:2] += column_sum(grad)
    sum_feats[...] += product(tn, halves(feats_ref[...]), halves(grad))

    @pl.when(at == pl.num_programs(0) - 1)
    def _():
        devices = shared.shape[0]
        shared[...] = jnp.zeros(shared.shape, F32)
        row = share_units(shared, 0, sum_up, sum_down, ffns)
        for block in range(3):
            row = share_rows(shared, row, sum_qkv[:, block * WIDTH : (block + 1) * WIDTH], devices)
        row = share_rows(shared, row, sum_out, devices)
        row = share_rows(shared, row, small_second[...], devices)
        row = share_rows(shared, row, small_ffn[...], devices)
        row = share_rows(shared, row, sum_feats, devices)
        shared[:, row : row + 2] = jnp.broadcast_to(small[0:2][None], (devices, 2, WIDTH))


def relay_kernel(early, late, hat_product, stats, bn_gain, returned, vfe_grads, *, ffns, counts):
    unit_rows, early_rows, late_rows, part = counts
    devices = returned.shape[0]
    early_total = jnp.sum(early[...], axis=0)
    late_total = jnp.sum(late[...], axis=0)
    begin = ffns * unit_rows
    end = begin + late_rows
    gain, shift = late_total[end + part : end + part + 1], late_total[end + part + 1 : end + part + 2]
    lanes = lax.broadcasted_iota(jnp.int32, (part, WIDTH), 1)
    mine = lax.axis_index(AXES) * part + lax.broadcasted_iota(jnp.int32, (part, WIDTH), 0)
    live_sum = jnp.sum(jnp.where(lanes == mine, stats[3:4], 0.0), axis=1, keepdims=True)
    grad_w_vfe = stats[2:3] * bn_gain[0:1] * (
        late_total[end : end + part] - (hat_product[:part] * gain + live_sum * shift) / stats[0:1]
    )
    rows = jnp.concatenate(
        [early_total[begin : begin + early_rows], late_total[begin:end], grad_w_vfe], axis=0
    )
    room = returned.shape[1] - 2 * unit_rows
    if rows.shape[0] < room:
        rows = jnp.concatenate([rows, jnp.zeros((room - rows.shape[0], WIDTH), F32)], axis=0)
    returned[:, 2 * unit_rows :] = jnp.broadcast_to(rows[None], (devices,) + rows.shape)
    for device in range(devices):
        block = device % ffns
        for at, total in enumerate((early_total, late_total)):
            returned[device, at * unit_rows : (at + 1) * unit_rows] = total[
                block * unit_rows : (block + 1) * unit_rows
            ]
    vfe_grads[...] = jnp.concatenate([gain, shift, jnp.zeros((6, WIDTH), F32)], axis=0)


def feats_back_kernel(grad_affine, vfe_hat, live_ref, stats, vfe_grads, bn_gain, weight_ref, grad_feats):
    sums = vfe_grads[...]
    scale = stats[2:3] * bn_gain[0:1]
    grad = scale * (
        grad_affine[...]
        - live_ref[...] * (vfe_hat[...] * sums[0:1] + sums[1:2]) / stats[0:1]
    )
    grad_feats[...] = product(nt, halves(grad), halves(weight_ref[...]))


def last_kernel(
    returned,
    vfe_grads,
    neck,
    grad_w_vfe,
    grad_bn_gain,
    grad_bn_shift,
    grad_w_qkv,
    grad_w_out,
    grad_w_in,
    grad_b_in,
    grad_w_back,
    grad_b_back,
    grad_ln_gain,
    grad_ln_shift,
    *,
    ffns,
):
    devices = returned.shape[0]
    units = grad_w_in.shape[1]
    part = share_of(WIDTH, devices)
    unit_rows = share_of(2 * units, devices)
    at = 0

    def take(count):
        nonlocal at
        rows = joined_rows(returned, at, count)
        at += share_of(count, devices)
        return rows

    blocks = [take(2 * units) for layer in range(2)]
    mine = lax.rem(lax.axis_index(AXES), ffns)
    for layer in (1, 0):
        grad_w_in[layer] = blocks[1 - layer][:units]
        grad_w_back[layer] = blocks[1 - layer][units:]
        for block in range(3):
            grad_w_qkv[layer, :, block * WIDTH : (block + 1) * WIDTH] = take(WIDTH)
        grad_w_out[layer] = take(WIDTH)
    for layer in (1, 0):
        small = take(8)
        grad_b_back[layer : layer + 1] = small[0:1]
        grad_ln_gain[2 * layer : 2 * layer + 1] = small[1:2]
        grad_ln_shift[2 * layer : 2 * layer + 1] = small[2:3]
        grad_ln_gain[2 * layer + 1 : 2 * layer + 2] = small[3:4]
        grad_ln_shift[2 * layer + 1 : 2 * layer + 2] = small[4:5]
        held = jnp.zeros((1, units), F32)
        for f in range(ffns):
            row, lane = divmod(f * units, WIDTH)
            held = jnp.where(mine == f, small[5 + row : 6 + row, lane : lane + units], held)
        grad_b_in[layer : layer + 1] = held
    grad_w_vfe[...] = take(WIDTH)
    grad_bn_gain[0:1] = vfe_grads[0:1]
    grad_bn_gain[1:2] = neck[0:1]
    grad_bn_shift[0:1] = vfe_grads[1:2]
    grad_bn_shift[1:2] = neck[1:2]


def spread_rows(pieces, axes):
    return lax.all_to_all(pieces, axes, 0, 0)


def passed_along(rows, by):
    peers = lax.axis_size(AXES)
    return lax.ppermute(rows, AXES, [(i, (i + by) % peers) for i in range(peers)])


def params():
    return pltpu.CompilerParams(vmem_limit_bytes=VMEM_LIMIT)


def cost(flops, size):
    return pl.CostEstimate(flops=int(flops), bytes_accessed=int(size), transcendentals=0)


def on_device(
    pillar_feats,
    occupied,
    shifted_source_rows,
    w_vfe,
    bn_gain,
    bn_shift,
    query_key_value_weight,
    attention_output_weight,
    up_weight_matrix,
    up_bias_rows,
    down_weight_matrix,
    down_bias_rows,
    layernorm_gains,
    layernorm_offsets,
    cotangent,
):
    row_count = pillar_feats.shape[0]
    steps = row_count // STEP
    held = row_count + -(-HALF // 16) * 16
    wins, ffns = lax.axis_size("win"), lax.axis_size("ffn")
    devices = wins * ffns
    units = up_weight_matrix.shape[2]
    hidden = units * ffns
    part = share_of(WIDTH, devices)
    stats_rows = -(-(4 + part) // 8) * 8

    lifted, live, sent, packed = pl.pallas_call(
        vfe_kernel,
        out_shape=(
            shape(row_count, WIDTH),
            shape(row_count, 1),
            shape(devices, stats_rows, WIDTH),
            shape(4 * units + 8, WIDTH),
        ),
        compiler_params=params(),
        name="vfe",
    )(
        pillar_feats,
        w_vfe,
        occupied,
        up_weight_matrix.transpose(0, 2, 1),
        down_weight_matrix,
        up_bias_rows,
    )
    seen = spread_rows(sent, AXES)
    packed = lax.all_gather(packed, "ffn", axis=0, tiled=False)
    qkv_high, qkv_low, out_high, out_low = pl.pallas_call(
        split_kernel,
        out_shape=(
            shape(2, WIDTH, 3 * WIDTH, dtype=BF16),
            shape(2, WIDTH, 3 * WIDTH, dtype=BF16),
            shape(2, WIDTH, WIDTH, dtype=BF16),
            shape(2, WIDTH, WIDTH, dtype=BF16),
        ),
        compiler_params=params(),
        cost_estimate=cost(1e6, 1e6),
        name="split",
    )(query_key_value_weight, attention_output_weight)

    rows_spec = rows_of(STEP, WIDTH)
    column_spec = rows_of(STEP, 1)
    qkv_specs = [whole(2, WIDTH, 3 * WIDTH)] * 2
    out_specs = [whole(2, WIDTH, WIDTH)] * 2
    packed_spec = whole(*packed.shape)
    norm_specs = [whole(4, WIDTH)] * 2
    pair_spec = whole(2, WIDTH)
    seen_spec = whole(devices, stats_rows, WIDTH)
    eight_spec = whole(8, WIDTH)
    unit_scratch = [pltpu.VMEM((hidden, WIDTH), BF16)] * 4 + [pltpu.VMEM((1, hidden), F32)]
    keep_specs = [
        rows_spec,
        rows_of(STEP, 3 * WIDTH),
        rows_of(STEP // CELLS, CELLS, HEADS * CELLS),
        rows_of(STEP // CELLS, CELLS, HEADS * CELLS),
        rows_spec,
        rows_spec,
        rows_spec,
        rows_of(STEP, hidden),
        rows_of(STEP, hidden),
        rows_spec,
        rows_spec,
    ]
    windows = row_count // CELLS
    row_shape = shape(row_count, WIDTH)
    keep_shapes = [
        row_shape,
        shape(row_count, 3 * WIDTH),
        shape(windows, CELLS, HEADS * CELLS, dtype=BF16),
        shape(windows, CELLS, HEADS * CELLS, dtype=BF16),
        row_shape,
        row_shape,
        row_shape,
        shape(row_count, hidden),
        shape(row_count, hidden),
        row_shape,
        row_shape,
    ]

    first_arrays = [row_shape, row_shape, row_shape] + keep_shapes
    first_specs = [rows_spec, rows_spec, rows_spec] + keep_specs
    first_shared = [pair_spec, pair_spec] + qkv_specs + out_specs + [packed_spec, pair_spec] + norm_specs
    first_held = (
        bn_gain,
        bn_shift,
        qkv_high,
        qkv_low,
        out_high,
        out_low,
        packed,
        down_bias_rows,
        layernorm_gains,
        layernorm_offsets,
    )
    edge, stats, hat_product, *first_arrays_out = pl.pallas_call(
        functools.partial(first_kernel, tail=False),
        grid=(1,),
        in_specs=[rows_spec, column_spec] + first_shared + [rows_spec, seen_spec],
        out_specs=[whole(HALF, 3 * WIDTH), eight_spec, eight_spec] + first_specs,
        out_shape=[shape(HALF, 3 * WIDTH), shape(8, WIDTH), shape(8, WIDTH)] + first_arrays,
        scratch_shapes=unit_scratch,
        compiler_params=params(),
        cost_estimate=cost(1e9, 4e6),
        name="first",
    )(lifted, live, *first_held, cotangent, seen)
    arrived = passed_along(edge, -1)
    first_out, vfe_hat, vfe_slope, *first_keep = pl.pallas_call(
        functools.partial(first_kernel, tail=True),
        grid=(steps - 1,),
        in_specs=[later(spec) for spec in (rows_spec, column_spec)]
        + first_shared
        + [eight_spec]
        + [pl.BlockSpec(memory_space=pl.ANY)] * len(first_arrays),
        out_specs=[later(spec) for spec in first_specs],
        out_shape=first_arrays,
        input_output_aliases={13 + at: at for at in range(len(first_arrays))},
        scratch_shapes=unit_scratch,
        compiler_params=params(),
        cost_estimate=cost(2e9, 8e6),
        name="first_rest",
    )(lifted, live, *first_held, stats, *first_arrays_out)
    edge = arrived
    second_out, sent, live_keep, cotangent_keep, *second_keep = pl.pallas_call(
        second_kernel,
        grid=(steps,),
        in_specs=[
            whole(row_count, WIDTH),
            whole(row_count, WIDTH),
            whole(row_count, 1),
            whole(HALF, 3 * WIDTH),
            whole(row_count),
        ]
        + qkv_specs
        + out_specs
        + [packed_spec, pair_spec]
        + norm_specs,
        out_specs=[rows_spec, whole(devices, 8, WIDTH), column_spec, rows_spec] + keep_specs,
        out_shape=[row_shape, shape(devices, 8, WIDTH), shape(row_count, 1), row_shape] + keep_shapes,
        scratch_shapes=unit_scratch
        + [pltpu.VMEM((held, 5 * WIDTH), BF16), pltpu.VMEM((8, WIDTH), F32), pltpu.VMEM((row_count, 1), jnp.int32)],
        compiler_params=params(),
        cost_estimate=cost(4e9, 12e6),
        name="second",
    )(
        first_out,
        cotangent,
        live,
        edge,
        shifted_source_rows,
        qkv_high,
        qkv_low,
        out_high,
        out_low,
        packed,
        down_bias_rows,
        layernorm_gains,
        layernorm_offsets,
    )
    seen = spread_rows(sent, AXES)
    piece = share_of(2 * units, devices)
    rest = 4 * part + 2 * share_of(8, devices)
    early_rows = -(-(ffns * piece + 4 * part) // 8) * 8
    late_rows = -(-(ffns * piece + rest + part + 2) // 8) * 8
    returned_rows = -(-(2 * piece + 4 * part + rest + part) // 8) * 8
    sum_scratch = [
        pltpu.VMEM((8, WIDTH), F32),
        pltpu.VMEM((WIDTH, 3 * WIDTH), F32),
        pltpu.VMEM((WIDTH, WIDTH), F32),
        pltpu.VMEM((hidden, WIDTH), F32),
        pltpu.VMEM((hidden, WIDTH), F32),
    ]
    shared, edge, grad_rows, out_rows, neck, small = pl.pallas_call(
        functools.partial(second_back_kernel, ffns=ffns),
        grid=(steps,),
        in_specs=[rows_spec, whole(devices, 8, WIDTH), pair_spec, pair_spec, whole(row_count)]
        + qkv_specs
        + out_specs
        + [packed_spec]
        + norm_specs
        + [column_spec, rows_spec]
        + keep_specs,
        out_specs=[
            whole(devices, early_rows, WIDTH),
            whole(HALF, 2 * WIDTH),
            whole(row_count, WIDTH),
            whole(row_count, WIDTH),
            eight_spec,
            eight_spec,
        ],
        out_shape=[
            shape(devices, early_rows, WIDTH),
            shape(HALF, 2 * WIDTH),
            row_shape,
            row_shape,
            shape(8, WIDTH),
            shape(8, WIDTH),
        ],
        scratch_shapes=unit_scratch
        + [pltpu.VMEM((8, WIDTH), F32)]
        + sum_scratch[1:]
        + [pltpu.VMEM((held, 2 * WIDTH), F32), pltpu.VMEM((steps, 1, STEP), jnp.int32)],
        compiler_params=params(),
        cost_estimate=cost(8e9, 12e6),
        name="second_back",
    )(
        second_out,
        seen,
        bn_gain,
        bn_shift,
        shifted_source_rows,
        qkv_high,
        qkv_low,
        out_high,
        out_low,
        packed,
        layernorm_gains,
        layernorm_offsets,
        live_keep,
        cotangent_keep,
        *second_keep,
    )
    arrived = passed_along(edge, 1)
    carried, packed_keep, high_keep, low_keep, *ffn_keep = first_keep
    back_specs = [rows_spec] + out_specs + [packed_spec] + norm_specs + keep_specs[4:]
    back_held = (grad_rows, out_high, out_low, packed, layernorm_gains, layernorm_offsets, *ffn_keep)
    sum_shapes = [shape(8, WIDTH), shape(WIDTH, WIDTH), shape(hidden, WIDTH), shape(hidden, WIDTH)]
    sum_specs = [whole(*held.shape) for held in sum_shapes]
    grad_joined, grad_mixed, *sums = pl.pallas_call(
        functools.partial(first_ffn_back_kernel, tail=False),
        grid=(steps - 1,),
        in_specs=[later(rows_spec)]
        + back_specs[1:6]
        + [later(spec) for spec in back_specs[6:]],
        out_specs=[later(rows_spec), later(rows_spec)] + sum_specs,
        out_shape=[row_shape, row_shape] + sum_shapes,
        scratch_shapes=unit_scratch,
        compiler_params=params(),
        cost_estimate=cost(2e9, 4e6),
        name="first_ffn_back",
    )(*back_held)
    shared, arrived, grad_joined = lax.optimization_barrier((shared, arrived, grad_joined))
    early = spread_rows(shared, AXES)
    grad_joined, grad_mixed, pillars_out, *sums = pl.pallas_call(
        functools.partial(first_ffn_back_kernel, tail=True),
        grid=(1,),
        in_specs=back_specs
        + [whole(HALF, 2 * WIDTH), rows_spec]
        + sum_specs
        + [pl.BlockSpec(memory_space=pl.ANY)] * 2,
        out_specs=[rows_spec] * 3 + sum_specs,
        out_shape=[row_shape] * 3 + sum_shapes,
        input_output_aliases={14: 2, 19: 0, 20: 1},
        scratch_shapes=unit_scratch + [pltpu.VMEM((STEP, WIDTH), F32)],
        compiler_params=params(),
        cost_estimate=cost(1e9, 2e6),
        name="first_ffn_back_edge",
    )(*back_held, arrived, out_rows, *sums, grad_joined, grad_mixed)
    grad_affine, shared = pl.pallas_call(
        functools.partial(first_attention_back_kernel, ffns=ffns),
        grid=(steps,),
        in_specs=[rows_spec, rows_spec, rows_spec, column_spec, rows_spec, rows_spec, rows_spec]
        + qkv_specs
        + keep_specs[1:4]
        + [eight_spec]
        + sum_specs,
        out_specs=[rows_spec, whole(devices, late_rows, WIDTH)],
        out_shape=[row_shape, shape(devices, late_rows, WIDTH)],
        scratch_shapes=[sum_scratch[1], sum_scratch[2], sum_scratch[0]],
        compiler_params=params(),
        cost_estimate=cost(6e9, 8e6),
        name="first_attention_back",
    )(
        grad_joined,
        grad_mixed,
        pillar_feats,
        live,
        carried,
        vfe_hat,
        vfe_slope,
        qkv_high,
        qkv_low,
        packed_keep,
        high_keep,
        low_keep,
        small,
        *sums,
    )
    early, shared = lax.optimization_barrier((early, shared))
    late = spread_rows(shared, AXES)
    returned, vfe_grads = pl.pallas_call(
        functools.partial(relay_kernel, ffns=ffns, counts=(piece, 4 * part, rest, part)),
        out_shape=(shape(devices, returned_rows, WIDTH), shape(8, WIDTH)),
        compiler_params=params(),
        name="relay",
    )(early, late, hat_product, stats, bn_gain)
    returned = spread_rows(returned, AXES)
    grad_feats = pl.pallas_call(
        feats_back_kernel,
        out_shape=row_shape,
        compiler_params=params(),
        cost_estimate=cost(1e8, 2e6),
        name="feats_back",
    )(grad_affine, vfe_hat, live, stats, vfe_grads, bn_gain, w_vfe)
    grads = list(pl.pallas_call(
        functools.partial(last_kernel, ffns=ffns),
        out_shape=(
            shape(WIDTH, WIDTH),
            shape(2, WIDTH),
            shape(2, WIDTH),
            shape(2, WIDTH, 3 * WIDTH),
            shape(2, WIDTH, WIDTH),
            shape(2, units, WIDTH),
            shape(2, units),
            shape(2, units, WIDTH),
            shape(2, WIDTH),
            shape(4, WIDTH),
            shape(4, WIDTH),
        ),
        compiler_params=params(),
        name="last",
    )(returned, vfe_grads, neck))
    grads[5] = grads[5].transpose(0, 2, 1)
    return (pillars_out, grad_feats, *grads)


def solution(mesh):
    return jax.shard_map(
        on_device,
        mesh=mesh,
        in_specs=(
            P(("win", "ffn"), None),
            P(("win", "ffn")),
            P(("win", "ffn")),
            P(),
            P(),
            P(),
            P(),
            P(),
            P(None, None, "ffn"),
            P(None, "ffn"),
            P(None, "ffn", None),
            P(),
            P(),
            P(),
            P(("win", "ffn"), None),
        ),
        out_specs=(
            P(("win", "ffn"), None),
            P(("win", "ffn"), None),
            P(),
            P(),
            P(),
            P(),
            P(),
            P(None, None, "ffn"),
            P(None, "ffn"),
            P(None, "ffn", None),
            P(),
            P(),
            P(),
        ),
        check_vma=False,
    )
```

```python
import functools

import jax
import jax.numpy as jnp
from jax import lax
from jax.experimental import pallas as pl
from jax.experimental.pallas import tpu as pltpu
from jax.sharding import PartitionSpec as P

HEADS = 8
CELLS = 144
HALF = CELLS // 2
WIDTH = 128
EPS_NORM = 1e-05
NEG_FILL = -1000000000.0
AXES = ("win", "ffn")
STEP = 3 * CELLS
TILE_ROWS = WIDTH // HEADS
TILES = CELLS // TILE_ROWS
CHUNKS = ((0, 2), (2, 4), (4, 6), (6, 8), (8, 9))
F32 = jnp.float32
BF16 = jnp.bfloat16
VMEM_LIMIT = 28 * 1024 * 1024


def shape(*dims, dtype=F32):
    return pltpu.HBM(dims, dtype)


def kept(*dims, dtype=F32):
    return pltpu.VMEM(dims, dtype)


class Pinned:
    def __init__(self, value):
        self.value = value


class Far:
    def __init__(self, value):
        self.value = value


def run(kernel, name, outs, args, scratch=(), copies=0, flops=1e8):
    near, far = pl.BlockSpec(memory_space=pltpu.VMEM), pl.BlockSpec(memory_space=pltpu.HBM)
    values = []
    for arg in args:
        space = pltpu.VMEM if isinstance(arg, Pinned) else pltpu.HBM
        value = arg.value if isinstance(arg, (Pinned, Far)) else arg
        values.append(pltpu.with_memory_space_constraint(value, space))
    scratch = list(scratch)
    if copies:
        scratch.append(pltpu.SemaphoreType.DMA((copies,)))
    return pl.pallas_call(
        kernel,
        out_shape=[out.value if isinstance(out, Far) else out for out in outs],
        in_specs=[far if isinstance(arg, Far) else near for arg in args],
        out_specs=[far if isinstance(out, Far) else near for out in outs],
        scratch_shapes=scratch,
        compiler_params=pltpu.CompilerParams(vmem_limit_bytes=VMEM_LIMIT),
        cost_estimate=pl.CostEstimate(flops=int(flops), bytes_accessed=1000000, transcendentals=0),
        name=name,
    )(*values)


def pinned(values):
    return [Pinned(value) for value in values]


class Copies:
    def __init__(self, semaphores):
        self.semaphores = semaphores
        self.started = []

    def start(self, source, target):
        copy = pltpu.make_async_copy(source, target, self.semaphores.at[len(self.started)])
        copy.start()
        self.started.append(copy)
        return copy


def scratch_like(arrays):
    return [pltpu.VMEM(array.shape, array.dtype) for array in arrays]


def share_of(rows, devices):
    return -(-rows // devices)


def halves(values):
    high = values.astype(BF16)
    return high, (values - high.astype(F32)).astype(BF16)


def nn(former, latter):
    return lax.dot_general(former, latter, (((1,), (0,)), ((), ())), preferred_element_type=F32)


def nt(former, latter):
    return lax.dot_general(former, latter, (((1,), (1,)), ((), ())), preferred_element_type=F32)


def tn(former, latter):
    return lax.dot_general(former, latter, (((0,), (0,)), ((), ())), preferred_element_type=F32)


def product(kind, former, latter):
    return kind(former[0], latter[0]) + (kind(former[0], latter[1]) + kind(former[1], latter[0]))


def gelu_parts(values):
    below = 0.5 * (1.0 + lax.erf(values * 0.7071067811865476))
    density = 0.3989422804014327 * jnp.exp(-0.5 * values * values)
    return values * below, below + values * density


def normed_rows(values):
    center = jnp.mean(values, axis=-1, keepdims=True)
    moved = values - center
    rate = lax.rsqrt(jnp.mean(moved * moved, axis=-1, keepdims=True) + EPS_NORM)
    return moved * rate, rate


def normed_back(grad, hat, rate, gain):
    scaled = grad * gain
    first = jnp.mean(scaled, axis=-1, keepdims=True)
    second = jnp.mean(scaled * hat, axis=-1, keepdims=True)
    return rate * (scaled - first - hat * second)


def live_column(occupied_ref):
    row = occupied_ref[...].astype(F32).reshape(1, occupied_ref.shape[0])
    return jnp.broadcast_to(row, (8, row.shape[1])).T[:, :1]


def column_sum(values):
    return jnp.sum(values, axis=0, keepdims=True)


def head_mask():
    dims = (HEADS, TILE_ROWS, WIDTH)
    lane_head = lax.broadcasted_iota(jnp.int32, dims, 2) // TILE_ROWS
    return (lane_head == lax.broadcasted_iota(jnp.int32, dims, 0)).astype(F32)


def per_head(rows, mask):
    count = rows.shape[0] // TILE_ROWS
    return (rows.reshape(count, 1, TILE_ROWS, WIDTH) * mask[None]).reshape(count * WIDTH, WIDTH)


def from_heads(table, mask):
    parts = []
    for at in range(0, table.shape[1], WIDTH):
        turned = table[:, at : at + WIDTH].T.reshape(HEADS, TILE_ROWS, WIDTH)
        parts.append(jnp.sum(turned * mask, axis=0))
    return parts


def high_and_low(values):
    high, low = halves(values.T)
    return jnp.concatenate([high, low], axis=0), high


def stacked_product(stack, high_alone, weights):
    both = nn(stack, weights[0])
    return both[:WIDTH] + (both[WIDTH:] + nn(high_alone, weights[1]))


def window_mix(query, key, value, live, mask, mask_low, keep_high, keep_low):
    query_high, query_low = halves(query)
    key_high, key_low = halves(key)
    key_stack = jnp.concatenate([key_high, key_low, key_high], axis=1)
    turned = high_and_low(value)
    mixed = []
    for first, last in CHUNKS:
        rows = slice(first * TILE_ROWS, last * TILE_ROWS)
        lanes = slice(first * WIDTH, last * WIDTH)
        high = per_head(query_high[rows], mask_low)
        low = per_head(query_low[rows], mask_low)
        scores = nt(key_stack, jnp.concatenate([high, high, low], axis=1))
        scores = jnp.where(live > 0, scores, NEG_FILL)
        weights = jnp.exp(scores - jnp.max(scores, axis=0, keepdims=True))
        weights = weights * (1.0 / column_sum(weights))
        weights = halves(weights)
        keep_high[:, lanes] = weights[0]
        keep_low[:, lanes] = weights[1]
        mixed += from_heads(stacked_product(*turned, weights), mask)
    return jnp.concatenate(mixed, axis=0)


def window_back(query, key, value, grad_mixed, live, mask, mask_low, high, low):
    query_high, query_low = (per_head(part, mask_low) for part in halves(query))
    grad_high, grad_low = (per_head(part, mask_low) for part in halves(grad_mixed))
    value_high, value_low = halves(value)
    value_stack = jnp.concatenate([value_high, value_low, value_high], axis=1)
    grad_weights = nt(value_stack, jnp.concatenate([grad_high, grad_high, grad_low], axis=1))
    weights = high.astype(F32) + low.astype(F32)
    grad_scores = weights * grad_weights
    grad_scores = live * (grad_scores - weights * column_sum(grad_scores))
    scores_high, scores_low = halves(grad_scores)

    def over_queries(upper, lower, high, low):
        both = nn(
            jnp.concatenate([upper, lower], axis=0), jnp.concatenate([high, low], axis=1)
        )
        return both[:CELLS, :WIDTH] + (both[:CELLS, WIDTH:] + both[CELLS:, :WIDTH])

    grad_query = stacked_product(*high_and_low(key), (scores_high, scores_low))
    return (
        0.25 * jnp.concatenate(from_heads(grad_query, mask), axis=0),
        over_queries(scores_high, scores_low, query_high, query_low),
        over_queries(high, low, grad_high, grad_low),
    )


def unpack(packed, qkv_ref, out_ref, up_high, up_low, down_high, down_low, bias, qkv_high, qkv_low, out_high, out_low):
    ffns = packed.shape[0]
    units = bias.shape[1] // ffns
    for one in range(2):
        for at in range(ffns):
            rows = slice(at * units, (at + 1) * units)
            high, low = halves(packed[at, one * units : (one + 1) * units])
            up_high[one, rows], up_low[one, rows] = high, low
            high, low = halves(packed[at, (2 + one) * units : (3 + one) * units])
            down_high[one, rows], down_low[one, rows] = high, low
        bias[one : one + 1] = jnp.concatenate(
            [packed[at, 4 * units + one : 4 * units + one + 1, :units] for at in range(ffns)], axis=1
        )
    qkv_high[...], qkv_low[...] = halves(qkv_ref[...])
    out_high[...], out_low[...] = halves(out_ref[...])


def layer_rows(one, values, live, weights, saved):
    up_high, up_low, down_high, down_low, bias, qkv_high, qkv_low, out_high, out_low, back_bias, gains, offsets = weights
    packed_keep, high_keep, low_keep, mixed_keep, hat_one, hidden_keep, slope, hat_two, rates = saved
    mask = head_mask()
    mask_low = mask.astype(BF16)
    qkv = product(nn, halves(values), (qkv_high[one], qkv_low[one]))
    query = 0.25 * qkv[:, :WIDTH]
    packed_keep[:, :WIDTH] = query
    packed_keep[:, WIDTH:] = qkv[:, WIDTH:]
    for at in range(STEP // CELLS):
        rows = slice(at * CELLS, (at + 1) * CELLS)
        mixed_keep[rows] = window_mix(
            query[rows],
            qkv[rows, WIDTH : 2 * WIDTH],
            qkv[rows, 2 * WIDTH :],
            live[rows],
            mask,
            mask_low,
            high_keep.at[at],
            low_keep.at[at],
        )
    mixed = mixed_keep[...]
    hat, rate = normed_rows(
        values + product(nn, halves(mixed), (out_high[one], out_low[one]))
    )
    hat_one[...] = hat
    first = hat * gains[2 * one : 2 * one + 1] + offsets[2 * one : 2 * one + 1]
    hidden, steep = gelu_parts(
        product(nt, halves(first), (up_high[one], up_low[one])) + bias[one : one + 1]
    )
    hidden_keep[...] = hidden
    slope[...] = steep
    summed = first + product(nn, halves(hidden), (down_high[one], down_low[one])) + back_bias[one : one + 1]
    hat, last_rate = normed_rows(summed)
    hat_two[...] = hat
    lanes = lax.broadcasted_iota(jnp.int32, hat.shape, 1)
    rates[...] = jnp.where(lanes < WIDTH // 2, rate, last_rate)
    return hat * gains[2 * one + 1 : 2 * one + 2] + offsets[2 * one + 1 : 2 * one + 2]


def ffn_rows_back(one, grad, saved, weights, sums):
    mixed_keep, hat_one, hidden_keep, slope, hat_two, rates = saved
    up_high, up_low, down_high, down_low, out_high, out_low, gains, offsets = weights
    up, down, out = (up_high[one], up_low[one]), (down_high[one], down_low[one]), (out_high[one], out_low[one])
    small, sum_out, sum_up, sum_down = sums
    hat = hat_two[...]
    grad_summed = normed_back(grad, hat, rates[:, WIDTH - 1 :], gains[2 * one + 1 : 2 * one + 2])
    small[3:4] += column_sum(grad * hat)
    small[4:5] += column_sum(grad)
    small[0:1] += column_sum(grad_summed)
    summed_halves = halves(grad_summed)
    grad_pre = product(nt, summed_halves, down) * slope[...]
    pre_halves = halves(grad_pre)
    hidden_halves = halves(hidden_keep[...])
    sum_down[...] += product(tn, hidden_halves, summed_halves)
    hat = hat_one[...]
    first = hat * gains[2 * one : 2 * one + 1] + offsets[2 * one : 2 * one + 1]
    sum_up[...] += product(tn, pre_halves, halves(first))
    bias_sum = column_sum(grad_pre)
    for at in range(bias_sum.shape[1] // WIDTH):
        small[5 + at : 6 + at] += bias_sum[:, at * WIDTH : (at + 1) * WIDTH]
    grad_first = grad_summed + product(nn, pre_halves, up)
    small[1:2] += column_sum(grad_first * hat)
    small[2:3] += column_sum(grad_first)
    grad_joined = normed_back(grad_first, hat, rates[:, 0:1], gains[2 * one : 2 * one + 1])
    joined_halves = halves(grad_joined)
    sum_out[...] += product(tn, halves(mixed_keep[...]), joined_halves)
    return grad_joined, product(nt, joined_halves, out)


def attention_rows_back(one, values, live, grad_joined, grad_mixed, saved, qkv_weights, sum_qkv):
    packed_keep, high_keep, low_keep = saved
    mask = head_mask()
    mask_low = mask.astype(BF16)
    parts = []
    for at in range(STEP // CELLS):
        rows = slice(at * CELLS, (at + 1) * CELLS)
        parts.append(
            window_back(
                packed_keep[rows, :WIDTH],
                packed_keep[rows, WIDTH : 2 * WIDTH],
                packed_keep[rows, 2 * WIDTH :],
                grad_mixed[rows],
                live[rows],
                mask,
                mask_low,
                high_keep[at],
                low_keep[at],
            )
        )
    grad_packed = halves(
        jnp.concatenate([jnp.concatenate(part, axis=1) for part in parts], axis=0)
    )
    sum_qkv[...] += product(tn, halves(values), grad_packed)
    return grad_joined + product(nt, grad_packed, (qkv_weights[0][one], qkv_weights[1][one]))


def share_rows(target, at, values, devices):
    count = values.shape[0]
    share = share_of(count, devices)
    for device in range(devices):
        begin = device * share
        if begin < count:
            held = min(share, count - begin)
            target[device, at : at + held] = values[begin : begin + held]
    return at + share


def share_units(target, at, sum_up, sum_down, ffns):
    units = sum_up.shape[0] // ffns
    for f in range(ffns):
        rows = slice(f * units, (f + 1) * units)
        joined = jnp.concatenate([sum_up[rows], sum_down[rows]], axis=0)
        at = share_rows(target, at, joined, target.shape[0])
    return at


def joined_rows(table, at, count):
    devices = table.shape[0]
    share = share_of(count, devices)
    if share % 8 == 0 and share * devices == count:
        return table[:, at : at + share].reshape(count, WIDTH)
    pieces = []
    for device in range(devices):
        begin = device * share
        if begin < count:
            pieces.append(table[device, at : at + min(share, count - begin)])
    return jnp.concatenate(pieces, axis=0)


def vfe_kernel(
    feats_ref, weight_ref, occupied_ref, up_ref, down_ref, bias_ref, lifted_ref, sent_ref, packed_ref
):
    devices = sent_ref.shape[0]
    units = up_ref.shape[1]
    feats = feats_ref[...]
    feats_halves = halves(feats)
    lifted = product(nn, feats_halves, halves(weight_ref[...]))
    lifted_ref[...] = lifted
    live = live_column(occupied_ref)
    count = jnp.sum(live, axis=0, keepdims=True)
    total = column_sum(live * lifted)
    moved = live * (lifted - total / jnp.maximum(count, 1.0))
    sent_ref[...] = jnp.zeros(sent_ref.shape, F32)
    stats = jnp.concatenate(
        [
            jnp.broadcast_to(count, (1, WIDTH)),
            total,
            column_sum(moved * moved),
            column_sum(live * feats),
        ],
        axis=0,
    )
    sent_ref[:, 0:4] = jnp.broadcast_to(stats[None], (devices, 4, WIDTH))
    share_rows(sent_ref, 4, product(tn, feats_halves, halves(moved)), devices)
    for one in range(2):
        packed_ref[one * units : (one + 1) * units] = up_ref[one]
        packed_ref[(2 + one) * units : (3 + one) * units] = down_ref[one]
    packed_ref[4 * units :] = jnp.zeros((8, WIDTH), F32)
    packed_ref[4 * units : 4 * units + 2, :units] = bias_ref[...]


def places_of(source_ref):
    row_count = source_ref.shape[0]
    places = source_ref[...].reshape(1, row_count) - lax.axis_index(AXES) * row_count
    return jnp.where(places < 0, places + row_count * lax.axis_size(AXES), places)


def one_hot(former, latter):
    return (former == latter).astype(F32).astype(BF16)


def vfe_stats(seen_ref, stats_ref, product_ref):
    counts, totals, squares, lives = (seen_ref[:, at] for at in range(4))
    count = column_sum(counts)
    center = column_sum(totals) / count
    moves = totals / jnp.maximum(counts, 1.0) - center
    rate = lax.rsqrt(column_sum(squares + counts * moves * moves) / count + EPS_NORM)
    stats_ref[...] = jnp.zeros(stats_ref.shape, F32)
    stats_ref[0:1] = count
    stats_ref[1:2] = center
    stats_ref[2:3] = rate
    stats_ref[3:4] = column_sum(lives)
    devices = seen_ref.shape[0]
    share = share_of(WIDTH, devices)
    mine = lax.axis_index(AXES) * share
    lanes = lax.broadcasted_iota(jnp.int32, lives.shape, 1)
    product_ref[...] = jnp.zeros(product_ref.shape, F32)
    for at in range(share):
        picked = jnp.sum(jnp.where(lanes == mine + at, lives, 0.0), axis=1, keepdims=True)
        product_ref[at : at + 1] = rate * column_sum(seen_ref[:, 4 + at] + picked * moves)


def step_of(refs, step):
    windows = STEP // CELLS
    return [
        ref.at[step * windows : (step + 1) * windows]
        if len(ref.shape) == 3
        else ref.at[step * STEP : (step + 1) * STEP]
        for ref in refs
    ]


def first_kernel(*refs, head):
    lifted_ref, occupied_ref, bn_gain, bn_shift, back_bias, gains, offsets = refs[:7]
    if head:
        seen_ref, packed, qkv_ref, out_ref, cotangent_ref = refs[7:12]
        weights = refs[12:21]
        stats, hat_product, edge = refs[21:24]
        arrays = refs[24:36]
        cotangent, semaphores = refs[36:]
        copies = Copies(semaphores)
        arrival = copies.start(cotangent_ref.at[:HALF], cotangent)
        unpack(packed, qkv_ref, out_ref, *weights)
        vfe_stats(seen_ref, stats, hat_product)
        rows = slice(0, STEP)
    else:
        stats = refs[7]
        weights = refs[8:17]
        arrays = refs[17:]
        rows = slice(STEP, 2 * STEP)
    result, vfe_slope, carried, *saved = arrays
    hat = (lifted_ref[rows] - stats[1:2]) * stats[2:3]
    values, steep = gelu_parts(hat * bn_gain[0:1] + bn_shift[0:1])
    vfe_slope[...] = steep
    carried[...] = values
    live = live_column(occupied_ref)[rows]
    rows = layer_rows(0, values, live, (*weights, back_bias, gains, offsets), saved)
    result[...] = rows
    if head:
        arrival.wait()
        edge[:, :WIDTH] = rows[:HALF]
        edge[:, WIDTH : 2 * WIDTH] = cotangent[...]
        edge[:, 2 * WIDTH :] = jnp.broadcast_to(live[:HALF], (HALF, WIDTH))


def second_kernel(first_ref, rest_ref, cotangent_ref, occupied_ref, edge, source_ref, *refs):
    weights = refs[:12]
    sent = refs[12]
    arrays = refs[13:-2]
    table, sums = refs[-2:]
    row_count = cotangent_ref.shape[0]
    for step, ref in enumerate((first_ref, rest_ref)):
        high, low = halves(ref[...])
        table[step * STEP : (step + 1) * STEP, :WIDTH] = high
        table[step * STEP : (step + 1) * STEP, WIDTH : 2 * WIDTH] = low
    high, low = halves(cotangent_ref[...])
    table[:row_count, 2 * WIDTH : 3 * WIDTH] = high
    table[:row_count, 3 * WIDTH : 4 * WIDTH] = low
    table[:row_count, 4 * WIDTH :] = jnp.broadcast_to(live_column(occupied_ref), (row_count, WIDTH)).astype(BF16)
    spare = table.shape[0] - row_count
    tail = jnp.concatenate([edge[...], jnp.zeros((spare - HALF, 3 * WIDTH), F32)], axis=0)
    high, low = halves(tail)
    table[row_count:, :WIDTH] = high[:, :WIDTH]
    table[row_count:, WIDTH : 2 * WIDTH] = low[:, :WIDTH]
    table[row_count:, 2 * WIDTH : 3 * WIDTH] = high[:, WIDTH : 2 * WIDTH]
    table[row_count:, 3 * WIDTH : 4 * WIDTH] = low[:, WIDTH : 2 * WIDTH]
    table[row_count:, 4 * WIDTH :] = high[:, 2 * WIDTH :]
    places = jnp.broadcast_to(places_of(source_ref).astype(F32), (8, row_count))
    column = places.T[:, :1].astype(jnp.int32)
    lanes = lax.broadcasted_iota(jnp.int32, (STEP, table.shape[0]), 1)
    for step in range(row_count // STEP):
        result, live_keep, cotangent_keep, carried, *saved = step_of(arrays, step)
        gathered = nn(one_hot(lanes, column[step * STEP : (step + 1) * STEP]), table[...])
        values = gathered[:, :WIDTH] + gathered[:, WIDTH : 2 * WIDTH]
        live = gathered[:, 4 * WIDTH :]
        grad = live * (gathered[:, 2 * WIDTH : 3 * WIDTH] + gathered[:, 3 * WIDTH : 4 * WIDTH])
        carried[...] = values
        cotangent_keep[...] = grad
        live_keep[...] = live[:, :1]
        rows = layer_rows(1, values, live[:, :1], weights, saved)
        result[...] = rows
        count = column_sum(live)
        if step == 0:
            sums[...] = jnp.zeros(sums.shape, F32)
            sums[5:6] = column_sum(live * rows) / jnp.maximum(count, 1.0)
        moved = rows - sums[5:6]
        sums[0:1] += count
        sums[1:2] += column_sum(live * moved)
        sums[2:3] += column_sum(live * moved * moved)
        sums[3:4] += column_sum(grad)
        sums[4:5] += column_sum(grad * moved)
    count = sums[0:1]
    move = sums[1:2] / jnp.maximum(count, 1.0)
    stats = jnp.concatenate(
        [
            count,
            sums[5:6] + move,
            sums[2:3] - count * move * move,
            sums[3:4],
            sums[4:5] - move * sums[3:4],
            jnp.zeros((3, WIDTH), F32),
        ],
        axis=0,
    )
    sent[...] = jnp.broadcast_to(stats[None], sent.shape)


def second_back_kernel(seen_ref, bn_gain, bn_shift, source_ref, *refs):
    weights = refs[:10]
    arrays = refs[10:23]
    edge, grad_head, grad_rest, out_rows, neck, sum_qkv, small, sum_out, sum_up, sum_down = refs[23:]
    row_count = out_rows.shape[0]
    counts, means, squares, grads, products = (seen_ref[:, row] for row in range(5))
    count = column_sum(counts)
    center = column_sum(counts * means) / count
    moves = means - center
    rate = lax.rsqrt(column_sum(squares + counts * moves * moves) / count + EPS_NORM)
    gain_grad = rate * column_sum(products + moves * grads)
    shift_grad = column_sum(grads)
    neck[...] = jnp.concatenate([gain_grad, shift_grad, jnp.zeros((6, WIDTH), F32)], axis=0)
    for held in (small, sum_qkv, sum_out, sum_up, sum_down):
        held[...] = jnp.zeros(held.shape, F32)
    places = places_of(source_ref)
    down = lax.broadcasted_iota(jnp.int32, (-(-(row_count + HALF) // 8) * 8, STEP), 0)
    placed = None
    for step in range(row_count // STEP):
        result, live_keep, cotangent_keep, carried, packed_keep, high_keep, low_keep, *keeps = step_of(arrays, step)
        live = live_keep[...]
        hat = (result[...] - center) * rate
        neck_rows = live * (hat * bn_gain[1:2] + bn_shift[1:2])
        grad = rate * bn_gain[1:2] * (
            cotangent_keep[...] - live * (hat * gain_grad + shift_grad) / count
        )
        grad_joined, grad_mixed = ffn_rows_back(
            1, grad, keeps, weights[:4] + weights[6:10], (small, sum_out, sum_up, sum_down)
        )
        grad_values = attention_rows_back(
            1,
            carried[...],
            live,
            grad_joined,
            grad_mixed,
            (packed_keep, high_keep, low_keep),
            weights[4:6],
            sum_qkv,
        )
        pieces = jnp.concatenate(halves(grad_values) + halves(neck_rows), axis=1)
        moved = nn(one_hot(down, places[:, step * STEP : (step + 1) * STEP]), pieces)
        moved = jnp.concatenate(
            [
                moved[:, :WIDTH] + moved[:, WIDTH : 2 * WIDTH],
                moved[:, 2 * WIDTH : 3 * WIDTH] + moved[:, 3 * WIDTH :],
            ],
            axis=1,
        )
        placed = moved if placed is None else placed + moved
    grad_head[...] = placed[:STEP, :WIDTH]
    grad_rest[...] = placed[STEP:row_count, :WIDTH]
    out_rows[...] = placed[:row_count, WIDTH:]
    edge[...] = placed[row_count : row_count + HALF]


def first_ffn_back_kernel(grad_rest, *refs):
    weights, keeps = refs[:8], refs[8:14]
    joined, mixed = refs[14:16]
    sums = refs[16:]
    for held in sums:
        held[...] = jnp.zeros(held.shape, F32)
    joined[...], mixed[...] = ffn_rows_back(0, grad_rest[...], keeps, weights, sums)


def share_layer(shared, row, sums, ffns):
    sum_qkv, sum_out, sum_up, sum_down = sums
    devices = shared.shape[0]
    row = share_units(shared, row, sum_up, sum_down, ffns)
    for block in range(3):
        row = share_rows(shared, row, sum_qkv[:, block * WIDTH : (block + 1) * WIDTH], devices)
    return share_rows(shared, row, sum_out, devices)


def first_back_kernel(*refs, ffns):
    edge, stats, gains, offsets, occupied_ref, out_rows, grad_head, lifted_ref, feats_ref = refs[:9]
    weights, head_ffn = refs[9:17], refs[17:23]
    joined_ref, mixed_ref = refs[23:25]
    held_sums = refs[25:29]
    small_second, *second_sums = refs[29:34]
    head_rows, rest_rows = refs[34:39], refs[39:44]
    pillars, grad_affine, shared = refs[44:47]
    grad, affine, small_ffn, sum_out, sum_up, sum_down, sum_qkv, sum_feats, small, semaphores = refs[47:]
    copies = Copies(semaphores)
    copies.start(edge.at[:, WIDTH:], pillars.at[:HALF])
    copies.start(out_rows.at[HALF:], pillars.at[HALF:])
    live = live_column(occupied_ref)
    sums = (small_ffn, sum_out, sum_up, sum_down)
    for held in (small, sum_qkv, sum_feats):
        held[...] = jnp.zeros(held.shape, F32)
    for held, before in zip(sums, held_sums):
        held[...] = before[...]
    grad[...] = grad_head[...]
    grad[:HALF] = edge[:, :WIDTH]
    ffn_weights = (*weights[:4], *weights[6:8], gains, offsets)
    joined, mixed = ffn_rows_back(0, grad[...], head_ffn, ffn_weights, sums)
    for step, arrays in enumerate((head_rows, rest_rows)):
        rows = slice(step * STEP, (step + 1) * STEP)
        vfe_slope, carried, packed_keep, high_keep, low_keep = arrays
        if step:
            joined, mixed = joined_ref[...], mixed_ref[...]
        rows_grad = attention_rows_back(
            0,
            carried[...],
            live[rows],
            joined,
            mixed,
            (packed_keep, high_keep, low_keep),
            weights[4:6],
            sum_qkv,
        )
        rows_grad = rows_grad * vfe_slope[...]
        affine[rows] = rows_grad
        copies.start(affine.at[rows], grad_affine.at[rows])
        small[0:1] += column_sum(rows_grad * (lifted_ref[rows] - stats[1:2]) * stats[2:3])
        small[1:2] += column_sum(rows_grad)
        sum_feats[...] += product(tn, halves(feats_ref[rows]), halves(rows_grad))
    devices = shared.shape[0]
    shared[...] = jnp.zeros(shared.shape, F32)
    row = share_layer(shared, 0, second_sums, ffns)
    row = share_layer(shared, row, (sum_qkv, sum_out, sum_up, sum_down), ffns)
    row = share_rows(shared, row, small_second[...], devices)
    row = share_rows(shared, row, small_ffn[...], devices)
    row = share_rows(shared, row, sum_feats, devices)
    shared[:, row : row + 2] = jnp.broadcast_to(small[0:2][None], (devices, 2, WIDTH))
    for copy in copies.started:
        copy.wait()


def relay_kernel(arrived, hat_product, stats, bn_gain, returned, vfe_grads, *, ffns, counts):
    unit_rows, layer_rows, small_rows, part = counts
    devices = returned.shape[0]
    total = jnp.sum(arrived[...], axis=0)
    begin = ffns * unit_rows
    later = begin + layer_rows
    end = later + begin + layer_rows + small_rows
    gain, shift = total[end + part : end + part + 1], total[end + part + 1 : end + part + 2]
    lanes = lax.broadcasted_iota(jnp.int32, (part, WIDTH), 1)
    mine = lax.axis_index(AXES) * part + lax.broadcasted_iota(jnp.int32, (part, WIDTH), 0)
    live_sum = jnp.sum(jnp.where(lanes == mine, stats[3:4], 0.0), axis=1, keepdims=True)
    grad_w_vfe = stats[2:3] * bn_gain[0:1] * (
        total[end : end + part] - (hat_product[:part] * gain + live_sum * shift) / stats[0:1]
    )
    rows = jnp.concatenate([total[begin:later], total[later + begin : end], grad_w_vfe], axis=0)
    room = returned.shape[1] - 2 * unit_rows
    if rows.shape[0] < room:
        rows = jnp.concatenate([rows, jnp.zeros((room - rows.shape[0], WIDTH), F32)], axis=0)
    returned[:, 2 * unit_rows :] = jnp.broadcast_to(rows[None], (devices,) + rows.shape)
    for device in range(devices):
        block = device % ffns
        for at, first in enumerate((0, later)):
            first += block * unit_rows
            returned[device, at * unit_rows : (at + 1) * unit_rows] = total[first : first + unit_rows]
    vfe_grads[...] = jnp.concatenate([gain, shift, jnp.zeros((6, WIDTH), F32)], axis=0)


def feats_back_kernel(grad_affine, lifted_ref, occupied_ref, stats, vfe_grads, bn_gain, weight_ref, grad_feats):
    sums = vfe_grads[...]
    scale = stats[2:3] * bn_gain[0:1]
    hat = (lifted_ref[...] - stats[1:2]) * stats[2:3]
    grad = scale * (
        grad_affine[...]
        - live_column(occupied_ref) * (hat * sums[0:1] + sums[1:2]) / stats[0:1]
    )
    grad_feats[...] = product(nt, halves(grad), halves(weight_ref[...]))


def last_kernel(
    returned,
    vfe_grads,
    neck,
    grad_w_vfe,
    grad_bn_gain,
    grad_bn_shift,
    grad_w_qkv,
    grad_w_out,
    grad_w_in,
    grad_b_in,
    grad_w_back,
    grad_b_back,
    grad_ln_gain,
    grad_ln_shift,
    *,
    ffns,
):
    devices = returned.shape[0]
    units = grad_w_in.shape[1]
    part = share_of(WIDTH, devices)
    unit_rows = share_of(2 * units, devices)
    at = 0

    def take(count):
        nonlocal at
        rows = joined_rows(returned, at, count)
        at += share_of(count, devices)
        return rows

    blocks = [take(2 * units) for layer in range(2)]
    mine = lax.rem(lax.axis_index(AXES), ffns)
    for layer in (1, 0):
        grad_w_in[layer] = blocks[1 - layer][:units]
        grad_w_back[layer] = blocks[1 - layer][units:]
        for block in range(3):
            grad_w_qkv[layer, :, block * WIDTH : (block + 1) * WIDTH] = take(WIDTH)
        grad_w_out[layer] = take(WIDTH)
    for layer in (1, 0):
        small = take(8)
        grad_b_back[layer : layer + 1] = small[0:1]
        grad_ln_gain[2 * layer : 2 * layer + 1] = small[1:2]
        grad_ln_shift[2 * layer : 2 * layer + 1] = small[2:3]
        grad_ln_gain[2 * layer + 1 : 2 * layer + 2] = small[3:4]
        grad_ln_shift[2 * layer + 1 : 2 * layer + 2] = small[4:5]
        held = jnp.zeros((1, units), F32)
        for f in range(ffns):
            row, lane = divmod(f * units, WIDTH)
            held = jnp.where(mine == f, small[5 + row : 6 + row, lane : lane + units], held)
        grad_b_in[layer : layer + 1] = held
    grad_w_vfe[...] = take(WIDTH)
    grad_bn_gain[0:1] = vfe_grads[0:1]
    grad_bn_gain[1:2] = neck[0:1]
    grad_bn_shift[0:1] = vfe_grads[1:2]
    grad_bn_shift[1:2] = neck[1:2]


def spread_rows(pieces, axes):
    return lax.all_to_all(pieces, axes, 0, 0)


def passed_along(rows, by):
    peers = lax.axis_size(AXES)
    return lax.ppermute(rows, AXES, [(i, (i + by) % peers) for i in range(peers)])


def on_device(
    pillar_feats,
    occupied,
    shifted_source_rows,
    w_vfe,
    bn_gain,
    bn_shift,
    query_key_value_weight,
    attention_output_weight,
    up_weight_matrix,
    up_bias_rows,
    down_weight_matrix,
    down_bias_rows,
    layernorm_gains,
    layernorm_offsets,
    cotangent,
):
    row_count = pillar_feats.shape[0]
    spread = row_count + -(-HALF // 16) * 16
    ffns = lax.axis_size("ffn")
    devices = lax.axis_size(AXES)
    units = up_weight_matrix.shape[2]
    hidden = units * ffns
    windows = row_count // CELLS
    part = share_of(WIDTH, devices)
    piece = share_of(2 * units, devices)
    rest = 4 * part + 2 * share_of(8, devices)
    stats_rows = -(-(4 + part) // 8) * 8
    shared_rows = -(-(2 * ffns * piece + 4 * part + rest + part + 2) // 8) * 8
    returned_rows = -(-(2 * piece + 4 * part + rest + part) // 8) * 8
    rows_shape = shape(row_count, WIDTH)
    step_rows = (STEP, WIDTH)
    step_hidden = (STEP, hidden)
    step_weights = (STEP // CELLS, CELLS, HEADS * CELLS)

    def keeps(make, rows):
        scale = rows // STEP
        weights = make(scale * step_weights[0], *step_weights[1:], dtype=BF16)
        plain, wide = make(rows, WIDTH), make(rows, hidden)
        return [plain, make(rows, 3 * WIDTH), weights, weights, plain, plain, wide, wide, plain, plain]

    lifted, sent, packed = run(
        vfe_kernel,
        "vfe",
        (rows_shape, shape(devices, stats_rows, WIDTH), shape(4 * units + 8, WIDTH)),
        (
            pillar_feats,
            w_vfe,
            occupied,
            up_weight_matrix.transpose(0, 2, 1),
            down_weight_matrix,
            up_bias_rows,
        ),
    )
    seen = spread_rows(sent, AXES)
    packed = lax.all_gather(packed, "ffn", axis=0, tiled=False)
    weight_dims = (
        [(2, hidden, WIDTH, BF16)] * 4
        + [(2, hidden, F32)]
        + [(2, WIDTH, 3 * WIDTH, BF16)] * 2
        + [(2, WIDTH, WIDTH, BF16)] * 2
    )
    norms = pinned((down_bias_rows, layernorm_gains, layernorm_offsets))
    bn_pair = pinned((bn_gain, bn_shift))
    first_arrays = [kept(*step_rows)] * 2 + keeps(kept, STEP)
    outs = run(
        functools.partial(first_kernel, head=True),
        "first",
        [kept(*dims[:-1], dtype=dims[-1]) for dims in weight_dims]
        + [kept(8, WIDTH), kept(8, WIDTH), kept(HALF, 3 * WIDTH)]
        + first_arrays,
        (
            lifted,
            Pinned(occupied),
            *bn_pair,
            *norms,
            Pinned(seen),
            packed,
            query_key_value_weight,
            attention_output_weight,
            Far(cotangent),
        ),
        scratch=[pltpu.VMEM((HALF, WIDTH), F32)],
        copies=1,
        flops=1e9,
    )
    weights, (stats, hat_product, edge) = outs[:9], outs[9:12]
    first_head, *head_keep = outs[12:]
    layer_weights = pinned(weights) + norms
    back_weights = pinned(weights[:4] + weights[5:]) + norms[1:]
    edge = passed_along(edge, -1)
    first_rest, *rest_keep = run(
        functools.partial(first_kernel, head=False),
        "first_rest",
        first_arrays,
        (Pinned(lifted), Pinned(occupied), *bn_pair, *norms, Pinned(stats), *pinned(weights)),
        flops=1e9,
    )
    sent, *second_keep = run(
        second_kernel,
        "second",
        [kept(devices, 8, WIDTH), kept(row_count, WIDTH), kept(row_count, 1), kept(row_count, WIDTH)]
        + [kept(row_count, WIDTH)]
        + keeps(kept, row_count)[1:],
        (
            Pinned(first_head),
            Pinned(first_rest),
            Pinned(cotangent),
            Pinned(occupied),
            Pinned(edge),
            Pinned(shifted_source_rows),
            *layer_weights,
        ),
        scratch=[pltpu.VMEM((spread, 5 * WIDTH), BF16), pltpu.VMEM((8, WIDTH), F32)],
        flops=2e9,
    )
    seen = spread_rows(sent, AXES)
    sum_shapes = [
        pltpu.VMEM((8, WIDTH), F32),
        pltpu.VMEM((WIDTH, WIDTH), F32),
        pltpu.VMEM((hidden, WIDTH), F32),
        pltpu.VMEM((hidden, WIDTH), F32),
    ]
    sum_qkv = pltpu.VMEM((WIDTH, 3 * WIDTH), F32)
    edge, grad_head, grad_rest, out_rows, neck, *second_sums = run(
        second_back_kernel,
        "second_back",
        [
            kept(HALF, 2 * WIDTH),
            kept(*step_rows),
            kept(*step_rows),
            kept(row_count, WIDTH),
            kept(8, WIDTH),
            sum_qkv,
        ]
        + sum_shapes,
        (Pinned(seen), *bn_pair, Pinned(shifted_source_rows), *back_weights, *pinned(second_keep)),
        flops=4e9,
    )
    second_sums = [second_sums[1], second_sums[0], *second_sums[2:]]
    edge = passed_along(edge, 1)
    grad_joined, grad_mixed, *sums = run(
        first_ffn_back_kernel,
        "first_ffn_back",
        [kept(*step_rows), kept(*step_rows)] + sum_shapes,
        (Pinned(grad_rest), *(back_weights[:4] + back_weights[6:]), *pinned(rest_keep[5:])),
        flops=1e9,
    )
    edge, grad_joined = lax.optimization_barrier((edge, grad_joined))
    pillars_out, grad_affine, shared = run(
        functools.partial(first_back_kernel, ffns=ffns),
        "first_back",
        [Far(rows_shape), Far(rows_shape), kept(devices, shared_rows, WIDTH)],
        pinned(
            (
                edge,
                stats,
                layernorm_gains,
                layernorm_offsets,
                occupied,
                out_rows,
                grad_head,
                lifted,
                pillar_feats,
                *weights[:4],
                *weights[5:],
                *head_keep[5:],
                grad_joined,
                grad_mixed,
                *sums,
                *second_sums,
                *head_keep[:5],
                *rest_keep[:5],
            )
        ),
        scratch=[pltpu.VMEM((STEP, WIDTH), F32), pltpu.VMEM((row_count, WIDTH), F32)]
        + sum_shapes
        + [sum_qkv, pltpu.VMEM((WIDTH, WIDTH), F32), pltpu.VMEM((8, WIDTH), F32)],
        copies=4,
        flops=4e9,
    )
    arrived = spread_rows(shared, AXES)
    returned, vfe_grads = run(
        functools.partial(relay_kernel, ffns=ffns, counts=(piece, 4 * part, rest - 4 * part, part)),
        "relay",
        (shape(devices, returned_rows, WIDTH), shape(8, WIDTH)),
        pinned((arrived, hat_product, stats, bn_gain)),
    )
    returned = spread_rows(returned, AXES)
    (grad_feats,) = run(
        feats_back_kernel,
        "feats_back",
        (rows_shape,),
        (grad_affine, lifted, occupied, stats, vfe_grads, bn_gain, w_vfe),
    )
    grads = list(run(
        functools.partial(last_kernel, ffns=ffns),
        "last",
        (
            shape(WIDTH, WIDTH),
            shape(2, WIDTH),
            shape(2, WIDTH),
            shape(2, WIDTH, 3 * WIDTH),
            shape(2, WIDTH, WIDTH),
            shape(2, units, WIDTH),
            shape(2, units),
            shape(2, units, WIDTH),
            shape(2, WIDTH),
            shape(4, WIDTH),
            shape(4, WIDTH),
        ),
        (Pinned(returned), vfe_grads, neck),
    ))
    grads[5] = grads[5].transpose(0, 2, 1)
    return (pillars_out, grad_feats, *grads)


def solution(mesh):
    return jax.shard_map(
        on_device,
        mesh=mesh,
        in_specs=(
            P(("win", "ffn"), None),
            P(("win", "ffn")),
            P(("win", "ffn")),
            P(),
            P(),
            P(),
            P(),
            P(),
            P(None, None, "ffn"),
            P(None, "ffn"),
            P(None, "ffn", None),
            P(),
            P(),
            P(),
            P(("win", "ffn"), None),
        ),
        out_specs=(
            P(("win", "ffn"), None),
            P(("win", "ffn"), None),
            P(),
            P(),
            P(),
            P(),
            P(),
            P(None, None, "ffn"),
            P(None, "ffn"),
            P(None, "ffn", None),
            P(),
            P(),
            P(),
        ),
        check_vma=False,
    )
```

```python
import functools

import jax
import jax.numpy as jnp
from jax import lax
from jax.experimental import pallas as pl
from jax.experimental.pallas import tpu as pltpu
from jax.sharding import PartitionSpec as P

HEADS = 8
CELLS = 144
HALF = CELLS // 2
WIDTH = 128
EPS_NORM = 1e-05
NEG_FILL = -1000000000.0
AXES = ("win", "ffn")
STEP = 3 * CELLS
HEAD = 2 * CELLS
TILE_ROWS = WIDTH // HEADS
TILES = CELLS // TILE_ROWS
CHUNKS = ((0, 2), (2, 4), (4, 6), (6, 8), (8, 9))
F32 = jnp.float32
BF16 = jnp.bfloat16
VMEM_LIMIT = 28 * 1024 * 1024


def shape(*dims, dtype=F32):
    return pltpu.HBM(dims, dtype)


def kept(*dims, dtype=F32):
    return pltpu.VMEM(dims, dtype)


class Pinned:
    def __init__(self, value):
        self.value = value


class Far:
    def __init__(self, value):
        self.value = value


def run(kernel, name, outs, args, scratch=(), copies=0, flops=1e8):
    near, far = pl.BlockSpec(memory_space=pltpu.VMEM), pl.BlockSpec(memory_space=pltpu.HBM)
    values = []
    for arg in args:
        space = pltpu.VMEM if isinstance(arg, Pinned) else pltpu.HBM
        value = arg.value if isinstance(arg, (Pinned, Far)) else arg
        values.append(pltpu.with_memory_space_constraint(value, space))
    scratch = list(scratch)
    if copies:
        scratch.append(pltpu.SemaphoreType.DMA((copies,)))
    return pl.pallas_call(
        kernel,
        out_shape=[out.value if isinstance(out, Far) else out for out in outs],
        in_specs=[far if isinstance(arg, Far) else near for arg in args],
        out_specs=[far if isinstance(out, Far) else near for out in outs],
        scratch_shapes=scratch,
        compiler_params=pltpu.CompilerParams(vmem_limit_bytes=VMEM_LIMIT),
        cost_estimate=pl.CostEstimate(flops=int(flops), bytes_accessed=1000000, transcendentals=0),
        name=name,
    )(*values)


def pinned(values):
    return [Pinned(value) for value in values]


class Copies:
    def __init__(self, semaphores):
        self.semaphores = semaphores
        self.started = []

    def start(self, source, target):
        copy = pltpu.make_async_copy(source, target, self.semaphores.at[len(self.started)])
        copy.start()
        self.started.append(copy)
        return copy


def scratch_like(arrays):
    return [pltpu.VMEM(array.shape, array.dtype) for array in arrays]


def ffn_index(ffns):
    return lax.rem(lax.axis_index(AXES), ffns)


def share_of(rows, devices):
    return -(-rows // devices)


def halves(values):
    high = values.astype(BF16)
    return high, (values - high.astype(F32)).astype(BF16)


def nn(former, latter):
    return lax.dot_general(former, latter, (((1,), (0,)), ((), ())), preferred_element_type=F32)


def nt(former, latter):
    return lax.dot_general(former, latter, (((1,), (1,)), ((), ())), preferred_element_type=F32)


def tn(former, latter):
    return lax.dot_general(former, latter, (((0,), (0,)), ((), ())), preferred_element_type=F32)


def product(kind, former, latter):
    return kind(former[0], latter[0]) + (kind(former[0], latter[1]) + kind(former[1], latter[0]))


def gelu_parts(values):
    below = 0.5 * (1.0 + lax.erf(values * 0.7071067811865476))
    density = 0.3989422804014327 * jnp.exp(-0.5 * values * values)
    return values * below, below + values * density


def normed_rows(values):
    center = jnp.mean(values, axis=-1, keepdims=True)
    moved = values - center
    rate = lax.rsqrt(jnp.mean(moved * moved, axis=-1, keepdims=True) + EPS_NORM)
    return moved * rate, rate


def normed_back(grad, hat, rate, gain):
    scaled = grad * gain
    first = jnp.mean(scaled, axis=-1, keepdims=True)
    second = jnp.mean(scaled * hat, axis=-1, keepdims=True)
    return rate * (scaled - first - hat * second)


def live_column(occupied_ref):
    row = occupied_ref[...].astype(F32).reshape(1, occupied_ref.shape[0])
    return jnp.broadcast_to(row, (8, row.shape[1])).T[:, :1]


def column_sum(values):
    return jnp.sum(values, axis=0, keepdims=True)


def head_mask():
    dims = (HEADS, TILE_ROWS, WIDTH)
    lane_head = lax.broadcasted_iota(jnp.int32, dims, 2) // TILE_ROWS
    return (lane_head == lax.broadcasted_iota(jnp.int32, dims, 0)).astype(F32)


def per_head(rows, mask):
    count = rows.shape[0] // TILE_ROWS
    return (rows.reshape(count, 1, TILE_ROWS, WIDTH) * mask[None]).reshape(count * WIDTH, WIDTH)


def from_heads(table, mask):
    parts = []
    for at in range(0, table.shape[1], WIDTH):
        turned = table[:, at : at + WIDTH].T.reshape(HEADS, TILE_ROWS, WIDTH)
        parts.append(jnp.sum(turned * mask, axis=0))
    return parts


def high_and_low(values):
    high, low = halves(values.T)
    return jnp.concatenate([high, low], axis=0), high


def stacked_product(stack, high_alone, weights):
    both = nn(stack, weights[0])
    return both[:WIDTH] + (both[WIDTH:] + nn(high_alone, weights[1]))


def window_mix(query, key, value, live, mask, mask_low, keep_high, keep_low):
    query_high, query_low = halves(query)
    key_high, key_low = halves(key)
    key_stack = jnp.concatenate([key_high, key_low, key_high], axis=1)
    turned = high_and_low(value)
    mixed = []
    for first, last in CHUNKS:
        rows = slice(first * TILE_ROWS, last * TILE_ROWS)
        lanes = slice(first * WIDTH, last * WIDTH)
        high = per_head(query_high[rows], mask_low)
        low = per_head(query_low[rows], mask_low)
        scores = nt(key_stack, jnp.concatenate([high, high, low], axis=1))
        scores = jnp.where(live > 0, scores, NEG_FILL)
        weights = jnp.exp(scores - jnp.max(scores, axis=0, keepdims=True))
        weights = weights * (1.0 / column_sum(weights))
        weights = halves(weights)
        keep_high[:, lanes] = weights[0]
        keep_low[:, lanes] = weights[1]
        mixed += from_heads(stacked_product(*turned, weights), mask)
    return jnp.concatenate(mixed, axis=0)


def window_back(query, key, value, grad_mixed, live, mask, mask_low, high, low):
    query_high, query_low = (per_head(part, mask_low) for part in halves(query))
    grad_high, grad_low = (per_head(part, mask_low) for part in halves(grad_mixed))
    value_high, value_low = halves(value)
    value_stack = jnp.concatenate([value_high, value_low, value_high], axis=1)
    grad_weights = nt(value_stack, jnp.concatenate([grad_high, grad_high, grad_low], axis=1))
    weights = high.astype(F32) + low.astype(F32)
    grad_scores = weights * grad_weights
    grad_scores = live * (grad_scores - weights * column_sum(grad_scores))
    scores_high, scores_low = halves(grad_scores)

    def over_queries(upper, lower, high, low):
        both = nn(
            jnp.concatenate([upper, lower], axis=0), jnp.concatenate([high, low], axis=1)
        )
        return both[:CELLS, :WIDTH] + (both[:CELLS, WIDTH:] + both[CELLS:, :WIDTH])

    grad_query = stacked_product(*high_and_low(key), (scores_high, scores_low))
    return (
        0.25 * jnp.concatenate(from_heads(grad_query, mask), axis=0),
        over_queries(scores_high, scores_low, query_high, query_low),
        over_queries(high, low, grad_high, grad_low),
    )


def unpack(packed, qkv_ref, out_ref, up_high, up_low, down_high, down_low, bias, qkv_high, qkv_low, out_high, out_low):
    ffns = packed.shape[0]
    units = bias.shape[1] // ffns
    for one in range(2):
        for at in range(ffns):
            rows = slice(at * units, (at + 1) * units)
            high, low = halves(packed[at, one * units : (one + 1) * units])
            up_high[one, rows], up_low[one, rows] = high, low
            high, low = halves(packed[at, (2 + one) * units : (3 + one) * units])
            down_high[one, rows], down_low[one, rows] = high, low
        bias[one : one + 1] = jnp.concatenate(
            [packed[at, 4 * units + one : 4 * units + one + 1, :units] for at in range(ffns)], axis=1
        )
    qkv_high[...], qkv_low[...] = halves(qkv_ref[...])
    out_high[...], out_low[...] = halves(out_ref[...])


def layer_rows(one, values, live, weights, saved):
    up_high, up_low, down_high, down_low, bias, qkv_high, qkv_low, out_high, out_low, back_bias, gains, offsets = weights
    packed_keep, high_keep, low_keep, mixed_keep, hat_one, hidden_keep, slope, hat_two, rates = saved
    mask = head_mask()
    mask_low = mask.astype(BF16)
    qkv = product(nn, halves(values), (qkv_high[one], qkv_low[one]))
    query = 0.25 * qkv[:, :WIDTH]
    packed_keep[:, :WIDTH] = query
    packed_keep[:, WIDTH:] = qkv[:, WIDTH:]
    for at in range(values.shape[0] // CELLS):
        rows = slice(at * CELLS, (at + 1) * CELLS)
        mixed_keep[rows] = window_mix(
            query[rows],
            qkv[rows, WIDTH : 2 * WIDTH],
            qkv[rows, 2 * WIDTH :],
            live[rows],
            mask,
            mask_low,
            high_keep.at[at],
            low_keep.at[at],
        )
    mixed = mixed_keep[...]
    hat, rate = normed_rows(
        values + product(nn, halves(mixed), (out_high[one], out_low[one]))
    )
    hat_one[...] = hat
    first = hat * gains[2 * one : 2 * one + 1] + offsets[2 * one : 2 * one + 1]
    hidden, steep = gelu_parts(
        product(nt, halves(first), (up_high[one], up_low[one])) + bias[one : one + 1]
    )
    hidden_keep[...] = hidden
    slope[...] = steep
    summed = first + product(nn, halves(hidden), (down_high[one], down_low[one])) + back_bias[one : one + 1]
    hat, last_rate = normed_rows(summed)
    hat_two[...] = hat
    lanes = lax.broadcasted_iota(jnp.int32, hat.shape, 1)
    rates[...] = jnp.where(lanes < WIDTH // 2, rate, last_rate)
    return hat * gains[2 * one + 1 : 2 * one + 2] + offsets[2 * one + 1 : 2 * one + 2]


def ffn_rows_back(one, grad, saved, weights, sums):
    mixed_keep, hat_one, hidden_keep, slope, hat_two, rates = saved
    up_high, up_low, down_high, down_low, out_high, out_low, gains, offsets = weights
    up, down, out = (up_high[one], up_low[one]), (down_high[one], down_low[one]), (out_high[one], out_low[one])
    small, sum_out, sum_up, sum_down = sums
    hat = hat_two[...]
    grad_summed = normed_back(grad, hat, rates[:, WIDTH - 1 :], gains[2 * one + 1 : 2 * one + 2])
    small[3:4] += column_sum(grad * hat)
    small[4:5] += column_sum(grad)
    small[0:1] += column_sum(grad_summed)
    summed_halves = halves(grad_summed)
    grad_pre = product(nt, summed_halves, down) * slope[...]
    pre_halves = halves(grad_pre)
    hidden_halves = halves(hidden_keep[...])
    sum_down[...] += product(tn, hidden_halves, summed_halves)
    hat = hat_one[...]
    first = hat * gains[2 * one : 2 * one + 1] + offsets[2 * one : 2 * one + 1]
    sum_up[...] += product(tn, pre_halves, halves(first))
    bias_sum = column_sum(grad_pre)
    for at in range(bias_sum.shape[1] // WIDTH):
        small[5 + at : 6 + at] += bias_sum[:, at * WIDTH : (at + 1) * WIDTH]
    grad_first = grad_summed + product(nn, pre_halves, up)
    small[1:2] += column_sum(grad_first * hat)
    small[2:3] += column_sum(grad_first)
    grad_joined = normed_back(grad_first, hat, rates[:, 0:1], gains[2 * one : 2 * one + 1])
    joined_halves = halves(grad_joined)
    sum_out[...] += product(tn, halves(mixed_keep[...]), joined_halves)
    return grad_joined, product(nt, joined_halves, out)


def attention_rows_back(one, values, live, grad_joined, grad_mixed, saved, qkv_weights, sum_qkv):
    packed_keep, high_keep, low_keep = saved
    mask = head_mask()
    mask_low = mask.astype(BF16)
    parts = []
    for at in range(values.shape[0] // CELLS):
        rows = slice(at * CELLS, (at + 1) * CELLS)
        parts.append(
            window_back(
                packed_keep[rows, :WIDTH],
                packed_keep[rows, WIDTH : 2 * WIDTH],
                packed_keep[rows, 2 * WIDTH :],
                grad_mixed[rows],
                live[rows],
                mask,
                mask_low,
                high_keep[at],
                low_keep[at],
            )
        )
    grad_packed = halves(
        jnp.concatenate([jnp.concatenate(part, axis=1) for part in parts], axis=0)
    )
    sum_qkv[...] += product(tn, halves(values), grad_packed)
    return grad_joined + product(nt, grad_packed, (qkv_weights[0][one], qkv_weights[1][one]))


def share_rows(target, at, values, devices):
    count = values.shape[0]
    share = share_of(count, devices)
    for device in range(devices):
        begin = device * share
        if begin < count:
            held = min(share, count - begin)
            target[device, at : at + held] = values[begin : begin + held]
    return at + share


def share_units(target, at, sum_up, sum_down, ffns):
    units = sum_up.shape[0] // ffns
    for f in range(ffns):
        rows = slice(f * units, (f + 1) * units)
        joined = jnp.concatenate([sum_up[rows], sum_down[rows]], axis=0)
        at = share_rows(target, at, joined, target.shape[0])
    return at


def joined_rows(table, at, count):
    devices = table.shape[0]
    share = share_of(count, devices)
    if share % 8 == 0 and share * devices == count:
        return table[:, at : at + share].reshape(count, WIDTH)
    pieces = []
    for device in range(devices):
        begin = device * share
        if begin < count:
            pieces.append(table[device, at : at + min(share, count - begin)])
    return jnp.concatenate(pieces, axis=0)


def vfe_kernel(
    feats_ref, weight_ref, occupied_ref, up_ref, down_ref, bias_ref, lifted_ref, sent_ref, packed_ref
):
    devices = sent_ref.shape[0]
    units = up_ref.shape[1]
    feats = feats_ref[...]
    feats_halves = halves(feats)
    lifted = product(nn, feats_halves, halves(weight_ref[...]))
    lifted_ref[...] = lifted
    live = live_column(occupied_ref)
    count = jnp.sum(live, axis=0, keepdims=True)
    total = column_sum(live * lifted)
    moved = live * (lifted - total / jnp.maximum(count, 1.0))
    sent_ref[...] = jnp.zeros(sent_ref.shape, F32)
    stats = jnp.concatenate(
        [
            jnp.broadcast_to(count, (1, WIDTH)),
            total,
            column_sum(moved * moved),
            column_sum(live * feats),
        ],
        axis=0,
    )
    sent_ref[:, 0:4] = jnp.broadcast_to(stats[None], (devices, 4, WIDTH))
    share_rows(sent_ref, 4, product(tn, feats_halves, halves(moved)), devices)
    for one in range(2):
        packed_ref[one * units : (one + 1) * units] = up_ref[one]
        packed_ref[(2 + one) * units : (3 + one) * units] = down_ref[one]
    packed_ref[4 * units :] = jnp.zeros((8, WIDTH), F32)
    packed_ref[4 * units : 4 * units + 2, :units] = bias_ref[...]


def places_of(source_ref):
    row_count = source_ref.shape[0]
    places = source_ref[...].reshape(1, row_count) - lax.axis_index(AXES) * row_count
    return jnp.where(places < 0, places + row_count * lax.axis_size(AXES), places)


def one_hot(former, latter):
    return (former == latter).astype(F32).astype(BF16)


def vfe_stats(seen_ref, stats_ref, product_ref):
    counts, totals, squares, lives = (seen_ref[:, at] for at in range(4))
    count = column_sum(counts)
    center = column_sum(totals) / count
    moves = totals / jnp.maximum(counts, 1.0) - center
    rate = lax.rsqrt(column_sum(squares + counts * moves * moves) / count + EPS_NORM)
    stats_ref[...] = jnp.zeros(stats_ref.shape, F32)
    stats_ref[0:1] = count
    stats_ref[1:2] = center
    stats_ref[2:3] = rate
    stats_ref[3:4] = column_sum(lives)
    devices = seen_ref.shape[0]
    share = share_of(WIDTH, devices)
    mine = lax.axis_index(AXES) * share
    lanes = lax.broadcasted_iota(jnp.int32, lives.shape, 1)
    product_ref[...] = jnp.zeros(product_ref.shape, F32)
    for at in range(share):
        picked = jnp.sum(jnp.where(lanes == mine + at, lives, 0.0), axis=1, keepdims=True)
        product_ref[at : at + 1] = rate * column_sum(seen_ref[:, 4 + at] + picked * moves)


def step_of(refs, step):
    windows = STEP // CELLS
    return [
        ref.at[step * windows : (step + 1) * windows]
        if len(ref.shape) == 3
        else ref.at[step * STEP : (step + 1) * STEP]
        for ref in refs
    ]


def first_kernel(*refs, head):
    lifted_ref, occupied_ref, bn_gain, bn_shift, back_bias, gains, offsets = refs[:7]
    if head:
        seen_ref, packed, qkv_ref, out_ref, cotangent_ref = refs[7:12]
        weights = refs[12:21]
        stats, hat_product, edge = refs[21:24]
        arrays = refs[24:36]
        cotangent, semaphores = refs[36:]
        copies = Copies(semaphores)
        arrival = copies.start(cotangent_ref.at[:HALF], cotangent)
        unpack(packed, qkv_ref, out_ref, *weights)
        vfe_stats(seen_ref, stats, hat_product)
        rows = slice(0, HEAD)
    else:
        stats = refs[7]
        weights = refs[8:17]
        arrays = refs[17:]
        rows = slice(HEAD, lifted_ref.shape[0])
    result, vfe_slope, carried, *saved = arrays
    hat = (lifted_ref[rows] - stats[1:2]) * stats[2:3]
    values, steep = gelu_parts(hat * bn_gain[0:1] + bn_shift[0:1])
    vfe_slope[...] = steep
    carried[...] = values
    live = live_column(occupied_ref)[rows]
    rows = layer_rows(0, values, live, (*weights, back_bias, gains, offsets), saved)
    result[...] = rows
    if head:
        arrival.wait()
        edge[:, :WIDTH] = rows[:HALF]
        edge[:, WIDTH : 2 * WIDTH] = cotangent[...]
        edge[:, 2 * WIDTH :] = jnp.broadcast_to(live[:HALF], (HALF, WIDTH))


def second_kernel(first_ref, rest_ref, cotangent_ref, occupied_ref, edge, source_ref, *refs):
    weights = refs[:12]
    sent = refs[12]
    arrays = refs[13:-2]
    table, sums = refs[-2:]
    row_count = cotangent_ref.shape[0]
    for rows, ref in ((slice(0, HEAD), first_ref), (slice(HEAD, row_count), rest_ref)):
        high, low = halves(ref[...])
        table[rows, :WIDTH] = high
        table[rows, WIDTH : 2 * WIDTH] = low
    high, low = halves(cotangent_ref[...])
    table[:row_count, 2 * WIDTH : 3 * WIDTH] = high
    table[:row_count, 3 * WIDTH : 4 * WIDTH] = low
    table[:row_count, 4 * WIDTH :] = jnp.broadcast_to(live_column(occupied_ref), (row_count, WIDTH)).astype(BF16)
    spare = table.shape[0] - row_count
    tail = jnp.concatenate([edge[...], jnp.zeros((spare - HALF, 3 * WIDTH), F32)], axis=0)
    high, low = halves(tail)
    table[row_count:, :WIDTH] = high[:, :WIDTH]
    table[row_count:, WIDTH : 2 * WIDTH] = low[:, :WIDTH]
    table[row_count:, 2 * WIDTH : 3 * WIDTH] = high[:, WIDTH : 2 * WIDTH]
    table[row_count:, 3 * WIDTH : 4 * WIDTH] = low[:, WIDTH : 2 * WIDTH]
    table[row_count:, 4 * WIDTH :] = high[:, 2 * WIDTH :]
    places = jnp.broadcast_to(places_of(source_ref).astype(F32), (8, row_count))
    column = places.T[:, :1].astype(jnp.int32)
    lanes = lax.broadcasted_iota(jnp.int32, (STEP, table.shape[0]), 1)
    for step in range(row_count // STEP):
        result, live_keep, cotangent_keep, carried, *saved = step_of(arrays, step)
        gathered = nn(one_hot(lanes, column[step * STEP : (step + 1) * STEP]), table[...])
        values = gathered[:, :WIDTH] + gathered[:, WIDTH : 2 * WIDTH]
        live = gathered[:, 4 * WIDTH :]
        grad = live * (gathered[:, 2 * WIDTH : 3 * WIDTH] + gathered[:, 3 * WIDTH : 4 * WIDTH])
        carried[...] = values
        cotangent_keep[...] = grad
        live_keep[...] = live[:, :1]
        rows = layer_rows(1, values, live[:, :1], weights, saved)
        result[...] = rows
        count = column_sum(live)
        if step == 0:
            sums[...] = jnp.zeros(sums.shape, F32)
            sums[5:6] = column_sum(live * rows) / jnp.maximum(count, 1.0)
        moved = rows - sums[5:6]
        sums[0:1] += count
        sums[1:2] += column_sum(live * moved)
        sums[2:3] += column_sum(live * moved * moved)
        sums[3:4] += column_sum(grad)
        sums[4:5] += column_sum(grad * moved)
    count = sums[0:1]
    move = sums[1:2] / jnp.maximum(count, 1.0)
    stats = jnp.concatenate(
        [
            count,
            sums[5:6] + move,
            sums[2:3] - count * move * move,
            sums[3:4],
            sums[4:5] - move * sums[3:4],
            jnp.zeros((3, WIDTH), F32),
        ],
        axis=0,
    )
    sent[...] = jnp.broadcast_to(stats[None], sent.shape)


def second_back_kernel(seen_ref, bn_gain, bn_shift, source_ref, *refs, ffns):
    weights = refs[:10]
    arrays = refs[10:23]
    edge, grad_head, grad_rest, out_rows, neck, small = refs[23:29]
    quarters = refs[29 : 29 + ffns]
    sum_qkv, sum_out, sum_up, sum_down, joined = refs[29 + ffns :]
    row_count = out_rows.shape[0]
    counts, means, squares, grads, products = (seen_ref[:, row] for row in range(5))
    count = column_sum(counts)
    center = column_sum(counts * means) / count
    moves = means - center
    rate = lax.rsqrt(column_sum(squares + counts * moves * moves) / count + EPS_NORM)
    gain_grad = rate * column_sum(products + moves * grads)
    shift_grad = column_sum(grads)
    neck[...] = jnp.concatenate([gain_grad, shift_grad, jnp.zeros((6, WIDTH), F32)], axis=0)
    for held in (small, sum_qkv, sum_out, sum_up, sum_down):
        held[...] = jnp.zeros(held.shape, F32)
    places = places_of(source_ref)
    down = lax.broadcasted_iota(jnp.int32, (-(-(row_count + HALF) // 8) * 8, STEP), 0)
    placed = None
    for step in range(row_count // STEP):
        result, live_keep, cotangent_keep, carried, packed_keep, high_keep, low_keep, *keeps = step_of(arrays, step)
        live = live_keep[...]
        hat = (result[...] - center) * rate
        neck_rows = live * (hat * bn_gain[1:2] + bn_shift[1:2])
        grad = rate * bn_gain[1:2] * (
            cotangent_keep[...] - live * (hat * gain_grad + shift_grad) / count
        )
        grad_joined, grad_mixed = ffn_rows_back(
            1, grad, keeps, weights[:4] + weights[6:10], (small, sum_out, sum_up, sum_down)
        )
        grad_values = attention_rows_back(
            1,
            carried[...],
            live,
            grad_joined,
            grad_mixed,
            (packed_keep, high_keep, low_keep),
            weights[4:6],
            sum_qkv,
        )
        pieces = jnp.concatenate(halves(grad_values) + halves(neck_rows), axis=1)
        moved = nn(one_hot(down, places[:, step * STEP : (step + 1) * STEP]), pieces)
        moved = jnp.concatenate(
            [
                moved[:, :WIDTH] + moved[:, WIDTH : 2 * WIDTH],
                moved[:, 2 * WIDTH : 3 * WIDTH] + moved[:, 3 * WIDTH :],
            ],
            axis=1,
        )
        placed = moved if placed is None else placed + moved
    grad_head[...] = placed[:HEAD, :WIDTH]
    grad_rest[...] = placed[HEAD:row_count, :WIDTH]
    out_rows[...] = placed[:row_count, WIDTH:]
    edge[...] = placed[row_count : row_count + HALF]
    for block in range(3):
        joined[block * WIDTH : (block + 1) * WIDTH] = sum_qkv[:, block * WIDTH : (block + 1) * WIDTH]
    joined[3 * WIDTH :] = sum_out[...]
    units, part = sum_up.shape[0] // ffns, joined.shape[0] // ffns
    mine = ffn_index(ffns)
    for k, quarter in enumerate(quarters):
        number = mine ^ k
        rows = pl.ds(pl.multiple_of(number * units, units), units)
        quarter[:units] = sum_up[rows]
        quarter[units : 2 * units] = sum_down[rows]
        quarter[2 * units :] = joined[pl.ds(pl.multiple_of(number * part, part), part)]


def share_layer(shared, row, sums, ffns):
    sum_qkv, sum_out, sum_up, sum_down = sums
    devices = shared.shape[0]
    row = share_units(shared, row, sum_up, sum_down, ffns)
    for block in range(3):
        row = share_rows(shared, row, sum_qkv[:, block * WIDTH : (block + 1) * WIDTH], devices)
    return share_rows(shared, row, sum_out, devices)


def first_back_kernel(*refs, head, ffns):
    grad_ref, stats, gains, offsets, occupied_ref, lifted_ref, feats_ref = refs[:7]
    weights, keeps, refs = refs[7:15], refs[15:26], refs[26:]
    rows = slice(0, HEAD) if head else slice(HEAD, lifted_ref.shape[0])
    if head:
        edge, out_rows, small_second = refs[:3]
        held_sums, quarters = refs[3:10], refs[10 : 10 + ffns]
        pillars, grad_affine, shared = refs[10 + ffns : 13 + ffns]
        sums, grad, affine, semaphores = refs[13 + ffns : 20 + ffns], *refs[20 + ffns :]
        for held, before in zip(sums, held_sums):
            held[...] = before[...]
        grad[...] = grad_ref[...]
        grad[:HALF] = edge[:, :WIDTH]
    else:
        grad_affine, sums, affine, semaphores = refs[0], refs[1:8], *refs[8:]
        for held in sums:
            held[...] = jnp.zeros(held.shape, F32)
        grad = grad_ref
    copies = Copies(semaphores)
    if head:
        copies.start(edge.at[:, WIDTH:], pillars.at[:HALF])
        copies.start(out_rows.at[HALF:], pillars.at[HALF:])
    small_ffn, sum_out, sum_up, sum_down, sum_qkv, sum_feats, small = sums
    joined, mixed = ffn_rows_back(
        0, grad[...], keeps[5:], (*weights[:4], *weights[6:8], gains, offsets), (small_ffn, sum_out, sum_up, sum_down)
    )
    vfe_slope, carried, packed_keep, high_keep, low_keep = keeps[:5]
    rows_grad = attention_rows_back(
        0,
        carried[...],
        live_column(occupied_ref)[rows],
        joined,
        mixed,
        (packed_keep, high_keep, low_keep),
        weights[4:6],
        sum_qkv,
    )
    rows_grad = rows_grad * vfe_slope[...]
    affine[...] = rows_grad
    copies.start(affine, grad_affine)
    small[0:1] += column_sum(rows_grad * (lifted_ref[rows] - stats[1:2]) * stats[2:3])
    small[1:2] += column_sum(rows_grad)
    sum_feats[...] += product(tn, halves(feats_ref[rows]), halves(rows_grad))
    if head:
        devices = shared.shape[0]
        shared[...] = jnp.zeros(shared.shape, F32)
        quarter = quarters[0][...]
        for other in quarters[1:]:
            quarter = quarter + other[...]
        units = sum_up.shape[0] // ffns
        row = share_rows(shared, 0, quarter[: 2 * units], devices)
        row = share_rows(shared, row, quarter[2 * units :], devices)
        row = share_layer(shared, row, (sum_qkv, sum_out, sum_up, sum_down), ffns)
        row = share_rows(shared, row, small_second[...], devices)
        row = share_rows(shared, row, small_ffn[...], devices)
        row = share_rows(shared, row, sum_feats, devices)
        shared[:, row : row + 2] = jnp.broadcast_to(small[0:2][None], (devices, 2, WIDTH))
    for copy in copies.started:
        copy.wait()


def relay_kernel(arrived, hat_product, stats, bn_gain, returned, vfe_grads, *, ffns, counts):
    unit_rows, quarter_rows, layer_rows, small_rows, part = counts
    devices = returned.shape[0]
    later = unit_rows + quarter_rows
    begin = later + ffns * unit_rows
    end = begin + layer_rows + small_rows
    total = jnp.sum(arrived[:, later:], axis=0)
    first_units, first_rest = total[: ffns * unit_rows], total[begin - later : end - later]
    tail = total[end - later :]
    blocks = []
    for f in range(ffns):
        block = arrived[f, :later]
        for device in range(f + ffns, devices, ffns):
            block = block + arrived[device, :later]
        blocks.append(block)
    gain, shift = tail[part : part + 1], tail[part + 1 : part + 2]
    lanes = lax.broadcasted_iota(jnp.int32, (part, WIDTH), 1)
    mine = lax.axis_index(AXES) * part + lax.broadcasted_iota(jnp.int32, (part, WIDTH), 0)
    live_sum = jnp.sum(jnp.where(lanes == mine, stats[3:4], 0.0), axis=1, keepdims=True)
    grad_w_vfe = stats[2:3] * bn_gain[0:1] * (
        tail[:part] - (hat_product[:part] * gain + live_sum * shift) / stats[0:1]
    )
    rows = jnp.concatenate([block[unit_rows:] for block in blocks] + [first_rest, grad_w_vfe], axis=0)
    room = returned.shape[1] - 2 * unit_rows
    if rows.shape[0] < room:
        rows = jnp.concatenate([rows, jnp.zeros((room - rows.shape[0], WIDTH), F32)], axis=0)
    returned[:, 2 * unit_rows :] = jnp.broadcast_to(rows[None], (devices,) + rows.shape)
    for device in range(devices):
        f = device % ffns
        returned[device, :unit_rows] = blocks[f][:unit_rows]
        returned[device, unit_rows : 2 * unit_rows] = first_units[f * unit_rows : (f + 1) * unit_rows]
    vfe_grads[...] = jnp.concatenate([gain, shift, jnp.zeros((6, WIDTH), F32)], axis=0)


def feats_back_kernel(affine_head, affine_rest, lifted_ref, occupied_ref, stats, vfe_grads, bn_gain, weight_ref, grad_feats):
    sums = vfe_grads[...]
    scale = stats[2:3] * bn_gain[0:1]
    hat = (lifted_ref[...] - stats[1:2]) * stats[2:3]
    grad = scale * (
        jnp.concatenate([affine_head[...], affine_rest[...]], axis=0)
        - live_column(occupied_ref) * (hat * sums[0:1] + sums[1:2]) / stats[0:1]
    )
    grad_feats[...] = product(nt, halves(grad), halves(weight_ref[...]))


def last_kernel(
    returned,
    vfe_grads,
    neck,
    grad_w_vfe,
    grad_bn_gain,
    grad_bn_shift,
    grad_w_qkv,
    grad_w_out,
    grad_w_in,
    grad_b_in,
    grad_w_back,
    grad_b_back,
    grad_ln_gain,
    grad_ln_shift,
    *,
    ffns,
):
    devices = returned.shape[0]
    units = grad_w_in.shape[1]
    part = share_of(WIDTH, devices)
    unit_rows = share_of(2 * units, devices)
    at = 0

    def take(count):
        nonlocal at
        rows = joined_rows(returned, at, count)
        at += share_of(count, devices)
        return rows

    blocks = [take(2 * units) for layer in range(2)]
    mine = lax.rem(lax.axis_index(AXES), ffns)
    for layer in (1, 0):
        grad_w_in[layer] = blocks[1 - layer][:units]
        grad_w_back[layer] = blocks[1 - layer][units:]
        if layer:
            rows = jnp.concatenate([take(4 * WIDTH // ffns) for f in range(ffns)], axis=0)
        else:
            rows = jnp.concatenate([take(WIDTH) for block in range(4)], axis=0)
        for block in range(3):
            grad_w_qkv[layer, :, block * WIDTH : (block + 1) * WIDTH] = rows[block * WIDTH : (block + 1) * WIDTH]
        grad_w_out[layer] = rows[3 * WIDTH :]
    for layer in (1, 0):
        small = take(8)
        grad_b_back[layer : layer + 1] = small[0:1]
        grad_ln_gain[2 * layer : 2 * layer + 1] = small[1:2]
        grad_ln_shift[2 * layer : 2 * layer + 1] = small[2:3]
        grad_ln_gain[2 * layer + 1 : 2 * layer + 2] = small[3:4]
        grad_ln_shift[2 * layer + 1 : 2 * layer + 2] = small[4:5]
        held = jnp.zeros((1, units), F32)
        for f in range(ffns):
            row, lane = divmod(f * units, WIDTH)
            held = jnp.where(mine == f, small[5 + row : 6 + row, lane : lane + units], held)
        grad_b_in[layer : layer + 1] = held
    grad_w_vfe[...] = take(WIDTH)
    grad_bn_gain[0:1] = vfe_grads[0:1]
    grad_bn_gain[1:2] = neck[0:1]
    grad_bn_shift[0:1] = vfe_grads[1:2]
    grad_bn_shift[1:2] = neck[1:2]


def spread_rows(pieces, axes):
    return lax.all_to_all(pieces, axes, 0, 0)


def partner(rows, k):
    return lax.ppermute(rows, "ffn", [(i, i ^ k) for i in range(lax.axis_size("ffn"))])


def passed_along(rows, by):
    peers = lax.axis_size(AXES)
    return lax.ppermute(rows, AXES, [(i, (i + by) % peers) for i in range(peers)])


def on_device(
    pillar_feats,
    occupied,
    shifted_source_rows,
    w_vfe,
    bn_gain,
    bn_shift,
    query_key_value_weight,
    attention_output_weight,
    up_weight_matrix,
    up_bias_rows,
    down_weight_matrix,
    down_bias_rows,
    layernorm_gains,
    layernorm_offsets,
    cotangent,
):
    row_count = pillar_feats.shape[0]
    spread = row_count + -(-HALF // 16) * 16
    ffns = lax.axis_size("ffn")
    devices = lax.axis_size(AXES)
    units = up_weight_matrix.shape[2]
    hidden = units * ffns
    windows = row_count // CELLS
    part = share_of(WIDTH, devices)
    piece = share_of(2 * units, devices)
    rest = 4 * part + 2 * share_of(8, devices)
    stats_rows = -(-(4 + part) // 8) * 8
    quarter_part = share_of(4 * WIDTH // ffns, devices)
    shared_rows = -(-((1 + ffns) * piece + quarter_part + rest + part + 2) // 8) * 8
    returned_rows = -(-(2 * piece + ffns * quarter_part + rest + part) // 8) * 8
    rows_shape = shape(row_count, WIDTH)
    rest_rows = row_count - HEAD

    def keeps(make, rows):
        weights = make(rows // CELLS, CELLS, HEADS * CELLS, dtype=BF16)
        plain, wide = make(rows, WIDTH), make(rows, hidden)
        return [plain, make(rows, 3 * WIDTH), weights, weights, plain, plain, wide, wide, plain, plain]

    lifted, sent, packed = run(
        vfe_kernel,
        "vfe",
        (rows_shape, shape(devices, stats_rows, WIDTH), shape(4 * units + 8, WIDTH)),
        (
            pillar_feats,
            w_vfe,
            occupied,
            up_weight_matrix.transpose(0, 2, 1),
            down_weight_matrix,
            up_bias_rows,
        ),
    )
    seen = spread_rows(sent, AXES)
    packed = lax.all_gather(packed, "ffn", axis=0, tiled=False)
    weight_dims = (
        [(2, hidden, WIDTH, BF16)] * 4
        + [(2, hidden, F32)]
        + [(2, WIDTH, 3 * WIDTH, BF16)] * 2
        + [(2, WIDTH, WIDTH, BF16)] * 2
    )
    norms = pinned((down_bias_rows, layernorm_gains, layernorm_offsets))
    bn_pair = pinned((bn_gain, bn_shift))
    head_arrays = [kept(HEAD, WIDTH)] * 2 + keeps(kept, HEAD)
    rest_arrays = [kept(rest_rows, WIDTH)] * 2 + keeps(kept, rest_rows)
    outs = run(
        functools.partial(first_kernel, head=True),
        "first",
        [kept(*dims[:-1], dtype=dims[-1]) for dims in weight_dims]
        + [kept(8, WIDTH), kept(8, WIDTH), kept(HALF, 3 * WIDTH)]
        + head_arrays,
        (
            lifted,
            occupied,
            bn_gain,
            bn_shift,
            down_bias_rows,
            layernorm_gains,
            layernorm_offsets,
            Pinned(seen),
            packed,
            query_key_value_weight,
            attention_output_weight,
            Far(cotangent),
        ),
        scratch=[pltpu.VMEM((HALF, WIDTH), F32)],
        copies=1,
        flops=1e9,
    )
    weights, (stats, hat_product, edge) = outs[:9], outs[9:12]
    first_head, *head_keep = outs[12:]
    layer_weights = pinned(weights) + norms
    back_weights = pinned(weights[:4] + weights[5:]) + norms[1:]
    edge = passed_along(edge, -1)
    first_rest, *rest_keep = run(
        functools.partial(first_kernel, head=False),
        "first_rest",
        rest_arrays,
        (Pinned(lifted), Pinned(occupied), *bn_pair, *norms, Pinned(stats), *pinned(weights)),
        flops=1e9,
    )
    sent, *second_keep = run(
        second_kernel,
        "second",
        [kept(devices, 8, WIDTH), kept(row_count, WIDTH), kept(row_count, 1), kept(row_count, WIDTH)]
        + [kept(row_count, WIDTH)]
        + keeps(kept, row_count)[1:],
        (
            Pinned(first_head),
            Pinned(first_rest),
            Pinned(cotangent),
            Pinned(occupied),
            Pinned(edge),
            Pinned(shifted_source_rows),
            *layer_weights,
        ),
        scratch=[pltpu.VMEM((spread, 5 * WIDTH), BF16), pltpu.VMEM((8, WIDTH), F32)],
        flops=2e9,
    )
    seen = spread_rows(sent, AXES)
    sum_shapes = [
        pltpu.VMEM((8, WIDTH), F32),
        pltpu.VMEM((WIDTH, WIDTH), F32),
        pltpu.VMEM((hidden, WIDTH), F32),
        pltpu.VMEM((hidden, WIDTH), F32),
    ]
    sum_qkv = pltpu.VMEM((WIDTH, 3 * WIDTH), F32)
    edge, grad_head, grad_rest, out_rows, neck, small, *quarters = run(
        functools.partial(second_back_kernel, ffns=ffns),
        "second_back",
        [
            kept(HALF, 2 * WIDTH),
            kept(HEAD, WIDTH),
            kept(rest_rows, WIDTH),
            kept(row_count, WIDTH),
            kept(8, WIDTH),
            kept(8, WIDTH),
        ]
        + [kept(2 * units + 4 * WIDTH // ffns, WIDTH)] * ffns,
        (Pinned(seen), *bn_pair, Pinned(shifted_source_rows), *back_weights, *pinned(second_keep)),
        scratch=[sum_qkv] + sum_shapes[1:] + [pltpu.VMEM((4 * WIDTH, WIDTH), F32)],
        flops=4e9,
    )
    edge = passed_along(edge, 1)
    quarters = [quarters[0]] + [partner(quarters[k], k) for k in range(1, ffns)]
    sums = sum_shapes + [sum_qkv, pltpu.VMEM((WIDTH, WIDTH), F32), pltpu.VMEM((8, WIDTH), F32)]
    first_back_args = (stats, layernorm_gains, layernorm_offsets, occupied, lifted, pillar_feats, *weights[:4], *weights[5:])
    affine_rest, *held_sums = run(
        functools.partial(first_back_kernel, head=False, ffns=ffns),
        "first_back",
        [Far(shape(rest_rows, WIDTH))] + sums,
        pinned((grad_rest, *first_back_args, *rest_keep)),
        scratch=[pltpu.VMEM((rest_rows, WIDTH), F32)],
        copies=1,
        flops=3e9,
    )
    pillars_out, affine_head, shared = run(
        functools.partial(first_back_kernel, head=True, ffns=ffns),
        "first_back_edge",
        [Far(rows_shape), Far(shape(HEAD, WIDTH)), kept(devices, shared_rows, WIDTH)],
        pinned((grad_head, *first_back_args, *head_keep, edge, out_rows, small, *held_sums, *quarters)),
        scratch=sums + [pltpu.VMEM((HEAD, WIDTH), F32)] * 2,
        copies=3,
        flops=3e9,
    )
    arrived = spread_rows(shared, AXES)
    returned, vfe_grads = run(
        functools.partial(relay_kernel, ffns=ffns, counts=(piece, quarter_part, 4 * part, rest - 4 * part, part)),
        "relay",
        (shape(devices, returned_rows, WIDTH), shape(8, WIDTH)),
        pinned((arrived, hat_product, stats, bn_gain)),
    )
    returned = spread_rows(returned, AXES)
    (grad_feats,) = run(
        feats_back_kernel,
        "feats_back",
        (rows_shape,),
        (affine_head, affine_rest, lifted, occupied, stats, vfe_grads, bn_gain, w_vfe),
    )
    grads = list(run(
        functools.partial(last_kernel, ffns=ffns),
        "last",
        (
            shape(WIDTH, WIDTH),
            shape(2, WIDTH),
            shape(2, WIDTH),
            shape(2, WIDTH, 3 * WIDTH),
            shape(2, WIDTH, WIDTH),
            shape(2, units, WIDTH),
            shape(2, units),
            shape(2, units, WIDTH),
            shape(2, WIDTH),
            shape(4, WIDTH),
            shape(4, WIDTH),
        ),
        (Pinned(returned), vfe_grads, neck),
    ))
    grads[5] = grads[5].transpose(0, 2, 1)
    return (pillars_out, grad_feats, *grads)


def solution(mesh):
    return jax.shard_map(
        on_device,
        mesh=mesh,
        in_specs=(
            P(("win", "ffn"), None),
            P(("win", "ffn")),
            P(("win", "ffn")),
            P(),
            P(),
            P(),
            P(),
            P(),
            P(None, None, "ffn"),
            P(None, "ffn"),
            P(None, "ffn", None),
            P(),
            P(),
            P(),
            P(("win", "ffn"), None),
        ),
        out_specs=(
            P(("win", "ffn"), None),
            P(("win", "ffn"), None),
            P(),
            P(),
            P(),
            P(),
            P(),
            P(None, None, "ffn"),
            P(None, "ffn"),
            P(None, "ffn", None),
            P(),
            P(),
            P(),
        ),
        check_vma=False,
    )
```

```python
import functools

import jax
import jax.numpy as jnp
from jax import lax
from jax.experimental import pallas as pl
from jax.experimental.pallas import tpu as pltpu
from jax.sharding import PartitionSpec as P

HEADS = 8
CELLS = 144
HALF = CELLS // 2
WIDTH = 128
EPS_NORM = 1e-05
NEG_FILL = -1000000000.0
AXES = ("win", "ffn")
STEP = 3 * CELLS
HEAD = 2 * CELLS
TILE_ROWS = WIDTH // HEADS
TILES = CELLS // TILE_ROWS
CHUNKS = ((0, 2), (2, 4), (4, 6), (6, 8), (8, 9))
F32 = jnp.float32
BF16 = jnp.bfloat16
VMEM_LIMIT = 28 * 1024 * 1024


def shape(*dims, dtype=F32):
    return pltpu.HBM(dims, dtype)


def kept(*dims, dtype=F32):
    return pltpu.VMEM(dims, dtype)


class Pinned:
    def __init__(self, value):
        self.value = value


class Far:
    def __init__(self, value):
        self.value = value


def run(kernel, name, outs, args, scratch=(), copies=0, flops=1e8):
    near, far = pl.BlockSpec(memory_space=pltpu.VMEM), pl.BlockSpec(memory_space=pltpu.HBM)
    values = []
    for arg in args:
        space = pltpu.VMEM if isinstance(arg, Pinned) else pltpu.HBM
        value = arg.value if isinstance(arg, (Pinned, Far)) else arg
        values.append(pltpu.with_memory_space_constraint(value, space))
    scratch = list(scratch)
    if copies:
        scratch.append(pltpu.SemaphoreType.DMA((copies,)))
    return pl.pallas_call(
        kernel,
        out_shape=[out.value if isinstance(out, Far) else out for out in outs],
        in_specs=[far if isinstance(arg, Far) else near for arg in args],
        out_specs=[far if isinstance(out, Far) else near for out in outs],
        scratch_shapes=scratch,
        compiler_params=pltpu.CompilerParams(vmem_limit_bytes=VMEM_LIMIT),
        cost_estimate=pl.CostEstimate(flops=int(flops), bytes_accessed=1000000, transcendentals=0),
        name=name,
    )(*values)


def pinned(values):
    return [Pinned(value) for value in values]


class Copies:
    def __init__(self, semaphores):
        self.semaphores = semaphores
        self.started = []

    def start(self, source, target):
        copy = pltpu.make_async_copy(source, target, self.semaphores.at[len(self.started)])
        copy.start()
        self.started.append(copy)
        return copy


def scratch_like(arrays):
    return [pltpu.VMEM(array.shape, array.dtype) for array in arrays]


def ffn_index(ffns):
    return lax.rem(lax.axis_index(AXES), ffns)


def share_of(rows, devices):
    return -(-rows // devices)


def halves(values):
    high = values.astype(BF16)
    return high, (values - high.astype(F32)).astype(BF16)


def nn(former, latter):
    return lax.dot_general(former, latter, (((1,), (0,)), ((), ())), preferred_element_type=F32)


def nt(former, latter):
    return lax.dot_general(former, latter, (((1,), (1,)), ((), ())), preferred_element_type=F32)


def tn(former, latter):
    return lax.dot_general(former, latter, (((0,), (0,)), ((), ())), preferred_element_type=F32)


def product(kind, former, latter):
    columns = latter[0].shape[0 if kind is nt else 1]
    if columns == WIDTH:
        both = kind(former[0], jnp.concatenate(latter, axis=0 if kind is nt else 1))
        return both[:, :columns] + (both[:, columns:] + kind(former[1], latter[0]))
    if kind is tn:
        rows = former[0].shape[1]
        both = kind(jnp.concatenate(former, axis=1), latter[0])
        return both[:rows] + (both[rows:] + kind(former[0], latter[1]))
    if former[0].shape[1] == WIDTH:
        twice = jnp.concatenate([latter[0]] * 2, axis=1 if kind is nt else 0)
        return kind(jnp.concatenate(former, axis=1), twice) + kind(former[0], latter[1])
    return kind(former[0], latter[0]) + (kind(former[0], latter[1]) + kind(former[1], latter[0]))


def gelu_parts(values):
    below = 0.5 * (1.0 + lax.erf(values * 0.7071067811865476))
    density = 0.3989422804014327 * jnp.exp(-0.5 * values * values)
    return values * below, below + values * density


def normed_rows(values):
    center = jnp.mean(values, axis=-1, keepdims=True)
    moved = values - center
    rate = lax.rsqrt(jnp.mean(moved * moved, axis=-1, keepdims=True) + EPS_NORM)
    return moved * rate, rate


def normed_back(grad, hat, rate, gain):
    scaled = grad * gain
    first = jnp.mean(scaled, axis=-1, keepdims=True)
    second = jnp.mean(scaled * hat, axis=-1, keepdims=True)
    return rate * (scaled - first - hat * second)


def live_column(occupied_ref):
    row = occupied_ref[...].astype(F32).reshape(1, occupied_ref.shape[0])
    return jnp.broadcast_to(row, (8, row.shape[1])).T[:, :1]


def column_sum(values):
    return jnp.sum(values, axis=0, keepdims=True)


def head_mask():
    dims = (HEADS, TILE_ROWS, WIDTH)
    lane_head = lax.broadcasted_iota(jnp.int32, dims, 2) // TILE_ROWS
    return (lane_head == lax.broadcasted_iota(jnp.int32, dims, 0)).astype(F32)


def per_head(rows, mask):
    count = rows.shape[0] // TILE_ROWS
    return (rows.reshape(count, 1, TILE_ROWS, WIDTH) * mask[None]).reshape(count * WIDTH, WIDTH)


def from_heads(table, mask):
    parts = []
    for at in range(0, table.shape[1], WIDTH):
        turned = table[:, at : at + WIDTH].T.reshape(HEADS, TILE_ROWS, WIDTH)
        parts.append(jnp.sum(turned * mask, axis=0))
    return parts


def high_and_low(values):
    high, low = halves(values.T)
    return jnp.concatenate([high, low], axis=0), high


def stacked_product(stack, high_alone, weights):
    both = nn(stack, weights[0])
    return both[:WIDTH] + (both[WIDTH:] + nn(high_alone, weights[1]))


def window_mix(query, key, value, live, mask, mask_low, keep_high, keep_low):
    query_high, query_low = halves(query)
    key_high, key_low = halves(key)
    key_stack = jnp.concatenate([key_high, key_low, key_high], axis=1)
    turned = high_and_low(value)
    mixed = []
    for first, last in CHUNKS:
        rows = slice(first * TILE_ROWS, last * TILE_ROWS)
        lanes = slice(first * WIDTH, last * WIDTH)
        high = per_head(query_high[rows], mask_low)
        low = per_head(query_low[rows], mask_low)
        scores = nt(key_stack, jnp.concatenate([high, high, low], axis=1))
        scores = jnp.where(live > 0, scores, NEG_FILL)
        weights = jnp.exp(scores - jnp.max(scores, axis=0, keepdims=True))
        weights = weights * (1.0 / column_sum(weights))
        weights = halves(weights)
        keep_high[:, lanes] = weights[0]
        keep_low[:, lanes] = weights[1]
        mixed += from_heads(stacked_product(*turned, weights), mask)
    return jnp.concatenate(mixed, axis=0)


def window_back(query, key, value, grad_mixed, live, mask, mask_low, high, low):
    query_high, query_low = (per_head(part, mask_low) for part in halves(query))
    grad_high, grad_low = (per_head(part, mask_low) for part in halves(grad_mixed))
    value_high, value_low = halves(value)
    value_stack = jnp.concatenate([value_high, value_low, value_high], axis=1)
    grad_weights = nt(value_stack, jnp.concatenate([grad_high, grad_high, grad_low], axis=1))
    weights = high.astype(F32) + low.astype(F32)
    grad_scores = weights * grad_weights
    grad_scores = live * (grad_scores - weights * column_sum(grad_scores))
    scores_high, scores_low = halves(grad_scores)

    def over_queries(upper, lower, high, low):
        both = nn(
            jnp.concatenate([upper, lower], axis=0), jnp.concatenate([high, low], axis=1)
        )
        return both[:CELLS, :WIDTH] + (both[:CELLS, WIDTH:] + both[CELLS:, :WIDTH])

    grad_query = stacked_product(*high_and_low(key), (scores_high, scores_low))
    return (
        0.25 * jnp.concatenate(from_heads(grad_query, mask), axis=0),
        over_queries(scores_high, scores_low, query_high, query_low),
        over_queries(high, low, grad_high, grad_low),
    )


def unpack(packed, qkv_ref, out_ref, up_high, up_low, down_high, down_low, bias, qkv_high, qkv_low, out_high, out_low):
    ffns = packed.shape[0]
    units = bias.shape[1] // ffns
    for one in range(2):
        for at in range(ffns):
            rows = slice(at * units, (at + 1) * units)
            high, low = halves(packed[at, one * units : (one + 1) * units])
            up_high[one, rows], up_low[one, rows] = high, low
            high, low = halves(packed[at, (2 + one) * units : (3 + one) * units])
            down_high[one, rows], down_low[one, rows] = high, low
        bias[one : one + 1] = jnp.concatenate(
            [packed[at, 4 * units + one : 4 * units + one + 1, :units] for at in range(ffns)], axis=1
        )
    qkv_high[...], qkv_low[...] = halves(qkv_ref[...])
    out_high[...], out_low[...] = halves(out_ref[...])


def layer_rows(one, values, live, weights, saved):
    up_high, up_low, down_high, down_low, bias, qkv_high, qkv_low, out_high, out_low, back_bias, gains, offsets = weights
    packed_keep, high_keep, low_keep, mixed_keep, hat_one, hidden_keep, slope, hat_two, rates = saved
    mask = head_mask()
    mask_low = mask.astype(BF16)
    qkv = product(nn, halves(values), (qkv_high[one], qkv_low[one]))
    query = 0.25 * qkv[:, :WIDTH]
    packed_keep[:, :WIDTH] = query
    packed_keep[:, WIDTH:] = qkv[:, WIDTH:]
    for at in range(values.shape[0] // CELLS):
        rows = slice(at * CELLS, (at + 1) * CELLS)
        mixed_keep[rows] = window_mix(
            query[rows],
            qkv[rows, WIDTH : 2 * WIDTH],
            qkv[rows, 2 * WIDTH :],
            live[rows],
            mask,
            mask_low,
            high_keep.at[at],
            low_keep.at[at],
        )
    mixed = mixed_keep[...]
    hat, rate = normed_rows(
        values + product(nn, halves(mixed), (out_high[one], out_low[one]))
    )
    hat_one[...] = hat
    first = hat * gains[2 * one : 2 * one + 1] + offsets[2 * one : 2 * one + 1]
    hidden, steep = gelu_parts(
        product(nt, halves(first), (up_high[one], up_low[one])) + bias[one : one + 1]
    )
    hidden_keep[...] = hidden
    slope[...] = steep
    summed = first + product(nn, halves(hidden), (down_high[one], down_low[one])) + back_bias[one : one + 1]
    hat, last_rate = normed_rows(summed)
    hat_two[...] = hat
    lanes = lax.broadcasted_iota(jnp.int32, hat.shape, 1)
    rates[...] = jnp.where(lanes < WIDTH // 2, rate, last_rate)
    return hat * gains[2 * one + 1 : 2 * one + 2] + offsets[2 * one + 1 : 2 * one + 2]


def ffn_rows_back(one, grad, saved, weights, sums):
    mixed_keep, hat_one, hidden_keep, slope, hat_two, rates = saved
    up_high, up_low, down_high, down_low, out_high, out_low, gains, offsets = weights
    up, down, out = (up_high[one], up_low[one]), (down_high[one], down_low[one]), (out_high[one], out_low[one])
    small, sum_out, sum_up, sum_down = sums
    hat = hat_two[...]
    grad_summed = normed_back(grad, hat, rates[:, WIDTH - 1 :], gains[2 * one + 1 : 2 * one + 2])
    small[3:4] += column_sum(grad * hat)
    small[4:5] += column_sum(grad)
    small[0:1] += column_sum(grad_summed)
    summed_halves = halves(grad_summed)
    grad_pre = product(nt, summed_halves, down) * slope[...]
    pre_halves = halves(grad_pre)
    hidden_halves = halves(hidden_keep[...])
    sum_down[...] += product(tn, hidden_halves, summed_halves)
    hat = hat_one[...]
    first = hat * gains[2 * one : 2 * one + 1] + offsets[2 * one : 2 * one + 1]
    sum_up[...] += product(tn, pre_halves, halves(first))
    bias_sum = column_sum(grad_pre)
    for at in range(bias_sum.shape[1] // WIDTH):
        small[5 + at : 6 + at] += bias_sum[:, at * WIDTH : (at + 1) * WIDTH]
    grad_first = grad_summed + product(nn, pre_halves, up)
    small[1:2] += column_sum(grad_first * hat)
    small[2:3] += column_sum(grad_first)
    grad_joined = normed_back(grad_first, hat, rates[:, 0:1], gains[2 * one : 2 * one + 1])
    joined_halves = halves(grad_joined)
    sum_out[...] += product(tn, halves(mixed_keep[...]), joined_halves)
    return grad_joined, product(nt, joined_halves, out)


def attention_rows_back(one, values, live, grad_joined, grad_mixed, saved, qkv_weights, sum_qkv):
    packed_keep, high_keep, low_keep = saved
    mask = head_mask()
    mask_low = mask.astype(BF16)
    parts = []
    for at in range(values.shape[0] // CELLS):
        rows = slice(at * CELLS, (at + 1) * CELLS)
        parts.append(
            window_back(
                packed_keep[rows, :WIDTH],
                packed_keep[rows, WIDTH : 2 * WIDTH],
                packed_keep[rows, 2 * WIDTH :],
                grad_mixed[rows],
                live[rows],
                mask,
                mask_low,
                high_keep[at],
                low_keep[at],
            )
        )
    grad_packed = halves(
        jnp.concatenate([jnp.concatenate(part, axis=1) for part in parts], axis=0)
    )
    sum_qkv[...] += product(tn, halves(values), grad_packed)
    return grad_joined + product(nt, grad_packed, (qkv_weights[0][one], qkv_weights[1][one]))


def share_rows(target, at, values, devices):
    count = values.shape[0]
    share = share_of(count, devices)
    for device in range(devices):
        begin = device * share
        if begin < count:
            held = min(share, count - begin)
            target[device, at : at + held] = values[begin : begin + held]
    return at + share


def share_units(target, at, sum_up, sum_down, ffns):
    units = sum_up.shape[0] // ffns
    for f in range(ffns):
        rows = slice(f * units, (f + 1) * units)
        joined = jnp.concatenate([sum_up[rows], sum_down[rows]], axis=0)
        at = share_rows(target, at, joined, target.shape[0])
    return at


def joined_rows(table, at, count):
    devices = table.shape[0]
    share = share_of(count, devices)
    if share % 8 == 0 and share * devices == count:
        return table[:, at : at + share].reshape(count, WIDTH)
    pieces = []
    for device in range(devices):
        begin = device * share
        if begin < count:
            pieces.append(table[device, at : at + min(share, count - begin)])
    return jnp.concatenate(pieces, axis=0)


def vfe_kernel(
    feats_ref, weight_ref, occupied_ref, up_ref, down_ref, bias_ref, lifted_ref, sent_ref, packed_ref
):
    devices = sent_ref.shape[0]
    units = up_ref.shape[1]
    feats = feats_ref[...]
    feats_halves = halves(feats)
    lifted = product(nn, feats_halves, halves(weight_ref[...]))
    lifted_ref[...] = lifted
    live = live_column(occupied_ref)
    count = jnp.sum(live, axis=0, keepdims=True)
    total = column_sum(live * lifted)
    moved = live * (lifted - total / jnp.maximum(count, 1.0))
    sent_ref[...] = jnp.zeros(sent_ref.shape, F32)
    stats = jnp.concatenate(
        [
            jnp.broadcast_to(count, (1, WIDTH)),
            total,
            column_sum(moved * moved),
            column_sum(live * feats),
        ],
        axis=0,
    )
    sent_ref[:, 0:4] = jnp.broadcast_to(stats[None], (devices, 4, WIDTH))
    share_rows(sent_ref, 4, product(tn, feats_halves, halves(moved)), devices)
    for one in range(2):
        packed_ref[one * units : (one + 1) * units] = up_ref[one]
        packed_ref[(2 + one) * units : (3 + one) * units] = down_ref[one]
    packed_ref[4 * units :] = jnp.zeros((8, WIDTH), F32)
    packed_ref[4 * units : 4 * units + 2, :units] = bias_ref[...]


def places_of(source_ref):
    row_count = source_ref.shape[0]
    places = source_ref[...].reshape(1, row_count) - lax.axis_index(AXES) * row_count
    return jnp.where(places < 0, places + row_count * lax.axis_size(AXES), places)


def one_hot(former, latter):
    return (former == latter).astype(F32).astype(BF16)


def vfe_stats(seen_ref, stats_ref, product_ref):
    counts, totals, squares, lives = (seen_ref[:, at] for at in range(4))
    count = column_sum(counts)
    center = column_sum(totals) / count
    moves = totals / jnp.maximum(counts, 1.0) - center
    rate = lax.rsqrt(column_sum(squares + counts * moves * moves) / count + EPS_NORM)
    stats_ref[...] = jnp.zeros(stats_ref.shape, F32)
    stats_ref[0:1] = count
    stats_ref[1:2] = center
    stats_ref[2:3] = rate
    stats_ref[3:4] = column_sum(lives)
    devices = seen_ref.shape[0]
    share = share_of(WIDTH, devices)
    mine = lax.axis_index(AXES) * share
    lanes = lax.broadcasted_iota(jnp.int32, lives.shape, 1)
    product_ref[...] = jnp.zeros(product_ref.shape, F32)
    for at in range(share):
        picked = jnp.sum(jnp.where(lanes == mine + at, lives, 0.0), axis=1, keepdims=True)
        product_ref[at : at + 1] = rate * column_sum(seen_ref[:, 4 + at] + picked * moves)


def step_of(refs, step):
    windows = STEP // CELLS
    return [
        ref.at[step * windows : (step + 1) * windows]
        if len(ref.shape) == 3
        else ref.at[step * STEP : (step + 1) * STEP]
        for ref in refs
    ]


def first_kernel(*refs, head):
    lifted_ref, occupied_ref, bn_gain, bn_shift, back_bias, gains, offsets = refs[:7]
    if head:
        seen_ref, packed, qkv_ref, out_ref, cotangent_ref = refs[7:12]
        weights = refs[12:21]
        stats, hat_product, edge = refs[21:24]
        arrays = refs[24:36]
        cotangent, semaphores = refs[36:]
        copies = Copies(semaphores)
        arrival = copies.start(cotangent_ref.at[:HALF], cotangent)
        unpack(packed, qkv_ref, out_ref, *weights)
        vfe_stats(seen_ref, stats, hat_product)
        rows = slice(0, HEAD)
    else:
        stats = refs[7]
        weights = refs[8:17]
        arrays = refs[17:]
        rows = slice(HEAD, lifted_ref.shape[0])
    result, vfe_slope, carried, *saved = arrays
    hat = (lifted_ref[rows] - stats[1:2]) * stats[2:3]
    values, steep = gelu_parts(hat * bn_gain[0:1] + bn_shift[0:1])
    vfe_slope[...] = steep
    carried[...] = values
    live = live_column(occupied_ref)[rows]
    rows = layer_rows(0, values, live, (*weights, back_bias, gains, offsets), saved)
    result[...] = rows
    if head:
        arrival.wait()
        edge[:, :WIDTH] = rows[:HALF]
        edge[:, WIDTH : 2 * WIDTH] = cotangent[...]
        edge[:, 2 * WIDTH :] = jnp.broadcast_to(live[:HALF], (HALF, WIDTH))


def second_kernel(first_ref, rest_ref, cotangent_ref, occupied_ref, edge, source_ref, *refs):
    weights = refs[:12]
    sent = refs[12]
    arrays = refs[13:-2]
    table, sums = refs[-2:]
    row_count = cotangent_ref.shape[0]
    for rows, ref in ((slice(0, HEAD), first_ref), (slice(HEAD, row_count), rest_ref)):
        high, low = halves(ref[...])
        table[rows, :WIDTH] = high
        table[rows, WIDTH : 2 * WIDTH] = low
    high, low = halves(cotangent_ref[...])
    table[:row_count, 2 * WIDTH : 3 * WIDTH] = high
    table[:row_count, 3 * WIDTH : 4 * WIDTH] = low
    table[:row_count, 4 * WIDTH :] = jnp.broadcast_to(live_column(occupied_ref), (row_count, WIDTH)).astype(BF16)
    spare = table.shape[0] - row_count
    tail = jnp.concatenate([edge[...], jnp.zeros((spare - HALF, 3 * WIDTH), F32)], axis=0)
    high, low = halves(tail)
    table[row_count:, :WIDTH] = high[:, :WIDTH]
    table[row_count:, WIDTH : 2 * WIDTH] = low[:, :WIDTH]
    table[row_count:, 2 * WIDTH : 3 * WIDTH] = high[:, WIDTH : 2 * WIDTH]
    table[row_count:, 3 * WIDTH : 4 * WIDTH] = low[:, WIDTH : 2 * WIDTH]
    table[row_count:, 4 * WIDTH :] = high[:, 2 * WIDTH :]
    places = jnp.broadcast_to(places_of(source_ref).astype(F32), (8, row_count))
    column = places.T[:, :1].astype(jnp.int32)
    lanes = lax.broadcasted_iota(jnp.int32, (STEP, table.shape[0]), 1)
    for step in range(row_count // STEP):
        result, live_keep, cotangent_keep, carried, *saved = step_of(arrays, step)
        gathered = nn(one_hot(lanes, column[step * STEP : (step + 1) * STEP]), table[...])
        values = gathered[:, :WIDTH] + gathered[:, WIDTH : 2 * WIDTH]
        live = gathered[:, 4 * WIDTH :]
        grad = live * (gathered[:, 2 * WIDTH : 3 * WIDTH] + gathered[:, 3 * WIDTH : 4 * WIDTH])
        carried[...] = values
        cotangent_keep[...] = grad
        live_keep[...] = live[:, :1]
        rows = layer_rows(1, values, live[:, :1], weights, saved)
        result[...] = rows
        count = column_sum(live)
        if step == 0:
            sums[...] = jnp.zeros(sums.shape, F32)
            sums[5:6] = column_sum(live * rows) / jnp.maximum(count, 1.0)
        moved = rows - sums[5:6]
        sums[0:1] += count
        sums[1:2] += column_sum(live * moved)
        sums[2:3] += column_sum(live * moved * moved)
        sums[3:4] += column_sum(grad)
        sums[4:5] += column_sum(grad * moved)
    count = sums[0:1]
    move = sums[1:2] / jnp.maximum(count, 1.0)
    stats = jnp.concatenate(
        [
            count,
            sums[5:6] + move,
            sums[2:3] - count * move * move,
            sums[3:4],
            sums[4:5] - move * sums[3:4],
            jnp.zeros((3, WIDTH), F32),
        ],
        axis=0,
    )
    sent[...] = jnp.broadcast_to(stats[None], sent.shape)


def second_back_kernel(seen_ref, bn_gain, bn_shift, source_ref, *refs, ffns):
    weights = refs[:10]
    arrays = refs[10:23]
    edge, grad_head, grad_rest, out_rows, neck, small = refs[23:29]
    quarters = refs[29 : 29 + ffns]
    sum_qkv, sum_out, sum_up, sum_down, joined = refs[29 + ffns :]
    row_count = out_rows.shape[0]
    counts, means, squares, grads, products = (seen_ref[:, row] for row in range(5))
    count = column_sum(counts)
    center = column_sum(counts * means) / count
    moves = means - center
    rate = lax.rsqrt(column_sum(squares + counts * moves * moves) / count + EPS_NORM)
    gain_grad = rate * column_sum(products + moves * grads)
    shift_grad = column_sum(grads)
    neck[...] = jnp.concatenate([gain_grad, shift_grad, jnp.zeros((6, WIDTH), F32)], axis=0)
    for held in (small, sum_qkv, sum_out, sum_up, sum_down):
        held[...] = jnp.zeros(held.shape, F32)
    places = places_of(source_ref)
    down = lax.broadcasted_iota(jnp.int32, (-(-(row_count + HALF) // 8) * 8, STEP), 0)
    placed = None
    for step in range(row_count // STEP):
        result, live_keep, cotangent_keep, carried, packed_keep, high_keep, low_keep, *keeps = step_of(arrays, step)
        live = live_keep[...]
        hat = (result[...] - center) * rate
        neck_rows = live * (hat * bn_gain[1:2] + bn_shift[1:2])
        grad = rate * bn_gain[1:2] * (
            cotangent_keep[...] - live * (hat * gain_grad + shift_grad) / count
        )
        grad_joined, grad_mixed = ffn_rows_back(
            1, grad, keeps, weights[:4] + weights[6:10], (small, sum_out, sum_up, sum_down)
        )
        grad_values = attention_rows_back(
            1,
            carried[...],
            live,
            grad_joined,
            grad_mixed,
            (packed_keep, high_keep, low_keep),
            weights[4:6],
            sum_qkv,
        )
        pieces = jnp.concatenate(halves(grad_values) + halves(neck_rows), axis=1)
        moved = nn(one_hot(down, places[:, step * STEP : (step + 1) * STEP]), pieces)
        moved = jnp.concatenate(
            [
                moved[:, :WIDTH] + moved[:, WIDTH : 2 * WIDTH],
                moved[:, 2 * WIDTH : 3 * WIDTH] + moved[:, 3 * WIDTH :],
            ],
            axis=1,
        )
        placed = moved if placed is None else placed + moved
    grad_head[...] = placed[:HEAD, :WIDTH]
    grad_rest[...] = placed[HEAD:row_count, :WIDTH]
    out_rows[...] = placed[:row_count, WIDTH:]
    edge[...] = placed[row_count : row_count + HALF]
    for block in range(3):
        joined[block * WIDTH : (block + 1) * WIDTH] = sum_qkv[:, block * WIDTH : (block + 1) * WIDTH]
    joined[3 * WIDTH :] = sum_out[...]
    units, part = sum_up.shape[0] // ffns, joined.shape[0] // ffns
    mine = ffn_index(ffns)
    for k, quarter in enumerate(quarters):
        number = mine ^ k
        rows = pl.ds(pl.multiple_of(number * units, units), units)
        quarter[:units] = sum_up[rows]
        quarter[units : 2 * units] = sum_down[rows]
        quarter[2 * units :] = joined[pl.ds(pl.multiple_of(number * part, part), part)]


def share_layer(shared, row, sums, ffns):
    sum_qkv, sum_out, sum_up, sum_down = sums
    devices = shared.shape[0]
    row = share_units(shared, row, sum_up, sum_down, ffns)
    for block in range(3):
        row = share_rows(shared, row, sum_qkv[:, block * WIDTH : (block + 1) * WIDTH], devices)
    return share_rows(shared, row, sum_out, devices)


def first_back_kernel(*refs, head, ffns):
    grad_ref, stats, gains, offsets, occupied_ref, lifted_ref, feats_ref = refs[:7]
    weights, keeps, refs = refs[7:15], refs[15:26], refs[26:]
    rows = slice(0, HEAD) if head else slice(HEAD, lifted_ref.shape[0])
    if head:
        edge, out_rows, small_second = refs[:3]
        held_sums, quarters = refs[3:10], refs[10 : 10 + ffns]
        pillars, grad_affine, shared = refs[10 + ffns : 13 + ffns]
        sums, grad, semaphores = refs[13 + ffns : 20 + ffns], *refs[20 + ffns :]
        for held, before in zip(sums, held_sums):
            held[...] = before[...]
        grad[...] = grad_ref[...]
        grad[:HALF] = edge[:, :WIDTH]
    else:
        grad_affine, sums = refs[0], refs[1:]
        for held in sums:
            held[...] = jnp.zeros(held.shape, F32)
        grad = grad_ref
    if head:
        copies = Copies(semaphores)
        copies.start(edge.at[:, WIDTH:], pillars.at[:HALF])
        copies.start(out_rows.at[HALF:], pillars.at[HALF:])
    small_ffn, sum_out, sum_up, sum_down, sum_qkv, sum_feats, small = sums
    joined, mixed = ffn_rows_back(
        0, grad[...], keeps[5:], (*weights[:4], *weights[6:8], gains, offsets), (small_ffn, sum_out, sum_up, sum_down)
    )
    vfe_slope, carried, packed_keep, high_keep, low_keep = keeps[:5]
    rows_grad = attention_rows_back(
        0,
        carried[...],
        live_column(occupied_ref)[rows],
        joined,
        mixed,
        (packed_keep, high_keep, low_keep),
        weights[4:6],
        sum_qkv,
    )
    rows_grad = rows_grad * vfe_slope[...]
    grad_affine[...] = rows_grad
    small[0:1] += column_sum(rows_grad * (lifted_ref[rows] - stats[1:2]) * stats[2:3])
    small[1:2] += column_sum(rows_grad)
    sum_feats[...] += product(tn, halves(feats_ref[rows]), halves(rows_grad))
    if head:
        devices = shared.shape[0]
        shared[...] = jnp.zeros(shared.shape, F32)
        quarter = quarters[0][...]
        for other in quarters[1:]:
            quarter = quarter + other[...]
        units = sum_up.shape[0] // ffns
        row = share_rows(shared, 0, quarter[: 2 * units], devices)
        row = share_rows(shared, row, quarter[2 * units :], devices)
        row = share_layer(shared, row, (sum_qkv, sum_out, sum_up, sum_down), ffns)
        row = share_rows(shared, row, small_second[...], devices)
        row = share_rows(shared, row, small_ffn[...], devices)
        row = share_rows(shared, row, sum_feats, devices)
        shared[:, row : row + 2] = jnp.broadcast_to(small[0:2][None], (devices, 2, WIDTH))
        for copy in copies.started:
            copy.wait()


def relay_kernel(
    arrived,
    hat_product,
    stats,
    bn_gain,
    affine_head,
    affine_rest,
    lifted_ref,
    occupied_ref,
    weight_ref,
    returned,
    vfe_grads,
    grad_feats,
    *,
    ffns,
    counts,
):
    unit_rows, quarter_rows, layer_rows, small_rows, part = counts
    devices = returned.shape[0]
    later = unit_rows + quarter_rows
    begin = later + ffns * unit_rows
    end = begin + layer_rows + small_rows
    total = jnp.sum(arrived[:, later:], axis=0)
    first_units, first_rest = total[: ffns * unit_rows], total[begin - later : end - later]
    tail = total[end - later :]
    blocks = []
    for f in range(ffns):
        block = arrived[f, :later]
        for device in range(f + ffns, devices, ffns):
            block = block + arrived[device, :later]
        blocks.append(block)
    gain, shift = tail[part : part + 1], tail[part + 1 : part + 2]
    lanes = lax.broadcasted_iota(jnp.int32, (part, WIDTH), 1)
    mine = lax.axis_index(AXES) * part + lax.broadcasted_iota(jnp.int32, (part, WIDTH), 0)
    live_sum = jnp.sum(jnp.where(lanes == mine, stats[3:4], 0.0), axis=1, keepdims=True)
    grad_w_vfe = stats[2:3] * bn_gain[0:1] * (
        tail[:part] - (hat_product[:part] * gain + live_sum * shift) / stats[0:1]
    )
    rows = jnp.concatenate([block[unit_rows:] for block in blocks] + [first_rest, grad_w_vfe], axis=0)
    room = returned.shape[1] - 2 * unit_rows
    if rows.shape[0] < room:
        rows = jnp.concatenate([rows, jnp.zeros((room - rows.shape[0], WIDTH), F32)], axis=0)
    returned[:, 2 * unit_rows :] = jnp.broadcast_to(rows[None], (devices,) + rows.shape)
    for device in range(devices):
        f = device % ffns
        returned[device, :unit_rows] = blocks[f][:unit_rows]
        returned[device, unit_rows : 2 * unit_rows] = first_units[f * unit_rows : (f + 1) * unit_rows]
    vfe_grads[...] = jnp.concatenate([gain, shift, jnp.zeros((6, WIDTH), F32)], axis=0)
    hat = (lifted_ref[...] - stats[1:2]) * stats[2:3]
    grad = jnp.concatenate([affine_head[...], affine_rest[...]], axis=0)
    grad = grad - live_column(occupied_ref) * (hat * gain + shift) / stats[0:1]
    grad = stats[2:3] * bn_gain[0:1] * grad
    grad_feats[...] = product(nt, halves(grad), halves(weight_ref[...]))


def last_kernel(
    returned,
    vfe_grads,
    neck,
    grad_w_vfe,
    grad_bn_gain,
    grad_bn_shift,
    grad_w_qkv,
    grad_w_out,
    grad_w_in,
    grad_b_in,
    grad_w_back,
    grad_b_back,
    grad_ln_gain,
    grad_ln_shift,
    *,
    ffns,
):
    devices = returned.shape[0]
    units = grad_w_in.shape[1]
    part = share_of(WIDTH, devices)
    unit_rows = share_of(2 * units, devices)
    at = 0

    def take(count):
        nonlocal at
        rows = joined_rows(returned, at, count)
        at += share_of(count, devices)
        return rows

    blocks = [take(2 * units) for layer in range(2)]
    mine = lax.rem(lax.axis_index(AXES), ffns)
    for layer in (1, 0):
        grad_w_in[layer] = blocks[1 - layer][:units]
        grad_w_back[layer] = blocks[1 - layer][units:]
        if layer:
            rows = jnp.concatenate([take(4 * WIDTH // ffns) for f in range(ffns)], axis=0)
        else:
            rows = jnp.concatenate([take(WIDTH) for block in range(4)], axis=0)
        for block in range(3):
            grad_w_qkv[layer, :, block * WIDTH : (block + 1) * WIDTH] = rows[block * WIDTH : (block + 1) * WIDTH]
        grad_w_out[layer] = rows[3 * WIDTH :]
    for layer in (1, 0):
        small = take(8)
        grad_b_back[layer : layer + 1] = small[0:1]
        grad_ln_gain[2 * layer : 2 * layer + 1] = small[1:2]
        grad_ln_shift[2 * layer : 2 * layer + 1] = small[2:3]
        grad_ln_gain[2 * layer + 1 : 2 * layer + 2] = small[3:4]
        grad_ln_shift[2 * layer + 1 : 2 * layer + 2] = small[4:5]
        held = jnp.zeros((1, units), F32)
        for f in range(ffns):
            row, lane = divmod(f * units, WIDTH)
            held = jnp.where(mine == f, small[5 + row : 6 + row, lane : lane + units], held)
        grad_b_in[layer : layer + 1] = held
    grad_w_vfe[...] = take(WIDTH)
    grad_bn_gain[0:1] = vfe_grads[0:1]
    grad_bn_gain[1:2] = neck[0:1]
    grad_bn_shift[0:1] = vfe_grads[1:2]
    grad_bn_shift[1:2] = neck[1:2]


def spread_rows(pieces, axes):
    return lax.all_to_all(pieces, axes, 0, 0)


def partner(rows, k):
    return lax.ppermute(rows, "ffn", [(i, i ^ k) for i in range(lax.axis_size("ffn"))])


def passed_along(rows, by):
    peers = lax.axis_size(AXES)
    return lax.ppermute(rows, AXES, [(i, (i + by) % peers) for i in range(peers)])


def on_device(
    pillar_feats,
    occupied,
    shifted_source_rows,
    w_vfe,
    bn_gain,
    bn_shift,
    query_key_value_weight,
    attention_output_weight,
    up_weight_matrix,
    up_bias_rows,
    down_weight_matrix,
    down_bias_rows,
    layernorm_gains,
    layernorm_offsets,
    cotangent,
):
    row_count = pillar_feats.shape[0]
    spread = row_count + -(-HALF // 16) * 16
    ffns = lax.axis_size("ffn")
    devices = lax.axis_size(AXES)
    units = up_weight_matrix.shape[2]
    hidden = units * ffns
    windows = row_count // CELLS
    part = share_of(WIDTH, devices)
    piece = share_of(2 * units, devices)
    rest = 4 * part + 2 * share_of(8, devices)
    stats_rows = -(-(4 + part) // 8) * 8
    quarter_part = share_of(4 * WIDTH // ffns, devices)
    shared_rows = -(-((1 + ffns) * piece + quarter_part + rest + part + 2) // 8) * 8
    returned_rows = -(-(2 * piece + ffns * quarter_part + rest + part) // 8) * 8
    rows_shape = shape(row_count, WIDTH)
    rest_rows = row_count - HEAD

    def keeps(make, rows):
        weights = make(rows // CELLS, CELLS, HEADS * CELLS, dtype=BF16)
        plain, wide = make(rows, WIDTH), make(rows, hidden)
        return [plain, make(rows, 3 * WIDTH), weights, weights, plain, plain, wide, wide, plain, plain]

    lifted, sent, packed = run(
        vfe_kernel,
        "vfe",
        (rows_shape, shape(devices, stats_rows, WIDTH), shape(4 * units + 8, WIDTH)),
        (
            pillar_feats,
            w_vfe,
            occupied,
            up_weight_matrix.transpose(0, 2, 1),
            down_weight_matrix,
            up_bias_rows,
        ),
    )
    seen = spread_rows(sent, AXES)
    packed = lax.all_gather(packed, "ffn", axis=0, tiled=False)
    weight_dims = (
        [(2, hidden, WIDTH, BF16)] * 4
        + [(2, hidden, F32)]
        + [(2, WIDTH, 3 * WIDTH, BF16)] * 2
        + [(2, WIDTH, WIDTH, BF16)] * 2
    )
    norms = pinned((down_bias_rows, layernorm_gains, layernorm_offsets))
    bn_pair = pinned((bn_gain, bn_shift))
    head_arrays = [kept(HEAD, WIDTH)] * 2 + keeps(kept, HEAD)
    rest_arrays = [kept(rest_rows, WIDTH)] * 2 + keeps(kept, rest_rows)
    outs = run(
        functools.partial(first_kernel, head=True),
        "first",
        [kept(*dims[:-1], dtype=dims[-1]) for dims in weight_dims]
        + [kept(8, WIDTH), kept(8, WIDTH), kept(HALF, 3 * WIDTH)]
        + head_arrays,
        (
            lifted,
            occupied,
            bn_gain,
            bn_shift,
            down_bias_rows,
            layernorm_gains,
            layernorm_offsets,
            Pinned(seen),
            packed,
            query_key_value_weight,
            attention_output_weight,
            Far(cotangent),
        ),
        scratch=[pltpu.VMEM((HALF, WIDTH), F32)],
        copies=1,
        flops=1e9,
    )
    weights, (stats, hat_product, edge) = outs[:9], outs[9:12]
    first_head, *head_keep = outs[12:]
    layer_weights = pinned(weights) + norms
    back_weights = pinned(weights[:4] + weights[5:]) + norms[1:]
    edge = passed_along(edge, -1)
    first_rest, *rest_keep = run(
        functools.partial(first_kernel, head=False),
        "first_rest",
        rest_arrays,
        (Pinned(lifted), Pinned(occupied), *bn_pair, *norms, Pinned(stats), *pinned(weights)),
        flops=1e9,
    )
    sent, *second_keep = run(
        second_kernel,
        "second",
        [kept(devices, 8, WIDTH), kept(row_count, WIDTH), kept(row_count, 1), kept(row_count, WIDTH)]
        + [kept(row_count, WIDTH)]
        + keeps(kept, row_count)[1:],
        (
            Pinned(first_head),
            Pinned(first_rest),
            Pinned(cotangent),
            Pinned(occupied),
            Pinned(edge),
            Pinned(shifted_source_rows),
            *layer_weights,
        ),
        scratch=[pltpu.VMEM((spread, 5 * WIDTH), BF16), pltpu.VMEM((8, WIDTH), F32)],
        flops=2e9,
    )
    seen = spread_rows(sent, AXES)
    sum_shapes = [
        pltpu.VMEM((8, WIDTH), F32),
        pltpu.VMEM((WIDTH, WIDTH), F32),
        pltpu.VMEM((hidden, WIDTH), F32),
        pltpu.VMEM((hidden, WIDTH), F32),
    ]
    sum_qkv = pltpu.VMEM((WIDTH, 3 * WIDTH), F32)
    edge, grad_head, grad_rest, out_rows, neck, small, *quarters = run(
        functools.partial(second_back_kernel, ffns=ffns),
        "second_back",
        [
            kept(HALF, 2 * WIDTH),
            kept(HEAD, WIDTH),
            kept(rest_rows, WIDTH),
            kept(row_count, WIDTH),
            kept(8, WIDTH),
            kept(8, WIDTH),
        ]
        + [kept(2 * units + 4 * WIDTH // ffns, WIDTH)] * ffns,
        (Pinned(seen), *bn_pair, Pinned(shifted_source_rows), *back_weights, *pinned(second_keep)),
        scratch=[sum_qkv] + sum_shapes[1:] + [pltpu.VMEM((4 * WIDTH, WIDTH), F32)],
        flops=4e9,
    )
    edge = passed_along(edge, 1)
    quarters = [quarters[0]] + [partner(quarters[k], k) for k in range(1, ffns)]
    sums = sum_shapes + [sum_qkv, pltpu.VMEM((WIDTH, WIDTH), F32), pltpu.VMEM((8, WIDTH), F32)]
    first_back_args = (stats, layernorm_gains, layernorm_offsets, occupied, lifted, pillar_feats, *weights[:4], *weights[5:])
    affine_rest, *held_sums = run(
        functools.partial(first_back_kernel, head=False, ffns=ffns),
        "first_back",
        [kept(rest_rows, WIDTH)] + sums,
        pinned((grad_rest, *first_back_args, *rest_keep)),
        flops=3e9,
    )
    pillars_out, affine_head, shared = run(
        functools.partial(first_back_kernel, head=True, ffns=ffns),
        "first_back_edge",
        [Far(rows_shape), kept(HEAD, WIDTH), kept(devices, shared_rows, WIDTH)],
        pinned((grad_head, *first_back_args, *head_keep, edge, out_rows, small, *held_sums, *quarters)),
        scratch=sums + [pltpu.VMEM((HEAD, WIDTH), F32)],
        copies=2,
        flops=3e9,
    )
    arrived = spread_rows(shared, AXES)
    returned, vfe_grads, grad_feats = run(
        functools.partial(relay_kernel, ffns=ffns, counts=(piece, quarter_part, 4 * part, rest - 4 * part, part)),
        "relay",
        (kept(devices, returned_rows, WIDTH), kept(8, WIDTH), rows_shape),
        pinned((arrived, hat_product, stats, bn_gain, affine_head, affine_rest, lifted, occupied, w_vfe)),
    )
    returned = spread_rows(returned, AXES)
    grads = list(run(
        functools.partial(last_kernel, ffns=ffns),
        "last",
        (
            shape(WIDTH, WIDTH),
            shape(2, WIDTH),
            shape(2, WIDTH),
            shape(2, WIDTH, 3 * WIDTH),
            shape(2, WIDTH, WIDTH),
            shape(2, units, WIDTH),
            shape(2, units),
            shape(2, units, WIDTH),
            shape(2, WIDTH),
            shape(4, WIDTH),
            shape(4, WIDTH),
        ),
        pinned((returned, vfe_grads, neck)),
    ))
    grads[5] = grads[5].transpose(0, 2, 1)
    return (pillars_out, grad_feats, *grads)


def solution(mesh):
    return jax.shard_map(
        on_device,
        mesh=mesh,
        in_specs=(
            P(("win", "ffn"), None),
            P(("win", "ffn")),
            P(("win", "ffn")),
            P(),
            P(),
            P(),
            P(),
            P(),
            P(None, None, "ffn"),
            P(None, "ffn"),
            P(None, "ffn", None),
            P(),
            P(),
            P(),
            P(("win", "ffn"), None),
        ),
        out_specs=(
            P(("win", "ffn"), None),
            P(("win", "ffn"), None),
            P(),
            P(),
            P(),
            P(),
            P(),
            P(None, None, "ffn"),
            P(None, "ffn"),
            P(None, "ffn", None),
            P(),
            P(),
            P(),
        ),
        check_vma=False,
    )
```

```python
import functools

import jax
import jax.numpy as jnp
from jax import lax
from jax.experimental import pallas as pl
from jax.experimental.pallas import tpu as pltpu
from jax.sharding import PartitionSpec as P

HEADS = 8
CELLS = 144
HALF = CELLS // 2
WIDTH = 128
EPS_NORM = 1e-05
NEG_FILL = -1000000000.0
AXES = ("win", "ffn")
STEP = 3 * CELLS
HEAD = 2 * CELLS
TILE_ROWS = WIDTH // HEADS
TILES = CELLS // TILE_ROWS
CHUNKS = ((0, 2), (2, 4), (4, 6), (6, 8), (8, 9))
F32 = jnp.float32
BF16 = jnp.bfloat16
VMEM_LIMIT = 28 * 1024 * 1024


def shape(*dims, dtype=F32):
    return pltpu.HBM(dims, dtype)


def kept(*dims, dtype=F32):
    return pltpu.VMEM(dims, dtype)


class Pinned:
    def __init__(self, value):
        self.value = value


class Far:
    def __init__(self, value):
        self.value = value


def run(kernel, name, outs, args, scratch=(), copies=0, aliases=None, flops=1e8):
    near, far = pl.BlockSpec(memory_space=pltpu.VMEM), pl.BlockSpec(memory_space=pltpu.HBM)
    values = []
    for arg in args:
        space = pltpu.VMEM if isinstance(arg, Pinned) else pltpu.HBM
        value = arg.value if isinstance(arg, (Pinned, Far)) else arg
        values.append(pltpu.with_memory_space_constraint(value, space))
    scratch = list(scratch)
    if copies:
        scratch.append(pltpu.SemaphoreType.DMA((copies,)))
    return pl.pallas_call(
        kernel,
        out_shape=[out.value if isinstance(out, Far) else out for out in outs],
        in_specs=[far if isinstance(arg, Far) else near for arg in args],
        out_specs=[far if isinstance(out, Far) else near for out in outs],
        scratch_shapes=scratch,
        input_output_aliases=aliases or {},
        compiler_params=pltpu.CompilerParams(vmem_limit_bytes=VMEM_LIMIT),
        cost_estimate=pl.CostEstimate(flops=int(flops), bytes_accessed=1000000, transcendentals=0),
        name=name,
    )(*values)


def pinned(values):
    return [Pinned(value) for value in values]


class Copies:
    def __init__(self, semaphores):
        self.semaphores = semaphores
        self.started = []

    def start(self, source, target):
        copy = pltpu.make_async_copy(source, target, self.semaphores.at[len(self.started)])
        copy.start()
        self.started.append(copy)
        return copy


def scratch_like(arrays):
    return [pltpu.VMEM(array.shape, array.dtype) for array in arrays]


def ffn_index(ffns):
    return lax.rem(lax.axis_index(AXES), ffns)


def share_of(rows, devices):
    return -(-rows // devices)


def halves(values):
    high = values.astype(BF16)
    return high, (values - high.astype(F32)).astype(BF16)


def nn(former, latter):
    return lax.dot_general(former, latter, (((1,), (0,)), ((), ())), preferred_element_type=F32)


def nt(former, latter):
    return lax.dot_general(former, latter, (((1,), (1,)), ((), ())), preferred_element_type=F32)


def tn(former, latter):
    return lax.dot_general(former, latter, (((0,), (0,)), ((), ())), preferred_element_type=F32)


def product(kind, former, latter):
    columns = latter[0].shape[0 if kind is nt else 1]
    if columns == WIDTH:
        both = kind(former[0], jnp.concatenate(latter, axis=0 if kind is nt else 1))
        return both[:, :columns] + (both[:, columns:] + kind(former[1], latter[0]))
    if kind is tn:
        rows = former[0].shape[1]
        both = kind(jnp.concatenate(former, axis=1), latter[0])
        return both[:rows] + (both[rows:] + kind(former[0], latter[1]))
    if former[0].shape[1] == WIDTH:
        twice = jnp.concatenate([latter[0]] * 2, axis=1 if kind is nt else 0)
        return kind(jnp.concatenate(former, axis=1), twice) + kind(former[0], latter[1])
    return kind(former[0], latter[0]) + (kind(former[0], latter[1]) + kind(former[1], latter[0]))


def gelu_parts(values):
    below = 0.5 * (1.0 + lax.erf(values * 0.7071067811865476))
    density = 0.3989422804014327 * jnp.exp(-0.5 * values * values)
    return values * below, below + values * density


def normed_rows(values):
    center = jnp.mean(values, axis=-1, keepdims=True)
    moved = values - center
    rate = lax.rsqrt(jnp.mean(moved * moved, axis=-1, keepdims=True) + EPS_NORM)
    return moved * rate, rate


def normed_back(grad, hat, rate, gain):
    scaled = grad * gain
    first = jnp.mean(scaled, axis=-1, keepdims=True)
    second = jnp.mean(scaled * hat, axis=-1, keepdims=True)
    return rate * (scaled - first - hat * second)


def live_column(occupied_ref):
    row = occupied_ref[...].astype(F32).reshape(1, occupied_ref.shape[0])
    return jnp.broadcast_to(row, (8, row.shape[1])).T[:, :1]


def column_sum(values):
    return jnp.sum(values, axis=0, keepdims=True)


def head_mask():
    dims = (HEADS, TILE_ROWS, WIDTH)
    lane_head = lax.broadcasted_iota(jnp.int32, dims, 2) // TILE_ROWS
    return (lane_head == lax.broadcasted_iota(jnp.int32, dims, 0)).astype(F32)


def per_head(rows, mask):
    count = rows.shape[0] // TILE_ROWS
    return (rows.reshape(count, 1, TILE_ROWS, WIDTH) * mask[None]).reshape(count * WIDTH, WIDTH)


def from_heads(table, mask):
    parts = []
    for at in range(0, table.shape[1], WIDTH):
        turned = table[:, at : at + WIDTH].T.reshape(HEADS, TILE_ROWS, WIDTH)
        parts.append(jnp.sum(turned * mask, axis=0))
    return parts


def high_and_low(values):
    high, low = halves(values.T)
    return jnp.concatenate([high, low], axis=0), high


def stacked_product(stack, high_alone, weights):
    both = nn(stack, weights[0])
    return both[:WIDTH] + (both[WIDTH:] + nn(high_alone, weights[1]))


def window_mix(query, key, value, live, mask, mask_low, keep_high, keep_low):
    query_high, query_low = halves(query)
    key_high, key_low = halves(key)
    key_stack = jnp.concatenate([key_high, key_low, key_high], axis=1)
    turned = high_and_low(value)
    mixed = []
    for first, last in CHUNKS:
        rows = slice(first * TILE_ROWS, last * TILE_ROWS)
        lanes = slice(first * WIDTH, last * WIDTH)
        high = per_head(query_high[rows], mask_low)
        low = per_head(query_low[rows], mask_low)
        scores = nt(key_stack, jnp.concatenate([high, high, low], axis=1))
        scores = jnp.where(live > 0, scores, NEG_FILL)
        weights = jnp.exp(scores - jnp.max(scores, axis=0, keepdims=True))
        weights = weights * (1.0 / column_sum(weights))
        weights = halves(weights)
        keep_high[:, lanes] = weights[0]
        keep_low[:, lanes] = weights[1]
        mixed += from_heads(stacked_product(*turned, weights), mask)
    return jnp.concatenate(mixed, axis=0)


def window_back(query, key, value, grad_mixed, live, mask, mask_low, high, low):
    query_high, query_low = (per_head(part, mask_low) for part in halves(query))
    grad_high, grad_low = (per_head(part, mask_low) for part in halves(grad_mixed))
    value_high, value_low = halves(value)
    value_stack = jnp.concatenate([value_high, value_low, value_high], axis=1)
    grad_weights = nt(value_stack, jnp.concatenate([grad_high, grad_high, grad_low], axis=1))
    weights = high.astype(F32) + low.astype(F32)
    grad_scores = weights * grad_weights
    grad_scores = live * (grad_scores - weights * column_sum(grad_scores))
    scores_high, scores_low = halves(grad_scores)

    def over_queries(upper, lower, high, low):
        both = nn(
            jnp.concatenate([upper, lower], axis=0), jnp.concatenate([high, low], axis=1)
        )
        return both[:CELLS, :WIDTH] + (both[:CELLS, WIDTH:] + both[CELLS:, :WIDTH])

    grad_query = stacked_product(*high_and_low(key), (scores_high, scores_low))
    return (
        0.25 * jnp.concatenate(from_heads(grad_query, mask), axis=0),
        over_queries(scores_high, scores_low, query_high, query_low),
        over_queries(high, low, grad_high, grad_low),
    )


def unpack(packed, qkv_ref, out_ref, up_high, up_low, down_high, down_low, bias, qkv_high, qkv_low, out_high, out_low):
    ffns = packed.shape[0]
    units = bias.shape[1] // ffns
    for one in range(2):
        for at in range(ffns):
            rows = slice(at * units, (at + 1) * units)
            high, low = halves(packed[at, one * units : (one + 1) * units])
            up_high[one, rows], up_low[one, rows] = high, low
            high, low = halves(packed[at, (2 + one) * units : (3 + one) * units])
            down_high[one, rows], down_low[one, rows] = high, low
        bias[one : one + 1] = jnp.concatenate(
            [packed[at, 4 * units + one : 4 * units + one + 1, :units] for at in range(ffns)], axis=1
        )
    qkv_high[...], qkv_low[...] = halves(qkv_ref[...])
    out_high[...], out_low[...] = halves(out_ref[...])


def layer_rows(one, values, live, weights, saved):
    up_high, up_low, down_high, down_low, bias, qkv_high, qkv_low, out_high, out_low, back_bias, gains, offsets = weights
    packed_keep, high_keep, low_keep, mixed_keep, hat_one, hidden_keep, slope, hat_two, rates = saved
    mask = head_mask()
    mask_low = mask.astype(BF16)
    qkv = product(nn, halves(values), (qkv_high[one], qkv_low[one]))
    query = 0.25 * qkv[:, :WIDTH]
    packed_keep[:, :WIDTH] = query
    packed_keep[:, WIDTH:] = qkv[:, WIDTH:]
    for at in range(values.shape[0] // CELLS):
        rows = slice(at * CELLS, (at + 1) * CELLS)
        mixed_keep[rows] = window_mix(
            query[rows],
            qkv[rows, WIDTH : 2 * WIDTH],
            qkv[rows, 2 * WIDTH :],
            live[rows],
            mask,
            mask_low,
            high_keep.at[at],
            low_keep.at[at],
        )
    mixed = mixed_keep[...]
    hat, rate = normed_rows(
        values + product(nn, halves(mixed), (out_high[one], out_low[one]))
    )
    hat_one[...] = hat
    first = hat * gains[2 * one : 2 * one + 1] + offsets[2 * one : 2 * one + 1]
    hidden, steep = gelu_parts(
        product(nt, halves(first), (up_high[one], up_low[one])) + bias[one : one + 1]
    )
    hidden_keep[...] = hidden
    slope[...] = steep
    summed = first + product(nn, halves(hidden), (down_high[one], down_low[one])) + back_bias[one : one + 1]
    hat, last_rate = normed_rows(summed)
    hat_two[...] = hat
    lanes = lax.broadcasted_iota(jnp.int32, hat.shape, 1)
    rates[...] = jnp.where(lanes < WIDTH // 2, rate, last_rate)
    return hat * gains[2 * one + 1 : 2 * one + 2] + offsets[2 * one + 1 : 2 * one + 2]


def ffn_rows_back(one, grad, saved, weights, small):
    mixed_keep, hat_one, hidden_keep, slope, hat_two, rates = saved
    up_high, up_low, down_high, down_low, out_high, out_low, gains, offsets = weights
    up, down, out = (up_high[one], up_low[one]), (down_high[one], down_low[one]), (out_high[one], out_low[one])
    hat = hat_two[...]
    grad_summed = normed_back(grad, hat, rates[:, WIDTH - 1 :], gains[2 * one + 1 : 2 * one + 2])
    small[3:4] += column_sum(grad * hat)
    small[4:5] += column_sum(grad)
    small[0:1] += column_sum(grad_summed)
    summed_halves = halves(grad_summed)
    grad_pre = product(nt, summed_halves, down) * slope[...]
    pre_halves = halves(grad_pre)
    hat = hat_one[...]
    bias_sum = column_sum(grad_pre)
    for at in range(bias_sum.shape[1] // WIDTH):
        small[5 + at : 6 + at] += bias_sum[:, at * WIDTH : (at + 1) * WIDTH]
    grad_first = grad_summed + product(nn, pre_halves, up)
    small[1:2] += column_sum(grad_first * hat)
    small[2:3] += column_sum(grad_first)
    grad_joined = normed_back(grad_first, hat, rates[:, 0:1], gains[2 * one : 2 * one + 1])
    joined_halves = halves(grad_joined)
    return grad_joined, product(nt, joined_halves, out), (summed_halves, pre_halves, joined_halves)


def ffn_weights_back(one, saved, norms, parts):
    mixed_keep, hat_one, hidden_keep = saved
    gains, offsets = norms
    summed_halves, pre_halves, joined_halves = parts
    first = hat_one[...] * gains[2 * one : 2 * one + 1] + offsets[2 * one : 2 * one + 1]
    return (
        product(tn, halves(mixed_keep[...]), joined_halves),
        product(tn, pre_halves, halves(first)),
        product(tn, halves(hidden_keep[...]), summed_halves),
    )


def attention_rows_back(one, live, grad_joined, grad_mixed, saved, qkv_weights):
    packed_keep, high_keep, low_keep = saved
    mask = head_mask()
    mask_low = mask.astype(BF16)
    parts = []
    for at in range(grad_joined.shape[0] // CELLS):
        rows = slice(at * CELLS, (at + 1) * CELLS)
        parts.append(
            window_back(
                packed_keep[rows, :WIDTH],
                packed_keep[rows, WIDTH : 2 * WIDTH],
                packed_keep[rows, 2 * WIDTH :],
                grad_mixed[rows],
                live[rows],
                mask,
                mask_low,
                high_keep[at],
                low_keep[at],
            )
        )
    grad_packed = halves(
        jnp.concatenate([jnp.concatenate(part, axis=1) for part in parts], axis=0)
    )
    return grad_joined + product(nt, grad_packed, (qkv_weights[0][one], qkv_weights[1][one])), grad_packed


def share_rows(target, at, values, devices):
    count = values.shape[0]
    share = share_of(count, devices)
    for device in range(devices):
        begin = device * share
        if begin < count:
            held = min(share, count - begin)
            target[device, at : at + held] = values[begin : begin + held]
    return at + share


def joined_rows(table, at, count):
    devices = table.shape[0]
    share = share_of(count, devices)
    if share % 8 == 0 and share * devices == count:
        return table[:, at : at + share].reshape(count, WIDTH)
    pieces = []
    for device in range(devices):
        begin = device * share
        if begin < count:
            pieces.append(table[device, at : at + min(share, count - begin)])
    return jnp.concatenate(pieces, axis=0)


def vfe_kernel(
    feats_ref, weight_ref, occupied_ref, up_ref, down_ref, bias_ref, lifted_ref, sent_ref, packed_ref
):
    devices = sent_ref.shape[0]
    units = up_ref.shape[1]
    feats = feats_ref[...]
    feats_halves = halves(feats)
    lifted = product(nn, feats_halves, halves(weight_ref[...]))
    lifted_ref[...] = lifted
    live = live_column(occupied_ref)
    count = jnp.sum(live, axis=0, keepdims=True)
    total = column_sum(live * lifted)
    moved = live * (lifted - total / jnp.maximum(count, 1.0))
    sent_ref[...] = jnp.zeros(sent_ref.shape, F32)
    stats = jnp.concatenate(
        [
            jnp.broadcast_to(count, (1, WIDTH)),
            total,
            column_sum(moved * moved),
            column_sum(live * feats),
        ],
        axis=0,
    )
    sent_ref[:, 0:4] = jnp.broadcast_to(stats[None], (devices, 4, WIDTH))
    share_rows(sent_ref, 4, product(tn, feats_halves, halves(moved)), devices)
    for one in range(2):
        packed_ref[one * units : (one + 1) * units] = up_ref[one]
        packed_ref[(2 + one) * units : (3 + one) * units] = down_ref[one]
    packed_ref[4 * units :] = jnp.zeros((8, WIDTH), F32)
    packed_ref[4 * units : 4 * units + 2, :units] = bias_ref[...]


def places_of(source_ref):
    row_count = source_ref.shape[0]
    places = source_ref[...].reshape(1, row_count) - lax.axis_index(AXES) * row_count
    return jnp.where(places < 0, places + row_count * lax.axis_size(AXES), places)


def one_hot(former, latter):
    return (former == latter).astype(F32).astype(BF16)


def vfe_stats(seen_ref, stats_ref, product_ref):
    counts, totals, squares, lives = (seen_ref[:, at] for at in range(4))
    count = column_sum(counts)
    center = column_sum(totals) / count
    moves = totals / jnp.maximum(counts, 1.0) - center
    rate = lax.rsqrt(column_sum(squares + counts * moves * moves) / count + EPS_NORM)
    stats_ref[...] = jnp.zeros(stats_ref.shape, F32)
    stats_ref[0:1] = count
    stats_ref[1:2] = center
    stats_ref[2:3] = rate
    stats_ref[3:4] = column_sum(lives)
    devices = seen_ref.shape[0]
    share = share_of(WIDTH, devices)
    mine = lax.axis_index(AXES) * share
    lanes = lax.broadcasted_iota(jnp.int32, lives.shape, 1)
    product_ref[...] = jnp.zeros(product_ref.shape, F32)
    for at in range(share):
        picked = jnp.sum(jnp.where(lanes == mine + at, lives, 0.0), axis=1, keepdims=True)
        product_ref[at : at + 1] = rate * column_sum(seen_ref[:, 4 + at] + picked * moves)


def rows_in(refs, begin, end):
    return [
        ref.at[begin // CELLS : end // CELLS] if len(ref.shape) == 3 else ref.at[begin:end]
        for ref in refs
    ]


def step_of(refs, step):
    return rows_in(refs, step * STEP, (step + 1) * STEP)


def first_kernel(*refs, head):
    lifted_ref, occupied_ref, bn_gain, bn_shift, back_bias, gains, offsets = refs[:7]
    if head:
        seen_ref, packed, qkv_ref, out_ref, cotangent_ref = refs[7:12]
        weights = refs[12:21]
        stats, hat_product, edge = refs[21:24]
        arrays = refs[24:36]
        cotangent, semaphores = refs[36:]
        copies = Copies(semaphores)
        arrival = copies.start(cotangent_ref.at[:HALF], cotangent)
        unpack(packed, qkv_ref, out_ref, *weights)
        vfe_stats(seen_ref, stats, hat_product)
        rows = slice(0, HEAD)
    else:
        stats = refs[7]
        weights = refs[8:17]
        arrays = refs[17 + (len(refs) - 17) // 2 :]
        rows = slice(HEAD, lifted_ref.shape[0])
    result, vfe_slope, carried, *saved = rows_in(arrays, rows.start, rows.stop)
    hat = (lifted_ref[rows] - stats[1:2]) * stats[2:3]
    values, steep = gelu_parts(hat * bn_gain[0:1] + bn_shift[0:1])
    vfe_slope[...] = steep
    carried[...] = values
    live = live_column(occupied_ref)[rows]
    rows = layer_rows(0, values, live, (*weights, back_bias, gains, offsets), saved)
    result[...] = rows
    if head:
        arrival.wait()
        edge[:, :WIDTH] = rows[:HALF]
        edge[:, WIDTH : 2 * WIDTH] = cotangent[...]
        edge[:, 2 * WIDTH :] = jnp.broadcast_to(live[:HALF], (HALF, WIDTH))


def second_kernel(first_ref, cotangent_ref, occupied_ref, edge, source_ref, *refs):
    weights = refs[:12]
    sent = refs[12]
    arrays = refs[13:-2]
    table, sums = refs[-2:]
    row_count = cotangent_ref.shape[0]
    high, low = halves(first_ref[...])
    table[:row_count, :WIDTH] = high
    table[:row_count, WIDTH : 2 * WIDTH] = low
    high, low = halves(cotangent_ref[...])
    table[:row_count, 2 * WIDTH : 3 * WIDTH] = high
    table[:row_count, 3 * WIDTH : 4 * WIDTH] = low
    table[:row_count, 4 * WIDTH :] = jnp.broadcast_to(live_column(occupied_ref), (row_count, WIDTH)).astype(BF16)
    spare = table.shape[0] - row_count
    tail = jnp.concatenate([edge[...], jnp.zeros((spare - HALF, 3 * WIDTH), F32)], axis=0)
    high, low = halves(tail)
    table[row_count:, :WIDTH] = high[:, :WIDTH]
    table[row_count:, WIDTH : 2 * WIDTH] = low[:, :WIDTH]
    table[row_count:, 2 * WIDTH : 3 * WIDTH] = high[:, WIDTH : 2 * WIDTH]
    table[row_count:, 3 * WIDTH : 4 * WIDTH] = low[:, WIDTH : 2 * WIDTH]
    table[row_count:, 4 * WIDTH :] = high[:, 2 * WIDTH :]
    places = jnp.broadcast_to(places_of(source_ref).astype(F32), (8, row_count))
    column = places.T[:, :1].astype(jnp.int32)
    lanes = lax.broadcasted_iota(jnp.int32, (STEP, table.shape[0]), 1)
    for step in range(row_count // STEP):
        result, live_keep, cotangent_keep, carried, *saved = step_of(arrays, step)
        gathered = nn(one_hot(lanes, column[step * STEP : (step + 1) * STEP]), table[...])
        values = gathered[:, :WIDTH] + gathered[:, WIDTH : 2 * WIDTH]
        live = gathered[:, 4 * WIDTH :]
        grad = live * (gathered[:, 2 * WIDTH : 3 * WIDTH] + gathered[:, 3 * WIDTH : 4 * WIDTH])
        carried[...] = values
        cotangent_keep[...] = grad
        live_keep[...] = live[:, :1]
        rows = layer_rows(1, values, live[:, :1], weights, saved)
        result[...] = rows
        count = column_sum(live)
        if step == 0:
            sums[...] = jnp.zeros(sums.shape, F32)
            sums[5:6] = column_sum(live * rows) / jnp.maximum(count, 1.0)
        moved = rows - sums[5:6]
        sums[0:1] += count
        sums[1:2] += column_sum(live * moved)
        sums[2:3] += column_sum(live * moved * moved)
        sums[3:4] += column_sum(grad)
        sums[4:5] += column_sum(grad * moved)
    count = sums[0:1]
    move = sums[1:2] / jnp.maximum(count, 1.0)
    stats = jnp.concatenate(
        [
            count,
            sums[5:6] + move,
            sums[2:3] - count * move * move,
            sums[3:4],
            sums[4:5] - move * sums[3:4],
            jnp.zeros((3, WIDTH), F32),
        ],
        axis=0,
    )
    sent[...] = jnp.broadcast_to(stats[None], sent.shape)


def second_back_kernel(seen_ref, bn_gain, bn_shift, source_ref, *refs):
    weights = refs[:10]
    arrays = refs[10:23]
    edge, grad_rows, out_rows, neck, small, summed_keep, pre_keep, joined_keep, packed_back = refs[23:]
    row_count = out_rows.shape[0]
    counts, means, squares, grads, products = (seen_ref[:, row] for row in range(5))
    count = column_sum(counts)
    center = column_sum(counts * means) / count
    moves = means - center
    rate = lax.rsqrt(column_sum(squares + counts * moves * moves) / count + EPS_NORM)
    gain_grad = rate * column_sum(products + moves * grads)
    shift_grad = column_sum(grads)
    neck[...] = jnp.concatenate([gain_grad, shift_grad, jnp.zeros((6, WIDTH), F32)], axis=0)
    small[...] = jnp.zeros(small.shape, F32)
    places = places_of(source_ref)
    down = lax.broadcasted_iota(jnp.int32, (-(-(row_count + HALF) // 8) * 8, STEP), 0)
    placed = None
    for step in range(row_count // STEP):
        rows = slice(step * STEP, (step + 1) * STEP)
        result, live_keep, cotangent_keep, carried, packed_keep, high_keep, low_keep, *keeps = step_of(arrays, step)
        live = live_keep[...]
        hat = (result[...] - center) * rate
        neck_rows = live * (hat * bn_gain[1:2] + bn_shift[1:2])
        grad = rate * bn_gain[1:2] * (
            cotangent_keep[...] - live * (hat * gain_grad + shift_grad) / count
        )
        grad_joined, grad_mixed, parts = ffn_rows_back(1, grad, keeps, weights[:4] + weights[6:10], small)
        grad_values, grad_packed = attention_rows_back(
            1, live, grad_joined, grad_mixed, (packed_keep, high_keep, low_keep), weights[4:6]
        )
        for kept_halves, part in zip((summed_keep, pre_keep, joined_keep, packed_back), (*parts, grad_packed)):
            kept_halves[rows] = jnp.concatenate(part, axis=1)
        pieces = jnp.concatenate(halves(grad_values) + halves(neck_rows), axis=1)
        moved = nn(one_hot(down, places[:, rows]), pieces)
        moved = jnp.concatenate(
            [
                moved[:, :WIDTH] + moved[:, WIDTH : 2 * WIDTH],
                moved[:, 2 * WIDTH : 3 * WIDTH] + moved[:, 3 * WIDTH :],
            ],
            axis=1,
        )
        placed = moved if placed is None else placed + moved
    grad_rows[...] = placed[:row_count, :WIDTH]
    out_rows[...] = placed[:row_count, WIDTH:]
    edge[...] = placed[row_count : row_count + HALF]


def quarter_rows(target, number, sum_up, sum_down, others):
    ffns = others.shape[0]
    units = sum_up.shape[0] // ffns
    rows = pl.ds(pl.multiple_of(number * units, units), units)
    target[:units] = sum_up[rows]
    target[units : 2 * units] = sum_down[rows]
    target[2 * units :] = others[number]


def second_sums_kernel(*refs, ffns):
    gains, offsets, carried, mixed_keep, hat_one, hidden_keep = refs[:6]
    quarters = refs[10 : 10 + ffns]
    sum_up, sum_down, others = refs[10 + ffns :]
    parts = []
    for ref in refs[6:10]:
        half = ref.shape[1] // 2
        parts.append((ref[:, :half], ref[:, half:]))
    out, sum_up[...], sum_down[...] = ffn_weights_back(
        1, (mixed_keep, hat_one, hidden_keep), (gains, offsets), parts[:3]
    )
    qkv = product(tn, halves(carried[...]), parts[3])
    blocks = [qkv[:, at * WIDTH : (at + 1) * WIDTH] for at in range(3)] + [out]
    others[...] = jnp.concatenate(blocks, axis=0).reshape(others.shape)
    for k, quarter in enumerate(quarters):
        quarter_rows(quarter, ffn_index(ffns) ^ k, sum_up, sum_down, others)


def first_ffn_back_kernel(grad_rows, edge, out_rows, small_second, *refs, ffns):
    weights, keeps = refs[:8], refs[8:14]
    joined_keep, mixed_keep, pillars = refs[14:17]
    quarters = refs[17 : 17 + ffns]
    grad, small, sum_up, sum_down, sum_out, others, semaphores = refs[17 + ffns :]
    copies = Copies(semaphores)
    copies.start(edge.at[:, WIDTH:], pillars.at[:HALF])
    copies.start(out_rows.at[HALF:], pillars.at[HALF:])
    small[...] = jnp.zeros(small.shape, F32)
    grad[HALF:] = grad_rows[HALF:]
    grad[:HALF] = edge[:, :WIDTH]
    for step in range(grad.shape[0] // STEP):
        rows = slice(step * STEP, (step + 1) * STEP)
        saved = step_of(keeps, step)
        joined_keep[rows], mixed_keep[rows], parts = ffn_rows_back(0, grad[rows], saved, weights, small)
        made = ffn_weights_back(0, (saved[0], saved[1], saved[2]), weights[6:8], parts)
        for held, part in zip((sum_out, sum_up, sum_down), made):
            held[...] = held[...] + part if step else part
    part, few = WIDTH // ffns, 2 * small.shape[0] // ffns
    smalls = jnp.concatenate([small[...], small_second[...]], axis=0)
    others[...] = jnp.zeros(others.shape, F32)
    for number in range(ffns):
        others[number, :part] = sum_out[number * part : (number + 1) * part]
        others[number, part : part + few] = smalls[number * few : (number + 1) * few]
    for k, quarter in enumerate(quarters):
        quarter_rows(quarter, ffn_index(ffns) ^ k, sum_up, sum_down, others)
    for copy in copies.started:
        copy.wait()


def first_attention_back_kernel(*refs):
    stats, occupied_ref, lifted_ref, feats_ref, joined_keep, mixed_keep = refs[:6]
    qkv_weights, arrays = refs[6:8], refs[8:13]
    grad_affine, sum_qkv, sum_feats, small = refs[13:]
    live = live_column(occupied_ref)
    small[...] = jnp.zeros(small.shape, F32)
    for step in range(live.shape[0] // STEP):
        rows = slice(step * STEP, (step + 1) * STEP)
        vfe_slope, carried, *saved = step_of(arrays, step)
        grad, grad_packed = attention_rows_back(0, live[rows], joined_keep[rows], mixed_keep[rows], saved, qkv_weights)
        grad = grad * vfe_slope[...]
        grad_affine[rows] = grad
        small[0:1] += column_sum(grad * (lifted_ref[rows] - stats[1:2]) * stats[2:3])
        small[1:2] += column_sum(grad)
        for held, part in (
            (sum_qkv, product(tn, halves(carried[...]), grad_packed)),
            (sum_feats, product(tn, halves(feats_ref[rows]), halves(grad))),
        ):
            held[...] = held[...] + part if step else part


def share_kernel(sum_qkv, sum_feats, small, *refs, ffns, cuts):
    shared = refs[2 * ffns]
    devices = shared.shape[0]
    shared[...] = jnp.zeros(shared.shape, F32)
    row = 0
    for layer, counts in enumerate(cuts):
        quarters = refs[layer * ffns : (layer + 1) * ffns]
        total = quarters[0][...]
        for other in quarters[1:]:
            total = total + other[...]
        begin = 0
        for count in counts:
            row = share_rows(shared, row, total[begin : begin + count], devices)
            begin += count
    for block in range(3):
        row = share_rows(shared, row, sum_qkv[:, block * WIDTH : (block + 1) * WIDTH], devices)
    row = share_rows(shared, row, sum_feats[...], devices)
    shared[:, row : row + 2] = jnp.broadcast_to(small[0:2][None], (devices, 2, WIDTH))


def relay_kernel(
    arrived,
    hat_product,
    stats,
    bn_gain,
    affine,
    lifted_ref,
    occupied_ref,
    weight_ref,
    returned,
    vfe_grads,
    grad_feats,
    *,
    ffns,
    counts,
):
    unit_rows, second_rows, out_rows, small_rows, part = counts
    devices = returned.shape[0]
    cuts = [0]
    for count in (unit_rows, second_rows, unit_rows, out_rows, small_rows):
        cuts.append(cuts[-1] + count)
    later = cuts[-1]
    total = jnp.sum(arrived[:, later:], axis=0)
    first_qkv, tail = total[: 3 * part], total[3 * part :]
    blocks = []
    for f in range(ffns):
        block = arrived[f, :later]
        for device in range(f + ffns, devices, ffns):
            block = block + arrived[device, :later]
        blocks.append(block)
    gain, shift = tail[part : part + 1], tail[part + 1 : part + 2]
    lanes = lax.broadcasted_iota(jnp.int32, (part, WIDTH), 1)
    mine = lax.axis_index(AXES) * part + lax.broadcasted_iota(jnp.int32, (part, WIDTH), 0)
    live_sum = jnp.sum(jnp.where(lanes == mine, stats[3:4], 0.0), axis=1, keepdims=True)
    grad_w_vfe = stats[2:3] * bn_gain[0:1] * (
        tail[:part] - (hat_product[:part] * gain + live_sum * shift) / stats[0:1]
    )
    rows = jnp.concatenate(
        [block[cuts[at] : cuts[at + 1]] for at in (1, 3, 4) for block in blocks] + [first_qkv, grad_w_vfe],
        axis=0,
    )
    room = returned.shape[1] - 2 * unit_rows
    if rows.shape[0] < room:
        rows = jnp.concatenate([rows, jnp.zeros((room - rows.shape[0], WIDTH), F32)], axis=0)
    returned[:, 2 * unit_rows :] = jnp.broadcast_to(rows[None], (devices,) + rows.shape)
    for device in range(devices):
        f = device % ffns
        returned[device, :unit_rows] = blocks[f][: cuts[1]]
        returned[device, unit_rows : 2 * unit_rows] = blocks[f][cuts[2] : cuts[3]]
    vfe_grads[...] = jnp.concatenate([gain, shift, jnp.zeros((6, WIDTH), F32)], axis=0)
    hat = (lifted_ref[...] - stats[1:2]) * stats[2:3]
    grad = affine[...] - live_column(occupied_ref) * (hat * gain + shift) / stats[0:1]
    grad = stats[2:3] * bn_gain[0:1] * grad
    grad_feats[...] = product(nt, halves(grad), halves(weight_ref[...]))


def last_kernel(
    returned,
    vfe_grads,
    neck,
    grad_w_vfe,
    grad_bn_gain,
    grad_bn_shift,
    grad_w_qkv,
    grad_w_out,
    grad_w_in,
    grad_b_in,
    grad_w_back,
    grad_b_back,
    grad_ln_gain,
    grad_ln_shift,
    *,
    ffns,
):
    devices = returned.shape[0]
    units = grad_w_in.shape[1]
    part = share_of(WIDTH, devices)
    unit_rows = share_of(2 * units, devices)
    at = 0

    def take(count):
        nonlocal at
        rows = joined_rows(returned, at, count)
        at += share_of(count, devices)
        return rows

    blocks = [take(2 * units) for layer in range(2)]
    mine = ffn_index(ffns)

    def take_blocks(count):
        return jnp.concatenate([take(count) for f in range(ffns)], axis=0)

    for layer in (1, 0):
        grad_w_in[layer] = blocks[1 - layer][:units]
        grad_w_back[layer] = blocks[1 - layer][units:]
    rows = take_blocks(4 * WIDTH // ffns)
    for block in range(3):
        grad_w_qkv[1, :, block * WIDTH : (block + 1) * WIDTH] = rows[block * WIDTH : (block + 1) * WIDTH]
    grad_w_out[1] = rows[3 * WIDTH :]
    grad_w_out[0] = take_blocks(WIDTH // ffns)
    smalls = take_blocks(16 // ffns)
    for block in range(3):
        grad_w_qkv[0, :, block * WIDTH : (block + 1) * WIDTH] = take(WIDTH)
    for layer in range(2):
        small = smalls[layer * 8 : (layer + 1) * 8]
        grad_b_back[layer : layer + 1] = small[0:1]
        grad_ln_gain[2 * layer : 2 * layer + 1] = small[1:2]
        grad_ln_shift[2 * layer : 2 * layer + 1] = small[2:3]
        grad_ln_gain[2 * layer + 1 : 2 * layer + 2] = small[3:4]
        grad_ln_shift[2 * layer + 1 : 2 * layer + 2] = small[4:5]
        held = jnp.zeros((1, units), F32)
        for f in range(ffns):
            row, lane = divmod(f * units, WIDTH)
            held = jnp.where(mine == f, small[5 + row : 6 + row, lane : lane + units], held)
        grad_b_in[layer : layer + 1] = held
    grad_w_vfe[...] = take(WIDTH)
    grad_bn_gain[0:1] = vfe_grads[0:1]
    grad_bn_gain[1:2] = neck[0:1]
    grad_bn_shift[0:1] = vfe_grads[1:2]
    grad_bn_shift[1:2] = neck[1:2]


def spread_rows(pieces, axes):
    return lax.all_to_all(pieces, axes, 0, 0)


def partner(rows, k):
    return lax.ppermute(rows, "ffn", [(i, i ^ k) for i in range(lax.axis_size("ffn"))])


def passed_along(rows, by):
    peers = lax.axis_size(AXES)
    return lax.ppermute(rows, AXES, [(i, (i + by) % peers) for i in range(peers)])


def on_device(
    pillar_feats,
    occupied,
    shifted_source_rows,
    w_vfe,
    bn_gain,
    bn_shift,
    query_key_value_weight,
    attention_output_weight,
    up_weight_matrix,
    up_bias_rows,
    down_weight_matrix,
    down_bias_rows,
    layernorm_gains,
    layernorm_offsets,
    cotangent,
):
    row_count = pillar_feats.shape[0]
    spread = row_count + -(-HALF // 16) * 16
    ffns = lax.axis_size("ffn")
    devices = lax.axis_size(AXES)
    units = up_weight_matrix.shape[2]
    hidden = units * ffns
    windows = row_count // CELLS
    part = share_of(WIDTH, devices)
    piece = share_of(2 * units, devices)
    stats_rows = -(-(4 + part) // 8) * 8
    out_part, small_part = WIDTH // ffns, 16 // ffns
    second_cuts = (2 * units, 4 * WIDTH // ffns)
    first_cuts = (2 * units, out_part, small_part)
    shares = [share_of(count, devices) for count in second_cuts + first_cuts]
    shared_rows = -(-(sum(shares) + 4 * part + 2) // 8) * 8
    returned_rows = -(-(2 * piece + ffns * (shares[1] + shares[3] + shares[4]) + 4 * part) // 8) * 8
    rows_shape = shape(row_count, WIDTH)
    weights_kept = kept(windows, CELLS, HEADS * CELLS, dtype=BF16)
    rows_kept, hidden_kept = kept(row_count, WIDTH), kept(row_count, hidden)
    keeps = [
        rows_kept,
        kept(row_count, 3 * WIDTH),
        weights_kept,
        weights_kept,
        rows_kept,
        rows_kept,
        hidden_kept,
        hidden_kept,
        rows_kept,
        rows_kept,
    ]

    lifted, sent, packed = run(
        vfe_kernel,
        "vfe",
        (rows_shape, shape(devices, stats_rows, WIDTH), shape(4 * units + 8, WIDTH)),
        (
            pillar_feats,
            w_vfe,
            occupied,
            up_weight_matrix.transpose(0, 2, 1),
            down_weight_matrix,
            up_bias_rows,
        ),
    )
    seen = spread_rows(sent, AXES)
    packed = lax.all_gather(packed, "ffn", axis=0, tiled=False)
    weight_dims = (
        [(2, hidden, WIDTH, BF16)] * 4
        + [(2, hidden, F32)]
        + [(2, WIDTH, 3 * WIDTH, BF16)] * 2
        + [(2, WIDTH, WIDTH, BF16)] * 2
    )
    norms = pinned((down_bias_rows, layernorm_gains, layernorm_offsets))
    bn_pair = pinned((bn_gain, bn_shift))
    first_arrays = [rows_kept, rows_kept] + keeps
    outs = run(
        functools.partial(first_kernel, head=True),
        "first",
        [kept(*dims[:-1], dtype=dims[-1]) for dims in weight_dims]
        + [kept(8, WIDTH), kept(8, WIDTH), kept(HALF, 3 * WIDTH)]
        + first_arrays,
        (
            lifted,
            occupied,
            bn_gain,
            bn_shift,
            down_bias_rows,
            layernorm_gains,
            layernorm_offsets,
            Pinned(seen),
            packed,
            query_key_value_weight,
            attention_output_weight,
            Far(cotangent),
        ),
        scratch=[pltpu.VMEM((HALF, WIDTH), F32)],
        copies=1,
        flops=1e9,
    )
    weights, (stats, hat_product, edge) = outs[:9], outs[9:12]
    layer_weights = pinned(weights) + norms
    back_weights = pinned(weights[:4] + weights[5:]) + norms[1:]
    edge = passed_along(edge, -1)
    first_out, *first_keep = run(
        functools.partial(first_kernel, head=False),
        "first_rest",
        first_arrays,
        (
            Pinned(lifted),
            Pinned(occupied),
            *bn_pair,
            *norms,
            Pinned(stats),
            *pinned(weights),
            *pinned(outs[12:]),
        ),
        aliases={17 + at: at for at in range(len(first_arrays))},
        flops=1e9,
    )
    sent, *second_keep = run(
        second_kernel,
        "second",
        [kept(devices, 8, WIDTH), rows_kept, kept(row_count, 1), rows_kept] + keeps,
        (
            Pinned(first_out),
            Pinned(cotangent),
            Pinned(occupied),
            Pinned(edge),
            Pinned(shifted_source_rows),
            *layer_weights,
        ),
        scratch=[pltpu.VMEM((spread, 5 * WIDTH), BF16), pltpu.VMEM((8, WIDTH), F32)],
        flops=2e9,
    )
    seen = spread_rows(sent, AXES)
    second_carried, second_mixed, second_hat, second_hidden = (second_keep[at] for at in (3, 7, 8, 9))
    edge, grad_rows, out_rows, neck, small, *parts = run(
        second_back_kernel,
        "second_back",
        [kept(HALF, 2 * WIDTH), rows_kept, rows_kept, kept(8, WIDTH), kept(8, WIDTH)]
        + [kept(row_count, width, dtype=BF16) for width in (2 * WIDTH, 2 * hidden, 2 * WIDTH, 6 * WIDTH)],
        (Pinned(seen), *bn_pair, Pinned(shifted_source_rows), *back_weights, *pinned(second_keep)),
        flops=4e9,
    )
    edge = passed_along(edge, 1)
    sums = [pltpu.VMEM((hidden, WIDTH), F32)] * 2

    def over_ffn(quarters):
        return [quarters[0]] + [partner(quarters[k], k) for k in range(1, ffns)]

    second_quarters = run(
        functools.partial(second_sums_kernel, ffns=ffns),
        "second_sums",
        [kept(sum(second_cuts), WIDTH)] * ffns,
        (*norms[1:], *pinned((second_carried, second_mixed, second_hat, second_hidden, *parts))),
        scratch=sums + [pltpu.VMEM((ffns, second_cuts[1], WIDTH), F32)],
        flops=1e9,
    )
    second_quarters = over_ffn(second_quarters)
    first_others = -(-(out_part + small_part) // 8) * 8
    grad_joined, grad_mixed, pillars_out, *first_quarters = run(
        functools.partial(first_ffn_back_kernel, ffns=ffns),
        "first_ffn_back",
        [rows_kept, rows_kept, Far(rows_shape)] + [kept(2 * units + first_others, WIDTH)] * ffns,
        (*pinned((grad_rows, edge, out_rows, small)), *back_weights[:4], *back_weights[6:], *pinned(first_keep[5:])),
        scratch=[pltpu.VMEM((row_count, WIDTH), F32), pltpu.VMEM((8, WIDTH), F32)]
        + sums
        + [pltpu.VMEM((WIDTH, WIDTH), F32), pltpu.VMEM((ffns, first_others, WIDTH), F32)],
        copies=2,
        flops=2e9,
    )
    first_quarters = over_ffn(first_quarters)
    grad_affine, *late_sums = run(
        first_attention_back_kernel,
        "first_attention_back",
        [rows_kept, kept(WIDTH, 3 * WIDTH), kept(WIDTH, WIDTH), kept(8, WIDTH)],
        pinned(
            (stats, occupied, lifted, pillar_feats, grad_joined, grad_mixed, *weights[5:7], *first_keep[:5])
        ),
        flops=4e9,
    )
    (shared,) = run(
        functools.partial(share_kernel, ffns=ffns, cuts=(second_cuts, first_cuts)),
        "share",
        [kept(devices, shared_rows, WIDTH)],
        pinned((*late_sums, *second_quarters, *first_quarters)),
    )
    arrived = spread_rows(shared, AXES)
    returned, vfe_grads, grad_feats = run(
        functools.partial(relay_kernel, ffns=ffns, counts=(*shares[:2], *shares[3:], part)),
        "relay",
        (kept(devices, returned_rows, WIDTH), kept(8, WIDTH), rows_shape),
        pinned((arrived, hat_product, stats, bn_gain, grad_affine, lifted, occupied, w_vfe)),
    )
    returned = spread_rows(returned, AXES)
    grads = list(run(
        functools.partial(last_kernel, ffns=ffns),
        "last",
        (
            shape(WIDTH, WIDTH),
            shape(2, WIDTH),
            shape(2, WIDTH),
            shape(2, WIDTH, 3 * WIDTH),
            shape(2, WIDTH, WIDTH),
            shape(2, units, WIDTH),
            shape(2, units),
            shape(2, units, WIDTH),
            shape(2, WIDTH),
            shape(4, WIDTH),
            shape(4, WIDTH),
        ),
        pinned((returned, vfe_grads, neck)),
    ))
    grads[5] = grads[5].transpose(0, 2, 1)
    return (pillars_out, grad_feats, *grads)


def solution(mesh):
    return jax.shard_map(
        on_device,
        mesh=mesh,
        in_specs=(
            P(("win", "ffn"), None),
            P(("win", "ffn")),
            P(("win", "ffn")),
            P(),
            P(),
            P(),
            P(),
            P(),
            P(None, None, "ffn"),
            P(None, "ffn"),
            P(None, "ffn", None),
            P(),
            P(),
            P(),
            P(("win", "ffn"), None),
        ),
        out_specs=(
            P(("win", "ffn"), None),
            P(("win", "ffn"), None),
            P(),
            P(),
            P(),
            P(),
            P(),
            P(None, None, "ffn"),
            P(None, "ffn"),
            P(None, "ffn", None),
            P(),
            P(),
            P(),
        ),
        check_vma=False,
    )
```

```python
import functools

import jax
import jax.numpy as jnp
from jax import lax
from jax.experimental import pallas as pl
from jax.experimental.pallas import tpu as pltpu
from jax.sharding import PartitionSpec as P

HEADS = 8
CELLS = 144
HALF = CELLS // 2
WIDTH = 128
EPS_NORM = 1e-05
NEG_FILL = -1000000000.0
AXES = ("win", "ffn")
STEP = 3 * CELLS
HEAD = 2 * CELLS
TILE_ROWS = WIDTH // HEADS
TILES = CELLS // TILE_ROWS
CHUNKS = ((0, 2), (2, 4), (4, 6), (6, 8), (8, 9))
F32 = jnp.float32
BF16 = jnp.bfloat16
VMEM_LIMIT = 28 * 1024 * 1024


def shape(*dims, dtype=F32):
    return pltpu.HBM(dims, dtype)


def kept(*dims, dtype=F32):
    return pltpu.VMEM(dims, dtype)


class Pinned:
    def __init__(self, value):
        self.value = value


class Far:
    def __init__(self, value):
        self.value = value


def run(kernel, name, outs, args, scratch=(), copies=0, aliases=None, flops=1e8):
    near, far = pl.BlockSpec(memory_space=pltpu.VMEM), pl.BlockSpec(memory_space=pltpu.HBM)
    values = []
    for arg in args:
        space = pltpu.VMEM if isinstance(arg, Pinned) else pltpu.HBM
        value = arg.value if isinstance(arg, (Pinned, Far)) else arg
        values.append(pltpu.with_memory_space_constraint(value, space))
    scratch = list(scratch)
    if copies:
        scratch.append(pltpu.SemaphoreType.DMA((copies,)))
    return pl.pallas_call(
        kernel,
        out_shape=[out.value if isinstance(out, Far) else out for out in outs],
        in_specs=[far if isinstance(arg, Far) else near for arg in args],
        out_specs=[far if isinstance(out, Far) else near for out in outs],
        scratch_shapes=scratch,
        input_output_aliases=aliases or {},
        compiler_params=pltpu.CompilerParams(vmem_limit_bytes=VMEM_LIMIT),
        cost_estimate=pl.CostEstimate(flops=int(flops), bytes_accessed=1000000, transcendentals=0),
        name=name,
    )(*values)


def pinned(values):
    return [Pinned(value) for value in values]


class Copies:
    def __init__(self, semaphores):
        self.semaphores = semaphores
        self.started = []

    def start(self, source, target):
        copy = pltpu.make_async_copy(source, target, self.semaphores.at[len(self.started)])
        copy.start()
        self.started.append(copy)
        return copy


def scratch_like(arrays):
    return [pltpu.VMEM(array.shape, array.dtype) for array in arrays]


def ffn_index(ffns):
    return lax.rem(lax.axis_index(AXES), ffns)


def share_of(rows, devices):
    return -(-rows // devices)


def halves(values):
    high = values.astype(BF16)
    return high, (values - high.astype(F32)).astype(BF16)


def nn(former, latter):
    return lax.dot_general(former, latter, (((1,), (0,)), ((), ())), preferred_element_type=F32)


def nt(former, latter):
    return lax.dot_general(former, latter, (((1,), (1,)), ((), ())), preferred_element_type=F32)


def tn(former, latter):
    return lax.dot_general(former, latter, (((0,), (0,)), ((), ())), preferred_element_type=F32)


def product(kind, former, latter):
    columns = latter[0].shape[0 if kind is nt else 1]
    if columns == WIDTH:
        both = kind(former[0], jnp.concatenate(latter, axis=0 if kind is nt else 1))
        return both[:, :columns] + (both[:, columns:] + kind(former[1], latter[0]))
    if kind is tn:
        rows = former[0].shape[1]
        both = kind(jnp.concatenate(former, axis=1), latter[0])
        return both[:rows] + (both[rows:] + kind(former[0], latter[1]))
    if former[0].shape[1] == WIDTH:
        twice = jnp.concatenate([latter[0]] * 2, axis=1 if kind is nt else 0)
        return kind(jnp.concatenate(former, axis=1), twice) + kind(former[0], latter[1])
    return kind(former[0], latter[0]) + (kind(former[0], latter[1]) + kind(former[1], latter[0]))


def gelu_parts(values):
    below = 0.5 * (1.0 + lax.erf(values * 0.7071067811865476))
    density = 0.3989422804014327 * jnp.exp(-0.5 * values * values)
    return values * below, below + values * density


def normed_rows(values):
    center = jnp.mean(values, axis=-1, keepdims=True)
    moved = values - center
    rate = lax.rsqrt(jnp.mean(moved * moved, axis=-1, keepdims=True) + EPS_NORM)
    return moved * rate, rate


def normed_back(grad, hat, rate, gain):
    scaled = grad * gain
    first = jnp.mean(scaled, axis=-1, keepdims=True)
    second = jnp.mean(scaled * hat, axis=-1, keepdims=True)
    return rate * (scaled - first - hat * second)


def live_column(occupied_ref):
    row = occupied_ref[...].astype(F32).reshape(1, occupied_ref.shape[0])
    return jnp.broadcast_to(row, (8, row.shape[1])).T[:, :1]


def column_sum(values):
    return jnp.sum(values, axis=0, keepdims=True)


def head_mask():
    dims = (HEADS, TILE_ROWS, WIDTH)
    lane_head = lax.broadcasted_iota(jnp.int32, dims, 2) // TILE_ROWS
    return (lane_head == lax.broadcasted_iota(jnp.int32, dims, 0)).astype(F32)


def per_head(rows, mask):
    count = rows.shape[0] // TILE_ROWS
    return (rows.reshape(count, 1, TILE_ROWS, WIDTH) * mask[None]).reshape(count * WIDTH, WIDTH)


def from_heads(table, mask):
    parts = []
    for at in range(0, table.shape[1], WIDTH):
        turned = table[:, at : at + WIDTH].T.reshape(HEADS, TILE_ROWS, WIDTH)
        parts.append(jnp.sum(turned * mask, axis=0))
    return parts


def high_and_low(values):
    high, low = halves(values.T)
    return jnp.concatenate([high, low], axis=0), high


def stacked_product(stack, high_alone, weights):
    both = nn(stack, weights[0])
    return both[:WIDTH] + (both[WIDTH:] + nn(high_alone, weights[1]))


def window_mix(query, key, value, live, mask, mask_low, keep_high, keep_low):
    query_high, query_low = halves(query)
    key_high, key_low = halves(key)
    key_stack = jnp.concatenate([key_high, key_low, key_high], axis=1)
    turned = high_and_low(value)
    mixed = []
    for first, last in CHUNKS:
        rows = slice(first * TILE_ROWS, last * TILE_ROWS)
        lanes = slice(first * WIDTH, last * WIDTH)
        high = per_head(query_high[rows], mask_low)
        low = per_head(query_low[rows], mask_low)
        scores = nt(key_stack, jnp.concatenate([high, high, low], axis=1))
        scores = jnp.where(live > 0, scores, NEG_FILL)
        weights = jnp.exp(scores - jnp.max(scores, axis=0, keepdims=True))
        weights = weights * (1.0 / column_sum(weights))
        weights = halves(weights)
        keep_high[:, lanes] = weights[0]
        keep_low[:, lanes] = weights[1]
        mixed += from_heads(stacked_product(*turned, weights), mask)
    return jnp.concatenate(mixed, axis=0)


def window_back(query, key, value, grad_mixed, live, mask, mask_low, high, low):
    query_high, query_low = (per_head(part, mask_low) for part in halves(query))
    grad_high, grad_low = (per_head(part, mask_low) for part in halves(grad_mixed))
    value_high, value_low = halves(value)
    value_stack = jnp.concatenate([value_high, value_low, value_high], axis=1)
    grad_weights = nt(value_stack, jnp.concatenate([grad_high, grad_high, grad_low], axis=1))
    weights = high.astype(F32) + low.astype(F32)
    grad_scores = weights * grad_weights
    grad_scores = live * (grad_scores - weights * column_sum(grad_scores))
    scores_high, scores_low = halves(grad_scores)

    def over_queries(upper, lower, high, low):
        both = nn(
            jnp.concatenate([upper, lower], axis=0), jnp.concatenate([high, low], axis=1)
        )
        return both[:CELLS, :WIDTH] + (both[:CELLS, WIDTH:] + both[CELLS:, :WIDTH])

    grad_query = stacked_product(*high_and_low(key), (scores_high, scores_low))
    return (
        0.25 * jnp.concatenate(from_heads(grad_query, mask), axis=0),
        over_queries(scores_high, scores_low, query_high, query_low),
        over_queries(high, low, grad_high, grad_low),
    )


def unpack(packed, qkv_ref, out_ref, up_high, up_low, down_high, down_low, bias, qkv_high, qkv_low, out_high, out_low):
    ffns = packed.shape[0]
    units = bias.shape[1] // ffns
    for one in range(2):
        for at in range(ffns):
            rows = slice(at * units, (at + 1) * units)
            high, low = halves(packed[at, one * units : (one + 1) * units])
            up_high[one, rows], up_low[one, rows] = high, low
            high, low = halves(packed[at, (2 + one) * units : (3 + one) * units])
            down_high[one, rows], down_low[one, rows] = high, low
        bias[one : one + 1] = jnp.concatenate(
            [packed[at, 4 * units + one : 4 * units + one + 1, :units] for at in range(ffns)], axis=1
        )
    qkv_high[...], qkv_low[...] = halves(qkv_ref[...])
    out_high[...], out_low[...] = halves(out_ref[...])


def layer_rows(one, values, live, weights, saved):
    up_high, up_low, down_high, down_low, bias, qkv_high, qkv_low, out_high, out_low, back_bias, gains, offsets = weights
    packed_keep, high_keep, low_keep, mixed_keep, hat_one, hidden_keep, slope, hat_two, rates = saved
    mask = head_mask()
    mask_low = mask.astype(BF16)
    qkv = product(nn, halves(values), (qkv_high[one], qkv_low[one]))
    query = 0.25 * qkv[:, :WIDTH]
    packed_keep[:, :WIDTH] = query
    packed_keep[:, WIDTH:] = qkv[:, WIDTH:]
    for at in range(values.shape[0] // CELLS):
        rows = slice(at * CELLS, (at + 1) * CELLS)
        mixed_keep[rows] = window_mix(
            query[rows],
            qkv[rows, WIDTH : 2 * WIDTH],
            qkv[rows, 2 * WIDTH :],
            live[rows],
            mask,
            mask_low,
            high_keep.at[at],
            low_keep.at[at],
        )
    mixed = mixed_keep[...]
    hat, rate = normed_rows(
        values + product(nn, halves(mixed), (out_high[one], out_low[one]))
    )
    hat_one[...] = hat
    first = hat * gains[2 * one : 2 * one + 1] + offsets[2 * one : 2 * one + 1]
    hidden, steep = gelu_parts(
        product(nt, halves(first), (up_high[one], up_low[one])) + bias[one : one + 1]
    )
    hidden_keep[...] = hidden
    slope[...] = steep
    summed = first + product(nn, halves(hidden), (down_high[one], down_low[one])) + back_bias[one : one + 1]
    hat, last_rate = normed_rows(summed)
    hat_two[...] = hat
    lanes = lax.broadcasted_iota(jnp.int32, hat.shape, 1)
    rates[...] = jnp.where(lanes < WIDTH // 2, rate, last_rate)
    return hat * gains[2 * one + 1 : 2 * one + 2] + offsets[2 * one + 1 : 2 * one + 2]


def ffn_rows_back(one, grad, saved, weights, small):
    mixed_keep, hat_one, hidden_keep, slope, hat_two, rates = saved
    up_high, up_low, down_high, down_low, out_high, out_low, gains, offsets = weights
    up, down, out = (up_high[one], up_low[one]), (down_high[one], down_low[one]), (out_high[one], out_low[one])
    hat = hat_two[...]
    grad_summed = normed_back(grad, hat, rates[:, WIDTH - 1 :], gains[2 * one + 1 : 2 * one + 2])
    small[3:4] += column_sum(grad * hat)
    small[4:5] += column_sum(grad)
    small[0:1] += column_sum(grad_summed)
    summed_halves = halves(grad_summed)
    grad_pre = product(nt, summed_halves, down) * slope[...]
    pre_halves = halves(grad_pre)
    hat = hat_one[...]
    bias_sum = column_sum(grad_pre)
    for at in range(bias_sum.shape[1] // WIDTH):
        small[5 + at : 6 + at] += bias_sum[:, at * WIDTH : (at + 1) * WIDTH]
    grad_first = grad_summed + product(nn, pre_halves, up)
    small[1:2] += column_sum(grad_first * hat)
    small[2:3] += column_sum(grad_first)
    grad_joined = normed_back(grad_first, hat, rates[:, 0:1], gains[2 * one : 2 * one + 1])
    joined_halves = halves(grad_joined)
    return grad_joined, product(nt, joined_halves, out), (summed_halves, pre_halves, joined_halves)


def ffn_weights_back(one, saved, norms, parts):
    mixed_keep, hat_one, hidden_keep = saved
    gains, offsets = norms
    summed_halves, pre_halves, joined_halves = parts
    first = hat_one[...] * gains[2 * one : 2 * one + 1] + offsets[2 * one : 2 * one + 1]
    return (
        product(tn, halves(mixed_keep[...]), joined_halves),
        product(tn, pre_halves, halves(first)),
        product(tn, halves(hidden_keep[...]), summed_halves),
    )


def attention_rows_back(one, live, grad_joined, grad_mixed, saved, qkv_weights):
    packed_keep, high_keep, low_keep = saved
    mask = head_mask()
    mask_low = mask.astype(BF16)
    parts = []
    for at in range(grad_joined.shape[0] // CELLS):
        rows = slice(at * CELLS, (at + 1) * CELLS)
        parts.append(
            window_back(
                packed_keep[rows, :WIDTH],
                packed_keep[rows, WIDTH : 2 * WIDTH],
                packed_keep[rows, 2 * WIDTH :],
                grad_mixed[rows],
                live[rows],
                mask,
                mask_low,
                high_keep[at],
                low_keep[at],
            )
        )
    grad_packed = halves(
        jnp.concatenate([jnp.concatenate(part, axis=1) for part in parts], axis=0)
    )
    return grad_joined + product(nt, grad_packed, (qkv_weights[0][one], qkv_weights[1][one])), grad_packed


def share_rows(target, at, values, devices):
    count = values.shape[0]
    share = share_of(count, devices)
    for device in range(devices):
        begin = device * share
        if begin < count:
            held = min(share, count - begin)
            target[device, at : at + held] = values[begin : begin + held]
    return at + share


def joined_rows(table, at, count):
    devices = 2 * table.shape[1]
    share = share_of(count, devices)
    pieces = []
    for device in range(devices):
        begin = device * share
        if begin < count:
            pieces.append(table[device % 2, device // 2, at : at + min(share, count - begin)])
    return jnp.concatenate(pieces, axis=0)


def vfe_kernel(
    feats_ref, weight_ref, occupied_ref, up_ref, down_ref, bias_ref, lifted_ref, sent_ref, packed_ref
):
    devices = sent_ref.shape[0]
    units = up_ref.shape[1]
    feats = feats_ref[...]
    feats_halves = halves(feats)
    lifted = product(nn, feats_halves, halves(weight_ref[...]))
    lifted_ref[...] = lifted
    live = live_column(occupied_ref)
    count = jnp.sum(live, axis=0, keepdims=True)
    total = column_sum(live * lifted)
    moved = live * (lifted - total / jnp.maximum(count, 1.0))
    sent_ref[...] = jnp.zeros(sent_ref.shape, F32)
    stats = jnp.concatenate(
        [
            jnp.broadcast_to(count, (1, WIDTH)),
            total,
            column_sum(moved * moved),
            column_sum(live * feats),
        ],
        axis=0,
    )
    sent_ref[:, 0:4] = jnp.broadcast_to(stats[None], (devices, 4, WIDTH))
    share_rows(sent_ref, 4, product(tn, feats_halves, halves(moved)), devices)
    for one in range(2):
        packed_ref[one * units : (one + 1) * units] = up_ref[one]
        packed_ref[(2 + one) * units : (3 + one) * units] = down_ref[one]
    packed_ref[4 * units :] = jnp.zeros((8, WIDTH), F32)
    packed_ref[4 * units : 4 * units + 2, :units] = bias_ref[...]


def places_of(source_ref):
    row_count = source_ref.shape[0]
    places = source_ref[...].reshape(1, row_count) - lax.axis_index(AXES) * row_count
    return jnp.where(places < 0, places + row_count * lax.axis_size(AXES), places)


def one_hot(former, latter):
    return (former == latter).astype(F32).astype(BF16)


def vfe_stats(seen_ref, stats_ref, product_ref):
    counts, totals, squares, lives = (seen_ref[:, at] for at in range(4))
    count = column_sum(counts)
    center = column_sum(totals) / count
    moves = totals / jnp.maximum(counts, 1.0) - center
    rate = lax.rsqrt(column_sum(squares + counts * moves * moves) / count + EPS_NORM)
    stats_ref[...] = jnp.zeros(stats_ref.shape, F32)
    stats_ref[0:1] = count
    stats_ref[1:2] = center
    stats_ref[2:3] = rate
    stats_ref[3:4] = column_sum(lives)
    devices = seen_ref.shape[0]
    share = share_of(WIDTH, devices)
    mine = lax.axis_index(AXES) * share
    lanes = lax.broadcasted_iota(jnp.int32, lives.shape, 1)
    product_ref[...] = jnp.zeros(product_ref.shape, F32)
    for at in range(share):
        picked = jnp.sum(jnp.where(lanes == mine + at, lives, 0.0), axis=1, keepdims=True)
        product_ref[at : at + 1] = rate * column_sum(seen_ref[:, 4 + at] + picked * moves)


def rows_in(refs, begin, end):
    return [
        ref.at[begin // CELLS : end // CELLS] if len(ref.shape) == 3 else ref.at[begin:end]
        for ref in refs
    ]


def step_of(refs, step):
    return rows_in(refs, step * STEP, (step + 1) * STEP)


def first_kernel(*refs, head):
    lifted_ref, occupied_ref, bn_gain, bn_shift, back_bias, gains, offsets = refs[:7]
    if head:
        seen_ref, packed, qkv_ref, out_ref, cotangent_ref = refs[7:12]
        weights = refs[12:21]
        stats, hat_product, edge = refs[21:24]
        arrays = refs[24:36]
        cotangent, semaphores = refs[36:]
        copies = Copies(semaphores)
        arrival = copies.start(cotangent_ref.at[:HALF], cotangent)
        unpack(packed, qkv_ref, out_ref, *weights)
        vfe_stats(seen_ref, stats, hat_product)
        rows = slice(0, HEAD)
    else:
        stats = refs[7]
        weights = refs[8:17]
        arrays = refs[17 + (len(refs) - 17) // 2 :]
        rows = slice(HEAD, lifted_ref.shape[0])
    result, vfe_slope, carried, *saved = rows_in(arrays, rows.start, rows.stop)
    hat = (lifted_ref[rows] - stats[1:2]) * stats[2:3]
    values, steep = gelu_parts(hat * bn_gain[0:1] + bn_shift[0:1])
    vfe_slope[...] = steep
    carried[...] = values
    live = live_column(occupied_ref)[rows]
    rows = layer_rows(0, values, live, (*weights, back_bias, gains, offsets), saved)
    result[...] = rows
    if head:
        arrival.wait()
        edge[:, :WIDTH] = rows[:HALF]
        edge[:, WIDTH : 2 * WIDTH] = cotangent[...]
        edge[:, 2 * WIDTH :] = jnp.broadcast_to(live[:HALF], (HALF, WIDTH))


def second_kernel(first_ref, cotangent_ref, occupied_ref, edge, source_ref, *refs):
    weights = refs[:12]
    sent = refs[12]
    arrays = refs[13:-2]
    table, sums = refs[-2:]
    row_count = cotangent_ref.shape[0]
    high, low = halves(first_ref[...])
    table[:row_count, :WIDTH] = high
    table[:row_count, WIDTH : 2 * WIDTH] = low
    high, low = halves(cotangent_ref[...])
    table[:row_count, 2 * WIDTH : 3 * WIDTH] = high
    table[:row_count, 3 * WIDTH : 4 * WIDTH] = low
    table[:row_count, 4 * WIDTH :] = jnp.broadcast_to(live_column(occupied_ref), (row_count, WIDTH)).astype(BF16)
    spare = table.shape[0] - row_count
    tail = jnp.concatenate([edge[...], jnp.zeros((spare - HALF, 3 * WIDTH), F32)], axis=0)
    high, low = halves(tail)
    table[row_count:, :WIDTH] = high[:, :WIDTH]
    table[row_count:, WIDTH : 2 * WIDTH] = low[:, :WIDTH]
    table[row_count:, 2 * WIDTH : 3 * WIDTH] = high[:, WIDTH : 2 * WIDTH]
    table[row_count:, 3 * WIDTH : 4 * WIDTH] = low[:, WIDTH : 2 * WIDTH]
    table[row_count:, 4 * WIDTH :] = high[:, 2 * WIDTH :]
    places = jnp.broadcast_to(places_of(source_ref).astype(F32), (8, row_count))
    column = places.T[:, :1].astype(jnp.int32)
    lanes = lax.broadcasted_iota(jnp.int32, (STEP, table.shape[0]), 1)
    for step in range(row_count // STEP):
        result, live_keep, cotangent_keep, carried, *saved = step_of(arrays, step)
        gathered = nn(one_hot(lanes, column[step * STEP : (step + 1) * STEP]), table[...])
        values = gathered[:, :WIDTH] + gathered[:, WIDTH : 2 * WIDTH]
        live = gathered[:, 4 * WIDTH :]
        grad = live * (gathered[:, 2 * WIDTH : 3 * WIDTH] + gathered[:, 3 * WIDTH : 4 * WIDTH])
        carried[...] = values
        cotangent_keep[...] = grad
        live_keep[...] = live[:, :1]
        rows = layer_rows(1, values, live[:, :1], weights, saved)
        result[...] = rows
        count = column_sum(live)
        if step == 0:
            sums[...] = jnp.zeros(sums.shape, F32)
            sums[5:6] = column_sum(live * rows) / jnp.maximum(count, 1.0)
        moved = rows - sums[5:6]
        sums[0:1] += count
        sums[1:2] += column_sum(live * moved)
        sums[2:3] += column_sum(live * moved * moved)
        sums[3:4] += column_sum(grad)
        sums[4:5] += column_sum(grad * moved)
    count = sums[0:1]
    move = sums[1:2] / jnp.maximum(count, 1.0)
    stats = jnp.concatenate(
        [
            count,
            sums[5:6] + move,
            sums[2:3] - count * move * move,
            sums[3:4],
            sums[4:5] - move * sums[3:4],
            jnp.zeros((3, WIDTH), F32),
        ],
        axis=0,
    )
    sent[...] = jnp.broadcast_to(stats[None], sent.shape)


def second_back_kernel(seen_ref, bn_gain, bn_shift, source_ref, *refs):
    weights = refs[:10]
    arrays = refs[10:23]
    edge, grad_rows, out_rows, neck, small, summed_keep, pre_keep, joined_keep, packed_back = refs[23:]
    row_count = out_rows.shape[0]
    counts, means, squares, grads, products = (seen_ref[:, row] for row in range(5))
    count = column_sum(counts)
    center = column_sum(counts * means) / count
    moves = means - center
    rate = lax.rsqrt(column_sum(squares + counts * moves * moves) / count + EPS_NORM)
    gain_grad = rate * column_sum(products + moves * grads)
    shift_grad = column_sum(grads)
    neck[...] = jnp.concatenate([gain_grad, shift_grad, jnp.zeros((6, WIDTH), F32)], axis=0)
    small[...] = jnp.zeros(small.shape, F32)
    places = places_of(source_ref)
    down = lax.broadcasted_iota(jnp.int32, (-(-(row_count + HALF) // 8) * 8, STEP), 0)
    placed = None
    for step in range(row_count // STEP):
        rows = slice(step * STEP, (step + 1) * STEP)
        result, live_keep, cotangent_keep, carried, packed_keep, high_keep, low_keep, *keeps = step_of(arrays, step)
        live = live_keep[...]
        hat = (result[...] - center) * rate
        neck_rows = live * (hat * bn_gain[1:2] + bn_shift[1:2])
        grad = rate * bn_gain[1:2] * (
            cotangent_keep[...] - live * (hat * gain_grad + shift_grad) / count
        )
        grad_joined, grad_mixed, parts = ffn_rows_back(1, grad, keeps, weights[:4] + weights[6:10], small)
        grad_values, grad_packed = attention_rows_back(
            1, live, grad_joined, grad_mixed, (packed_keep, high_keep, low_keep), weights[4:6]
        )
        for kept_halves, part in zip((summed_keep, pre_keep, joined_keep, packed_back), (*parts, grad_packed)):
            kept_halves[rows] = jnp.concatenate(part, axis=1)
        pieces = jnp.concatenate(halves(grad_values) + halves(neck_rows), axis=1)
        moved = nn(one_hot(down, places[:, rows]), pieces)
        moved = jnp.concatenate(
            [
                moved[:, :WIDTH] + moved[:, WIDTH : 2 * WIDTH],
                moved[:, 2 * WIDTH : 3 * WIDTH] + moved[:, 3 * WIDTH :],
            ],
            axis=1,
        )
        placed = moved if placed is None else placed + moved
    grad_rows[...] = placed[:row_count, :WIDTH]
    out_rows[...] = placed[:row_count, WIDTH:]
    edge[...] = placed[row_count : row_count + HALF]


def quarter_rows(target, number, sum_up, sum_down, others):
    ffns = others.shape[0]
    units = sum_up.shape[0] // ffns
    rows = pl.ds(pl.multiple_of(number * units, units), units)
    target[:units] = sum_up[rows]
    target[units : 2 * units] = sum_down[rows]
    target[2 * units :] = others[number]


def second_sums_kernel(*refs, ffns):
    gains, offsets, carried, mixed_keep, hat_one, hidden_keep = refs[:6]
    quarters = refs[10 : 10 + ffns]
    sum_up, sum_down, others = refs[10 + ffns :]
    parts = []
    for ref in refs[6:10]:
        half = ref.shape[1] // 2
        parts.append((ref[:, :half], ref[:, half:]))
    out, sum_up[...], sum_down[...] = ffn_weights_back(
        1, (mixed_keep, hat_one, hidden_keep), (gains, offsets), parts[:3]
    )
    qkv = product(tn, halves(carried[...]), parts[3])
    blocks = [qkv[:, at * WIDTH : (at + 1) * WIDTH] for at in range(3)] + [out]
    others[...] = jnp.concatenate(blocks, axis=0).reshape(others.shape)
    for k, quarter in enumerate(quarters):
        quarter_rows(quarter, ffn_index(ffns) ^ k, sum_up, sum_down, others)


def first_ffn_back_kernel(grad_rows, edge, out_rows, small_second, *refs, ffns):
    weights, keeps = refs[:8], refs[8:14]
    joined_keep, mixed_keep, pillars = refs[14:17]
    quarters = refs[17 : 17 + ffns]
    grad, small, sum_up, sum_down, sum_out, others, semaphores = refs[17 + ffns :]
    copies = Copies(semaphores)
    copies.start(edge.at[:, WIDTH:], pillars.at[:HALF])
    copies.start(out_rows.at[HALF:], pillars.at[HALF:])
    small[...] = jnp.zeros(small.shape, F32)
    grad[HALF:] = grad_rows[HALF:]
    grad[:HALF] = edge[:, :WIDTH]
    for step in range(grad.shape[0] // STEP):
        rows = slice(step * STEP, (step + 1) * STEP)
        saved = step_of(keeps, step)
        joined_keep[rows], mixed_keep[rows], parts = ffn_rows_back(0, grad[rows], saved, weights, small)
        made = ffn_weights_back(0, (saved[0], saved[1], saved[2]), weights[6:8], parts)
        for held, part in zip((sum_out, sum_up, sum_down), made):
            held[...] = held[...] + part if step else part
    part, few = WIDTH // ffns, 2 * small.shape[0] // ffns
    smalls = jnp.concatenate([small[...], small_second[...]], axis=0)
    others[...] = jnp.zeros(others.shape, F32)
    for number in range(ffns):
        others[number, :part] = sum_out[number * part : (number + 1) * part]
        others[number, part : part + few] = smalls[number * few : (number + 1) * few]
    for k, quarter in enumerate(quarters):
        quarter_rows(quarter, ffn_index(ffns) ^ k, sum_up, sum_down, others)
    for copy in copies.started:
        copy.wait()


def first_attention_back_kernel(*refs):
    stats, occupied_ref, lifted_ref, feats_ref, joined_keep, mixed_keep = refs[:6]
    qkv_weights, arrays = refs[6:8], refs[8:13]
    grad_affine, sum_qkv, sum_feats, small = refs[13:]
    live = live_column(occupied_ref)
    small[...] = jnp.zeros(small.shape, F32)
    for step in range(live.shape[0] // STEP):
        rows = slice(step * STEP, (step + 1) * STEP)
        vfe_slope, carried, *saved = step_of(arrays, step)
        grad, grad_packed = attention_rows_back(0, live[rows], joined_keep[rows], mixed_keep[rows], saved, qkv_weights)
        grad = grad * vfe_slope[...]
        grad_affine[rows] = grad
        small[0:1] += column_sum(grad * (lifted_ref[rows] - stats[1:2]) * stats[2:3])
        small[1:2] += column_sum(grad)
        for held, part in (
            (sum_qkv, product(tn, halves(carried[...]), grad_packed)),
            (sum_feats, product(tn, halves(feats_ref[rows]), halves(grad))),
        ):
            held[...] = held[...] + part if step else part


def share_kernel(sum_qkv, sum_feats, small, *refs, ffns, cuts):
    shared = refs[2 * ffns]
    devices = shared.shape[0]
    shared[...] = jnp.zeros(shared.shape, F32)
    row = 0
    for layer, counts in enumerate(cuts):
        quarters = refs[layer * ffns : (layer + 1) * ffns]
        total = quarters[0][...]
        for other in quarters[1:]:
            total = total + other[...]
        begin = 0
        for count in counts:
            row = share_rows(shared, row, total[begin : begin + count], devices)
            begin += count
    for block in range(3):
        row = share_rows(shared, row, sum_qkv[:, block * WIDTH : (block + 1) * WIDTH], devices)
    row = share_rows(shared, row, sum_feats[...], devices)
    shared[:, row : row + 2] = jnp.broadcast_to(small[0:2][None], (devices, 2, WIDTH))


def relay_kernel(
    arrived,
    hat_product,
    stats,
    bn_gain,
    affine,
    lifted_ref,
    occupied_ref,
    weight_ref,
    returned,
    vfe_grads,
    grad_feats,
    *,
    ffns,
    counts,
):
    unit_rows, second_rows, out_rows, small_rows, part = counts
    devices = arrived.shape[0]
    cuts = [0]
    for count in (unit_rows, second_rows, unit_rows, out_rows, small_rows):
        cuts.append(cuts[-1] + count)
    later = cuts[-1]
    total = jnp.sum(arrived[:, later:], axis=0)
    first_qkv, tail = total[: 3 * part], total[3 * part :]
    blocks = []
    for f in range(ffns):
        block = arrived[f, :later]
        for device in range(f + ffns, devices, ffns):
            block = block + arrived[device, :later]
        blocks.append(block)
    gain, shift = tail[part : part + 1], tail[part + 1 : part + 2]
    lanes = lax.broadcasted_iota(jnp.int32, (part, WIDTH), 1)
    mine = lax.axis_index(AXES) * part + lax.broadcasted_iota(jnp.int32, (part, WIDTH), 0)
    live_sum = jnp.sum(jnp.where(lanes == mine, stats[3:4], 0.0), axis=1, keepdims=True)
    grad_w_vfe = stats[2:3] * bn_gain[0:1] * (
        tail[:part] - (hat_product[:part] * gain + live_sum * shift) / stats[0:1]
    )
    rows = jnp.concatenate(
        [block[cuts[at] : cuts[at + 1]] for at in (1, 3, 4) for block in blocks] + [first_qkv, grad_w_vfe],
        axis=0,
    )
    room = returned.shape[1] - 4 * unit_rows
    if rows.shape[0] < room:
        rows = jnp.concatenate([rows, jnp.zeros((room - rows.shape[0], WIDTH), F32)], axis=0)
    returned[:, 4 * unit_rows :] = jnp.broadcast_to(rows[None], (devices // 2,) + rows.shape)
    for chip in range(devices // 2):
        f = 2 * chip % ffns
        for at, block in enumerate((blocks[f], blocks[f + 1])):
            returned[chip, at * unit_rows : (at + 1) * unit_rows] = block[: cuts[1]]
            returned[chip, (2 + at) * unit_rows : (3 + at) * unit_rows] = block[cuts[2] : cuts[3]]
    vfe_grads[...] = jnp.concatenate([gain, shift, jnp.zeros((6, WIDTH), F32)], axis=0)
    hat = (lifted_ref[...] - stats[1:2]) * stats[2:3]
    grad = affine[...] - live_column(occupied_ref) * (hat * gain + shift) / stats[0:1]
    grad = stats[2:3] * bn_gain[0:1] * grad
    grad_feats[...] = product(nt, halves(grad), halves(weight_ref[...]))


def last_kernel(
    returned,
    vfe_grads,
    neck,
    grad_w_vfe,
    grad_bn_gain,
    grad_bn_shift,
    grad_w_qkv,
    grad_w_out,
    grad_w_in,
    grad_b_in,
    grad_w_back,
    grad_b_back,
    grad_ln_gain,
    grad_ln_shift,
    *,
    ffns,
):
    devices = 2 * returned.shape[1]
    units = grad_w_in.shape[1]
    at = 0

    def take(count):
        nonlocal at
        rows = joined_rows(returned, at, count)
        at += share_of(count, devices)
        return rows

    mine = ffn_index(ffns)
    core = lax.rem(mine, 2)
    blocks = []
    for layer in range(2):
        pair = take(2 * units), take(2 * units)
        blocks.append(jnp.where(core == 0, *pair))

    def take_blocks(count):
        return jnp.concatenate([take(count) for f in range(ffns)], axis=0)

    for layer in (1, 0):
        grad_w_in[layer] = blocks[1 - layer][:units]
        grad_w_back[layer] = blocks[1 - layer][units:]
    rows = take_blocks(4 * WIDTH // ffns)
    for block in range(3):
        grad_w_qkv[1, :, block * WIDTH : (block + 1) * WIDTH] = rows[block * WIDTH : (block + 1) * WIDTH]
    grad_w_out[1] = rows[3 * WIDTH :]
    grad_w_out[0] = take_blocks(WIDTH // ffns)
    smalls = take_blocks(16 // ffns)
    for block in range(3):
        grad_w_qkv[0, :, block * WIDTH : (block + 1) * WIDTH] = take(WIDTH)
    for layer in range(2):
        small = smalls[layer * 8 : (layer + 1) * 8]
        grad_b_back[layer : layer + 1] = small[0:1]
        grad_ln_gain[2 * layer : 2 * layer + 1] = small[1:2]
        grad_ln_shift[2 * layer : 2 * layer + 1] = small[2:3]
        grad_ln_gain[2 * layer + 1 : 2 * layer + 2] = small[3:4]
        grad_ln_shift[2 * layer + 1 : 2 * layer + 2] = small[4:5]
        held = jnp.zeros((1, units), F32)
        for f in range(ffns):
            row, lane = divmod(f * units, WIDTH)
            held = jnp.where(mine == f, small[5 + row : 6 + row, lane : lane + units], held)
        grad_b_in[layer : layer + 1] = held
    grad_w_vfe[...] = take(WIDTH)
    grad_bn_gain[0:1] = vfe_grads[0:1]
    grad_bn_gain[1:2] = neck[0:1]
    grad_bn_shift[0:1] = vfe_grads[1:2]
    grad_bn_shift[1:2] = neck[1:2]


def spread_rows(pieces, axes):
    return lax.all_to_all(pieces, axes, 0, 0)


def same_core(devices):
    return [list(range(core, devices, 2)) for core in range(2)]


def between_cores(rows, ffns):
    pairs = [[at, at + 1] for at in range(0, ffns, 2)]
    return lax.all_gather(rows, "ffn", axis=0, tiled=False, axis_index_groups=pairs)


def partner(rows, k):
    return lax.ppermute(rows, "ffn", [(i, i ^ k) for i in range(lax.axis_size("ffn"))])


def passed_along(rows, by):
    peers = lax.axis_size(AXES)
    return lax.ppermute(rows, AXES, [(i, (i + by) % peers) for i in range(peers)])


def on_device(
    pillar_feats,
    occupied,
    shifted_source_rows,
    w_vfe,
    bn_gain,
    bn_shift,
    query_key_value_weight,
    attention_output_weight,
    up_weight_matrix,
    up_bias_rows,
    down_weight_matrix,
    down_bias_rows,
    layernorm_gains,
    layernorm_offsets,
    cotangent,
):
    row_count = pillar_feats.shape[0]
    spread = row_count + -(-HALF // 16) * 16
    ffns = lax.axis_size("ffn")
    devices = lax.axis_size(AXES)
    units = up_weight_matrix.shape[2]
    hidden = units * ffns
    windows = row_count // CELLS
    part = share_of(WIDTH, devices)
    piece = share_of(2 * units, devices)
    stats_rows = -(-(4 + part) // 8) * 8
    out_part, small_part = WIDTH // ffns, 16 // ffns
    second_cuts = (2 * units, 4 * WIDTH // ffns)
    first_cuts = (2 * units, out_part, small_part)
    shares = [share_of(count, devices) for count in second_cuts + first_cuts]
    shared_rows = -(-(sum(shares) + 4 * part + 2) // 8) * 8
    returned_rows = -(-(4 * piece + ffns * (shares[1] + shares[3] + shares[4]) + 4 * part) // 8) * 8
    rows_shape = shape(row_count, WIDTH)
    weights_kept = kept(windows, CELLS, HEADS * CELLS, dtype=BF16)
    rows_kept, hidden_kept = kept(row_count, WIDTH), kept(row_count, hidden)
    keeps = [
        rows_kept,
        kept(row_count, 3 * WIDTH),
        weights_kept,
        weights_kept,
        rows_kept,
        rows_kept,
        hidden_kept,
        hidden_kept,
        rows_kept,
        rows_kept,
    ]

    lifted, sent, packed = run(
        vfe_kernel,
        "vfe",
        (rows_shape, shape(devices, stats_rows, WIDTH), shape(4 * units + 8, WIDTH)),
        (
            pillar_feats,
            w_vfe,
            occupied,
            up_weight_matrix.transpose(0, 2, 1),
            down_weight_matrix,
            up_bias_rows,
        ),
    )
    seen = spread_rows(sent, AXES)
    packed = lax.all_gather(packed, "ffn", axis=0, tiled=False)
    weight_dims = (
        [(2, hidden, WIDTH, BF16)] * 4
        + [(2, hidden, F32)]
        + [(2, WIDTH, 3 * WIDTH, BF16)] * 2
        + [(2, WIDTH, WIDTH, BF16)] * 2
    )
    norms = pinned((down_bias_rows, layernorm_gains, layernorm_offsets))
    bn_pair = pinned((bn_gain, bn_shift))
    first_arrays = [rows_kept, rows_kept] + keeps
    outs = run(
        functools.partial(first_kernel, head=True),
        "first",
        [kept(*dims[:-1], dtype=dims[-1]) for dims in weight_dims]
        + [kept(8, WIDTH), kept(8, WIDTH), kept(HALF, 3 * WIDTH)]
        + first_arrays,
        (
            lifted,
            occupied,
            bn_gain,
            bn_shift,
            down_bias_rows,
            layernorm_gains,
            layernorm_offsets,
            Pinned(seen),
            packed,
            query_key_value_weight,
            attention_output_weight,
            Far(cotangent),
        ),
        scratch=[pltpu.VMEM((HALF, WIDTH), F32)],
        copies=1,
        flops=1e9,
    )
    weights, (stats, hat_product, edge) = outs[:9], outs[9:12]
    layer_weights = pinned(weights) + norms
    back_weights = pinned(weights[:4] + weights[5:]) + norms[1:]
    edge = passed_along(edge, -1)
    first_out, *first_keep = run(
        functools.partial(first_kernel, head=False),
        "first_rest",
        first_arrays,
        (
            Pinned(lifted),
            Pinned(occupied),
            *bn_pair,
            *norms,
            Pinned(stats),
            *pinned(weights),
            *pinned(outs[12:]),
        ),
        aliases={17 + at: at for at in range(len(first_arrays))},
        flops=1e9,
    )
    sent, *second_keep = run(
        second_kernel,
        "second",
        [kept(devices, 8, WIDTH), rows_kept, kept(row_count, 1), rows_kept] + keeps,
        (
            Pinned(first_out),
            Pinned(cotangent),
            Pinned(occupied),
            Pinned(edge),
            Pinned(shifted_source_rows),
            *layer_weights,
        ),
        scratch=[pltpu.VMEM((spread, 5 * WIDTH), BF16), pltpu.VMEM((8, WIDTH), F32)],
        flops=2e9,
    )
    seen = spread_rows(sent, AXES)
    second_carried, second_mixed, second_hat, second_hidden = (second_keep[at] for at in (3, 7, 8, 9))
    edge, grad_rows, out_rows, neck, small, *parts = run(
        second_back_kernel,
        "second_back",
        [kept(HALF, 2 * WIDTH), rows_kept, rows_kept, kept(8, WIDTH), kept(8, WIDTH)]
        + [kept(row_count, width, dtype=BF16) for width in (2 * WIDTH, 2 * hidden, 2 * WIDTH, 6 * WIDTH)],
        (Pinned(seen), *bn_pair, Pinned(shifted_source_rows), *back_weights, *pinned(second_keep)),
        flops=4e9,
    )
    edge = passed_along(edge, 1)
    sums = [pltpu.VMEM((hidden, WIDTH), F32)] * 2

    def over_ffn(quarters):
        return [quarters[0]] + [partner(quarters[k], k) for k in range(1, ffns)]

    second_quarters = run(
        functools.partial(second_sums_kernel, ffns=ffns),
        "second_sums",
        [kept(sum(second_cuts), WIDTH)] * ffns,
        (*norms[1:], *pinned((second_carried, second_mixed, second_hat, second_hidden, *parts))),
        scratch=sums + [pltpu.VMEM((ffns, second_cuts[1], WIDTH), F32)],
        flops=1e9,
    )
    second_quarters = over_ffn(second_quarters)
    first_others = -(-(out_part + small_part) // 8) * 8
    grad_joined, grad_mixed, pillars_out, *first_quarters = run(
        functools.partial(first_ffn_back_kernel, ffns=ffns),
        "first_ffn_back",
        [rows_kept, rows_kept, Far(rows_shape)] + [kept(2 * units + first_others, WIDTH)] * ffns,
        (*pinned((grad_rows, edge, out_rows, small)), *back_weights[:4], *back_weights[6:], *pinned(first_keep[5:])),
        scratch=[pltpu.VMEM((row_count, WIDTH), F32), pltpu.VMEM((8, WIDTH), F32)]
        + sums
        + [pltpu.VMEM((WIDTH, WIDTH), F32), pltpu.VMEM((ffns, first_others, WIDTH), F32)],
        copies=2,
        flops=2e9,
    )
    first_quarters = over_ffn(first_quarters)
    grad_affine, *late_sums = run(
        first_attention_back_kernel,
        "first_attention_back",
        [rows_kept, kept(WIDTH, 3 * WIDTH), kept(WIDTH, WIDTH), kept(8, WIDTH)],
        pinned(
            (stats, occupied, lifted, pillar_feats, grad_joined, grad_mixed, *weights[5:7], *first_keep[:5])
        ),
        flops=4e9,
    )
    (shared,) = run(
        functools.partial(share_kernel, ffns=ffns, cuts=(second_cuts, first_cuts)),
        "share",
        [kept(devices, shared_rows, WIDTH)],
        pinned((*late_sums, *second_quarters, *first_quarters)),
    )
    arrived = spread_rows(shared, AXES)
    returned, vfe_grads, grad_feats = run(
        functools.partial(relay_kernel, ffns=ffns, counts=(*shares[:2], *shares[3:], part)),
        "relay",
        (kept(devices // 2, returned_rows, WIDTH), kept(8, WIDTH), rows_shape),
        pinned((arrived, hat_product, stats, bn_gain, grad_affine, lifted, occupied, w_vfe)),
    )
    returned = lax.all_to_all(returned, AXES, 0, 0, axis_index_groups=same_core(devices))
    returned = between_cores(returned, ffns)
    grads = list(run(
        functools.partial(last_kernel, ffns=ffns),
        "last",
        (
            shape(WIDTH, WIDTH),
            shape(2, WIDTH),
            shape(2, WIDTH),
            shape(2, WIDTH, 3 * WIDTH),
            shape(2, WIDTH, WIDTH),
            shape(2, units, WIDTH),
            shape(2, units),
            shape(2, units, WIDTH),
            shape(2, WIDTH),
            shape(4, WIDTH),
            shape(4, WIDTH),
        ),
        pinned((returned, vfe_grads, neck)),
    ))
    grads[5] = grads[5].transpose(0, 2, 1)
    return (pillars_out, grad_feats, *grads)


def solution(mesh):
    return jax.shard_map(
        on_device,
        mesh=mesh,
        in_specs=(
            P(("win", "ffn"), None),
            P(("win", "ffn")),
            P(("win", "ffn")),
            P(),
            P(),
            P(),
            P(),
            P(),
            P(None, None, "ffn"),
            P(None, "ffn"),
            P(None, "ffn", None),
            P(),
            P(),
            P(),
            P(("win", "ffn"), None),
        ),
        out_specs=(
            P(("win", "ffn"), None),
            P(("win", "ffn"), None),
            P(),
            P(),
            P(),
            P(),
            P(),
            P(None, None, "ffn"),
            P(None, "ffn"),
            P(None, "ffn", None),
            P(),
            P(),
            P(),
        ),
        check_vma=False,
    )
```

```python
import functools

import jax
import jax.numpy as jnp
from jax import lax
from jax.experimental import pallas as pl
from jax.experimental.pallas import tpu as pltpu
from jax.sharding import PartitionSpec as P

HEADS = 8
CELLS = 144
HALF = CELLS // 2
WIDTH = 128
EPS_NORM = 1e-05
NEG_FILL = -1000000000.0
AXES = ("win", "ffn")
STEP = 6 * CELLS
HEAD = 2 * CELLS
TILE_ROWS = WIDTH // HEADS
TILES = CELLS // TILE_ROWS
CHUNKS = ((0, 2), (2, 4), (4, 6), (6, 8), (8, 9))
F32 = jnp.float32
BF16 = jnp.bfloat16
VMEM_LIMIT = 28 * 1024 * 1024


def shape(*dims, dtype=F32):
    return pltpu.HBM(dims, dtype)


def kept(*dims, dtype=F32):
    return pltpu.VMEM(dims, dtype)


class Pinned:
    def __init__(self, value):
        self.value = value


class Far:
    def __init__(self, value):
        self.value = value


def run(kernel, name, outs, args, scratch=(), copies=0, aliases=None, flops=1e8):
    near, far = pl.BlockSpec(memory_space=pltpu.VMEM), pl.BlockSpec(memory_space=pltpu.HBM)
    values = []
    for arg in args:
        space = pltpu.VMEM if isinstance(arg, Pinned) else pltpu.HBM
        value = arg.value if isinstance(arg, (Pinned, Far)) else arg
        values.append(pltpu.with_memory_space_constraint(value, space))
    scratch = list(scratch)
    if copies:
        scratch.append(pltpu.SemaphoreType.DMA((copies,)))
    return pl.pallas_call(
        kernel,
        out_shape=[out.value if isinstance(out, Far) else out for out in outs],
        in_specs=[far if isinstance(arg, Far) else near for arg in args],
        out_specs=[far if isinstance(out, Far) else near for out in outs],
        scratch_shapes=scratch,
        input_output_aliases=aliases or {},
        compiler_params=pltpu.CompilerParams(vmem_limit_bytes=VMEM_LIMIT),
        cost_estimate=pl.CostEstimate(flops=int(flops), bytes_accessed=1000000, transcendentals=0),
        name=name,
    )(*values)


def pinned(values):
    return [Pinned(value) for value in values]


class Copies:
    def __init__(self, semaphores):
        self.semaphores = semaphores
        self.started = []

    def start(self, source, target):
        copy = pltpu.make_async_copy(source, target, self.semaphores.at[len(self.started)])
        copy.start()
        self.started.append(copy)
        return copy


def scratch_like(arrays):
    return [pltpu.VMEM(array.shape, array.dtype) for array in arrays]


def ffn_index(ffns):
    return lax.rem(lax.axis_index(AXES), ffns)


def share_of(rows, devices):
    return -(-rows // devices)


def halves(values):
    high = values.astype(BF16)
    return high, (values - high.astype(F32)).astype(BF16)


def nn(former, latter):
    return lax.dot_general(former, latter, (((1,), (0,)), ((), ())), preferred_element_type=F32)


def nt(former, latter):
    return lax.dot_general(former, latter, (((1,), (1,)), ((), ())), preferred_element_type=F32)


def tn(former, latter):
    return lax.dot_general(former, latter, (((0,), (0,)), ((), ())), preferred_element_type=F32)


def product(kind, former, latter):
    columns = latter[0].shape[0 if kind is nt else 1]
    if columns == WIDTH:
        both = kind(former[0], jnp.concatenate(latter, axis=0 if kind is nt else 1))
        return both[:, :columns] + (both[:, columns:] + kind(former[1], latter[0]))
    if kind is tn:
        rows = former[0].shape[1]
        both = kind(jnp.concatenate(former, axis=1), latter[0])
        return both[:rows] + (both[rows:] + kind(former[0], latter[1]))
    if former[0].shape[1] == WIDTH:
        twice = jnp.concatenate([latter[0]] * 2, axis=1 if kind is nt else 0)
        return kind(jnp.concatenate(former, axis=1), twice) + kind(former[0], latter[1])
    return kind(former[0], latter[0]) + (kind(former[0], latter[1]) + kind(former[1], latter[0]))


def thirds(values):
    high = values.astype(BF16)
    rest = values - high.astype(F32)
    middle = rest.astype(BF16)
    return high, middle, (rest - middle.astype(F32)).astype(BF16)


def sharp_product(former, latter):
    upper = jnp.concatenate(former[:2], axis=1)
    outer = jnp.concatenate([former[0], former[2]], axis=1)
    small = nn(upper, jnp.concatenate([latter[1]] * 2, axis=0)) + nn(
        outer, jnp.concatenate([latter[2], latter[0]], axis=0)
    )
    return nn(upper, jnp.concatenate([latter[0]] * 2, axis=0)) + small


def gelu_parts(values):
    below = 0.5 * (1.0 + lax.erf(values * 0.7071067811865476))
    density = 0.3989422804014327 * jnp.exp(-0.5 * values * values)
    return values * below, below + values * density


def normed_rows(values):
    center = jnp.mean(values, axis=-1, keepdims=True)
    moved = values - center
    rate = lax.rsqrt(jnp.mean(moved * moved, axis=-1, keepdims=True) + EPS_NORM)
    return moved * rate, rate


def normed_back(grad, hat, rate, gain):
    scaled = grad * gain
    first = jnp.mean(scaled, axis=-1, keepdims=True)
    second = jnp.mean(scaled * hat, axis=-1, keepdims=True)
    return rate * (scaled - first - hat * second)


def live_column(occupied_ref):
    row = occupied_ref[...].astype(F32).reshape(1, occupied_ref.shape[0])
    return jnp.broadcast_to(row, (8, row.shape[1])).T[:, :1]


def column_sum(values):
    return jnp.sum(values, axis=0, keepdims=True)


def head_mask():
    dims = (HEADS, TILE_ROWS, WIDTH)
    lane_head = lax.broadcasted_iota(jnp.int32, dims, 2) // TILE_ROWS
    return (lane_head == lax.broadcasted_iota(jnp.int32, dims, 0)).astype(F32)


def per_head(rows, mask):
    count = rows.shape[0] // TILE_ROWS
    return (rows.reshape(count, 1, TILE_ROWS, WIDTH) * mask[None]).reshape(count * WIDTH, WIDTH)


def from_heads(table, mask):
    parts = []
    for at in range(0, table.shape[1], WIDTH):
        turned = table[:, at : at + WIDTH].T.reshape(HEADS, TILE_ROWS, WIDTH)
        parts.append(jnp.sum(turned * mask, axis=0))
    return parts


def high_and_low(values):
    high, low = halves(values.T)
    return jnp.concatenate([high, low], axis=0), high


def stacked_product(stack, high_alone, weights):
    both = nn(stack, weights[0])
    return both[:WIDTH] + (both[WIDTH:] + nn(high_alone, weights[1]))


def window_mix(query, key, value, live, mask, mask_low, keep_high, keep_low):
    query_high, query_low = halves(query)
    key_high, key_low = halves(key)
    key_stack = jnp.concatenate([key_high, key_low, key_high], axis=1)
    turned = high_and_low(value)
    mixed = []
    for first, last in CHUNKS:
        rows = slice(first * TILE_ROWS, last * TILE_ROWS)
        lanes = slice(first * WIDTH, last * WIDTH)
        high = per_head(query_high[rows], mask_low)
        low = per_head(query_low[rows], mask_low)
        scores = nt(key_stack, jnp.concatenate([high, high, low], axis=1))
        scores = jnp.where(live > 0, scores, NEG_FILL)
        weights = jnp.exp(scores - jnp.max(scores, axis=0, keepdims=True))
        weights = weights * (1.0 / column_sum(weights))
        weights = halves(weights)
        keep_high[:, lanes] = weights[0]
        keep_low[:, lanes] = weights[1]
        mixed += from_heads(stacked_product(*turned, weights), mask)
    return jnp.concatenate(mixed, axis=0)


def window_back(query, key, value, grad_mixed, live, mask, mask_low, high, low):
    query_high, query_low = (per_head(part, mask_low) for part in halves(query))
    grad_high, grad_low = (per_head(part, mask_low) for part in halves(grad_mixed))
    value_high, value_low = halves(value)
    value_stack = jnp.concatenate([value_high, value_low, value_high], axis=1)
    grad_weights = nt(value_stack, jnp.concatenate([grad_high, grad_high, grad_low], axis=1))
    weights = high.astype(F32) + low.astype(F32)
    grad_scores = weights * grad_weights
    grad_scores = live * (grad_scores - weights * column_sum(grad_scores))
    scores_high, scores_low = halves(grad_scores)

    def over_queries(upper, lower, high, low):
        both = nn(
            jnp.concatenate([upper, lower], axis=0), jnp.concatenate([high, low], axis=1)
        )
        return both[:CELLS, :WIDTH] + (both[:CELLS, WIDTH:] + both[CELLS:, :WIDTH])

    grad_query = stacked_product(*high_and_low(key), (scores_high, scores_low))
    return (
        0.25 * jnp.concatenate(from_heads(grad_query, mask), axis=0),
        over_queries(scores_high, scores_low, query_high, query_low),
        over_queries(high, low, grad_high, grad_low),
    )


def unpack(packed, qkv_ref, out_ref, up_high, up_low, down_high, down_low, bias, qkv_high, qkv_low, out_high, out_low, qkv_least):
    ffns = packed.shape[0]
    units = bias.shape[1] // ffns
    for one in range(2):
        for at in range(ffns):
            rows = slice(at * units, (at + 1) * units)
            high, low = halves(packed[at, one * units : (one + 1) * units])
            up_high[one, rows], up_low[one, rows] = high, low
            high, low = halves(packed[at, (2 + one) * units : (3 + one) * units])
            down_high[one, rows], down_low[one, rows] = high, low
        bias[one : one + 1] = jnp.concatenate(
            [packed[at, 4 * units + one : 4 * units + one + 1, :units] for at in range(ffns)], axis=1
        )
    qkv_high[...], qkv_low[...], qkv_least[...] = thirds(qkv_ref[...])
    out_high[...], out_low[...] = halves(out_ref[...])


def layer_rows(one, values, live, weights, saved):
    up_high, up_low, down_high, down_low, bias, qkv_high, qkv_low, out_high, out_low, qkv_least = weights[:10]
    back_bias, gains, offsets = weights[10:]
    packed_keep, high_keep, low_keep, mixed_keep, hat_one, hidden_keep, slope, hat_two, rates = saved
    mask = head_mask()
    mask_low = mask.astype(BF16)
    qkv = sharp_product(thirds(values), (qkv_high[one], qkv_low[one], qkv_least[one]))
    query = 0.25 * qkv[:, :WIDTH]
    packed_keep[:, :WIDTH] = query
    packed_keep[:, WIDTH:] = qkv[:, WIDTH:]
    for at in range(values.shape[0] // CELLS):
        rows = slice(at * CELLS, (at + 1) * CELLS)
        mixed_keep[rows] = window_mix(
            query[rows],
            qkv[rows, WIDTH : 2 * WIDTH],
            qkv[rows, 2 * WIDTH :],
            live[rows],
            mask,
            mask_low,
            high_keep.at[at],
            low_keep.at[at],
        )
    mixed = mixed_keep[...]
    hat, rate = normed_rows(
        values + product(nn, halves(mixed), (out_high[one], out_low[one]))
    )
    hat_one[...] = hat
    first = hat * gains[2 * one : 2 * one + 1] + offsets[2 * one : 2 * one + 1]
    hidden, steep = gelu_parts(
        product(nt, halves(first), (up_high[one], up_low[one])) + bias[one : one + 1]
    )
    hidden_keep[...] = hidden
    slope[...] = steep
    summed = first + product(nn, halves(hidden), (down_high[one], down_low[one])) + back_bias[one : one + 1]
    hat, last_rate = normed_rows(summed)
    hat_two[...] = hat
    lanes = lax.broadcasted_iota(jnp.int32, hat.shape, 1)
    rates[...] = jnp.where(lanes < WIDTH // 2, rate, last_rate)
    return hat * gains[2 * one + 1 : 2 * one + 2] + offsets[2 * one + 1 : 2 * one + 2]


def ffn_rows_back(one, grad, saved, weights, small):
    mixed_keep, hat_one, hidden_keep, slope, hat_two, rates = saved
    up_high, up_low, down_high, down_low, out_high, out_low, gains, offsets = weights
    up, down, out = (up_high[one], up_low[one]), (down_high[one], down_low[one]), (out_high[one], out_low[one])
    hat = hat_two[...]
    grad_summed = normed_back(grad, hat, rates[:, WIDTH - 1 :], gains[2 * one + 1 : 2 * one + 2])
    small[3:4] += column_sum(grad * hat)
    small[4:5] += column_sum(grad)
    small[0:1] += column_sum(grad_summed)
    summed_halves = halves(grad_summed)
    grad_pre = product(nt, summed_halves, down) * slope[...]
    pre_halves = halves(grad_pre)
    hat = hat_one[...]
    bias_sum = column_sum(grad_pre)
    for at in range(bias_sum.shape[1] // WIDTH):
        small[5 + at : 6 + at] += bias_sum[:, at * WIDTH : (at + 1) * WIDTH]
    grad_first = grad_summed + product(nn, pre_halves, up)
    small[1:2] += column_sum(grad_first * hat)
    small[2:3] += column_sum(grad_first)
    grad_joined = normed_back(grad_first, hat, rates[:, 0:1], gains[2 * one : 2 * one + 1])
    joined_halves = halves(grad_joined)
    return grad_joined, product(nt, joined_halves, out), (summed_halves, pre_halves, joined_halves)


def ffn_weights_back(one, saved, norms, parts):
    mixed_keep, hat_one, hidden_keep = saved
    gains, offsets = norms
    summed_halves, pre_halves, joined_halves = parts
    first = hat_one[...] * gains[2 * one : 2 * one + 1] + offsets[2 * one : 2 * one + 1]
    return (
        product(tn, halves(mixed_keep[...]), joined_halves),
        product(tn, pre_halves, halves(first)),
        product(tn, halves(hidden_keep[...]), summed_halves),
    )


def attention_rows_back(one, live, grad_joined, grad_mixed, saved, qkv_weights):
    packed_keep, high_keep, low_keep = saved
    mask = head_mask()
    mask_low = mask.astype(BF16)
    parts = []
    for at in range(grad_joined.shape[0] // CELLS):
        rows = slice(at * CELLS, (at + 1) * CELLS)
        parts.append(
            window_back(
                packed_keep[rows, :WIDTH],
                packed_keep[rows, WIDTH : 2 * WIDTH],
                packed_keep[rows, 2 * WIDTH :],
                grad_mixed[rows],
                live[rows],
                mask,
                mask_low,
                high_keep[at],
                low_keep[at],
            )
        )
    grad_packed = halves(
        jnp.concatenate([jnp.concatenate(part, axis=1) for part in parts], axis=0)
    )
    return grad_joined + product(nt, grad_packed, (qkv_weights[0][one], qkv_weights[1][one])), grad_packed


def share_rows(target, at, values, devices):
    count = values.shape[0]
    share = share_of(count, devices)
    for device in range(devices):
        begin = device * share
        if begin < count:
            held = min(share, count - begin)
            target[device, at : at + held] = values[begin : begin + held]
    return at + share


def joined_rows(table, at, count):
    devices = 2 * table.shape[1]
    share = share_of(count, devices)
    pieces = []
    for device in range(devices):
        begin = device * share
        if begin < count:
            pieces.append(table[device % 2, device // 2, at : at + min(share, count - begin)])
    return jnp.concatenate(pieces, axis=0)


def vfe_kernel(
    feats_ref, weight_ref, occupied_ref, up_ref, down_ref, bias_ref, lifted_ref, sent_ref, packed_ref
):
    devices = sent_ref.shape[0]
    units = up_ref.shape[1]
    feats = feats_ref[...]
    feats_halves = halves(feats)
    lifted = sharp_product(thirds(feats), thirds(weight_ref[...]))
    lifted_ref[...] = lifted
    live = live_column(occupied_ref)
    count = jnp.sum(live, axis=0, keepdims=True)
    total = column_sum(live * lifted)
    moved = live * (lifted - total / jnp.maximum(count, 1.0))
    sent_ref[...] = jnp.zeros(sent_ref.shape, F32)
    stats = jnp.concatenate(
        [
            jnp.broadcast_to(count, (1, WIDTH)),
            total,
            column_sum(moved * moved),
            column_sum(live * feats),
        ],
        axis=0,
    )
    sent_ref[:, 0:4] = jnp.broadcast_to(stats[None], (devices, 4, WIDTH))
    share_rows(sent_ref, 4, product(tn, feats_halves, halves(moved)), devices)
    for one in range(2):
        packed_ref[one * units : (one + 1) * units] = up_ref[one]
        packed_ref[(2 + one) * units : (3 + one) * units] = down_ref[one]
    packed_ref[4 * units :] = jnp.zeros((8, WIDTH), F32)
    packed_ref[4 * units : 4 * units + 2, :units] = bias_ref[...]


def places_of(source_ref):
    row_count = source_ref.shape[0]
    places = source_ref[...].reshape(1, row_count) - lax.axis_index(AXES) * row_count
    return jnp.where(places < 0, places + row_count * lax.axis_size(AXES), places)


def one_hot(former, latter):
    return (former == latter).astype(F32).astype(BF16)


def vfe_stats(seen_ref, stats_ref, product_ref):
    counts, totals, squares, lives = (seen_ref[:, at] for at in range(4))
    count = column_sum(counts)
    center = column_sum(totals) / count
    moves = totals / jnp.maximum(counts, 1.0) - center
    rate = lax.rsqrt(column_sum(squares + counts * moves * moves) / count + EPS_NORM)
    stats_ref[...] = jnp.zeros(stats_ref.shape, F32)
    stats_ref[0:1] = count
    stats_ref[1:2] = center
    stats_ref[2:3] = rate
    stats_ref[3:4] = column_sum(lives)
    devices = seen_ref.shape[0]
    share = share_of(WIDTH, devices)
    mine = lax.axis_index(AXES) * share
    lanes = lax.broadcasted_iota(jnp.int32, lives.shape, 1)
    product_ref[...] = jnp.zeros(product_ref.shape, F32)
    for at in range(share):
        picked = jnp.sum(jnp.where(lanes == mine + at, lives, 0.0), axis=1, keepdims=True)
        product_ref[at : at + 1] = rate * column_sum(seen_ref[:, 4 + at] + picked * moves)


def rows_in(refs, begin, end):
    return [
        ref.at[begin // CELLS : end // CELLS] if len(ref.shape) == 3 else ref.at[begin:end]
        for ref in refs
    ]


def step_of(refs, step):
    return rows_in(refs, step * STEP, (step + 1) * STEP)


def first_kernel(*refs, head):
    lifted_ref, occupied_ref, bn_gain, bn_shift, back_bias, gains, offsets = refs[:7]
    if head:
        seen_ref, packed, qkv_ref, out_ref, cotangent_ref = refs[7:12]
        weights = refs[12:22]
        stats, hat_product, edge = refs[22:25]
        arrays = refs[25:37]
        cotangent, semaphores = refs[37:]
        copies = Copies(semaphores)
        arrival = copies.start(cotangent_ref.at[:HALF], cotangent)
        unpack(packed, qkv_ref, out_ref, *weights)
        vfe_stats(seen_ref, stats, hat_product)
        rows = slice(0, HEAD)
    else:
        stats = refs[7]
        weights = refs[8:18]
        arrays = refs[18 + (len(refs) - 18) // 2 :]
        rows = slice(HEAD, lifted_ref.shape[0])
    result, vfe_slope, carried, *saved = rows_in(arrays, rows.start, rows.stop)
    hat = (lifted_ref[rows] - stats[1:2]) * stats[2:3]
    values, steep = gelu_parts(hat * bn_gain[0:1] + bn_shift[0:1])
    vfe_slope[...] = steep
    carried[...] = values
    live = live_column(occupied_ref)[rows]
    rows = layer_rows(0, values, live, (*weights, back_bias, gains, offsets), saved)
    result[...] = rows
    if head:
        arrival.wait()
        edge[:, :WIDTH] = rows[:HALF]
        edge[:, WIDTH : 2 * WIDTH] = cotangent[...]
        edge[:, 2 * WIDTH :] = jnp.broadcast_to(live[:HALF], (HALF, WIDTH))


def second_kernel(first_ref, cotangent_ref, occupied_ref, edge, source_ref, *refs):
    weights = refs[:13]
    sent = refs[13]
    arrays = refs[14:-2]
    table, sums = refs[-2:]
    row_count = cotangent_ref.shape[0]
    high, low = halves(first_ref[...])
    table[:row_count, :WIDTH] = high
    table[:row_count, WIDTH : 2 * WIDTH] = low
    high, low = halves(cotangent_ref[...])
    table[:row_count, 2 * WIDTH : 3 * WIDTH] = high
    table[:row_count, 3 * WIDTH : 4 * WIDTH] = low
    table[:row_count, 4 * WIDTH :] = jnp.broadcast_to(live_column(occupied_ref), (row_count, WIDTH)).astype(BF16)
    spare = table.shape[0] - row_count
    tail = jnp.concatenate([edge[...], jnp.zeros((spare - HALF, 3 * WIDTH), F32)], axis=0)
    high, low = halves(tail)
    table[row_count:, :WIDTH] = high[:, :WIDTH]
    table[row_count:, WIDTH : 2 * WIDTH] = low[:, :WIDTH]
    table[row_count:, 2 * WIDTH : 3 * WIDTH] = high[:, WIDTH : 2 * WIDTH]
    table[row_count:, 3 * WIDTH : 4 * WIDTH] = low[:, WIDTH : 2 * WIDTH]
    table[row_count:, 4 * WIDTH :] = high[:, 2 * WIDTH :]
    places = jnp.broadcast_to(places_of(source_ref).astype(F32), (8, row_count))
    column = places.T[:, :1].astype(jnp.int32)
    lanes = lax.broadcasted_iota(jnp.int32, (STEP, table.shape[0]), 1)
    for step in range(row_count // STEP):
        result, live_keep, cotangent_keep, carried, *saved = step_of(arrays, step)
        gathered = nn(one_hot(lanes, column[step * STEP : (step + 1) * STEP]), table[...])
        values = gathered[:, :WIDTH] + gathered[:, WIDTH : 2 * WIDTH]
        live = gathered[:, 4 * WIDTH :]
        grad = live * (gathered[:, 2 * WIDTH : 3 * WIDTH] + gathered[:, 3 * WIDTH : 4 * WIDTH])
        carried[...] = values
        cotangent_keep[...] = grad
        live_keep[...] = live[:, :1]
        rows = layer_rows(1, values, live[:, :1], weights, saved)
        result[...] = rows
        count = column_sum(live)
        if step == 0:
            sums[...] = jnp.zeros(sums.shape, F32)
            sums[5:6] = column_sum(live * rows) / jnp.maximum(count, 1.0)
        moved = rows - sums[5:6]
        sums[0:1] += count
        sums[1:2] += column_sum(live * moved)
        sums[2:3] += column_sum(live * moved * moved)
        sums[3:4] += column_sum(grad)
        sums[4:5] += column_sum(grad * moved)
    count = sums[0:1]
    move = sums[1:2] / jnp.maximum(count, 1.0)
    stats = jnp.concatenate(
        [
            count,
            sums[5:6] + move,
            sums[2:3] - count * move * move,
            sums[3:4],
            sums[4:5] - move * sums[3:4],
            jnp.zeros((3, WIDTH), F32),
        ],
        axis=0,
    )
    sent[...] = jnp.broadcast_to(stats[None], sent.shape)


def second_back_kernel(seen_ref, bn_gain, bn_shift, source_ref, *refs):
    weights = refs[:10]
    arrays = refs[10:23]
    edge, grad_rows, out_rows, neck, small, summed_keep, pre_keep, joined_keep, packed_back = refs[23:]
    row_count = out_rows.shape[0]
    counts, means, squares, grads, products = (seen_ref[:, row] for row in range(5))
    count = column_sum(counts)
    center = column_sum(counts * means) / count
    moves = means - center
    rate = lax.rsqrt(column_sum(squares + counts * moves * moves) / count + EPS_NORM)
    gain_grad = rate * column_sum(products + moves * grads)
    shift_grad = column_sum(grads)
    neck[...] = jnp.concatenate([gain_grad, shift_grad, jnp.zeros((6, WIDTH), F32)], axis=0)
    small[...] = jnp.zeros(small.shape, F32)
    places = places_of(source_ref)
    down = lax.broadcasted_iota(jnp.int32, (-(-(row_count + HALF) // 8) * 8, STEP), 0)
    placed = None
    for step in range(row_count // STEP):
        rows = slice(step * STEP, (step + 1) * STEP)
        result, live_keep, cotangent_keep, carried, packed_keep, high_keep, low_keep, *keeps = step_of(arrays, step)
        live = live_keep[...]
        hat = (result[...] - center) * rate
        neck_rows = live * (hat * bn_gain[1:2] + bn_shift[1:2])
        grad = rate * bn_gain[1:2] * (
            cotangent_keep[...] - live * (hat * gain_grad + shift_grad) / count
        )
        grad_joined, grad_mixed, parts = ffn_rows_back(1, grad, keeps, weights[:4] + weights[6:10], small)
        grad_values, grad_packed = attention_rows_back(
            1, live, grad_joined, grad_mixed, (packed_keep, high_keep, low_keep), weights[4:6]
        )
        for kept_halves, part in zip((summed_keep, pre_keep, joined_keep, packed_back), (*parts, grad_packed)):
            kept_halves[rows] = jnp.concatenate(part, axis=1)
        pieces = jnp.concatenate(halves(grad_values) + halves(neck_rows), axis=1)
        moved = nn(one_hot(down, places[:, rows]), pieces)
        moved = jnp.concatenate(
            [
                moved[:, :WIDTH] + moved[:, WIDTH : 2 * WIDTH],
                moved[:, 2 * WIDTH : 3 * WIDTH] + moved[:, 3 * WIDTH :],
            ],
            axis=1,
        )
        placed = moved if placed is None else placed + moved
    grad_rows[...] = placed[:row_count, :WIDTH]
    out_rows[...] = placed[:row_count, WIDTH:]
    edge[...] = placed[row_count : row_count + HALF]


def quarter_rows(target, number, sum_up, sum_down, others):
    ffns = others.shape[0]
    units = sum_up.shape[0] // ffns
    rows = pl.ds(pl.multiple_of(number * units, units), units)
    target[:units] = sum_up[rows]
    target[units : 2 * units] = sum_down[rows]
    target[2 * units :] = others[number]


def second_sums_kernel(*refs, ffns):
    gains, offsets, carried, mixed_keep, hat_one, hidden_keep = refs[:6]
    quarters = refs[10 : 10 + ffns]
    sum_up, sum_down, others = refs[10 + ffns :]
    parts = []
    for ref in refs[6:10]:
        half = ref.shape[1] // 2
        parts.append((ref[:, :half], ref[:, half:]))
    out, sum_up[...], sum_down[...] = ffn_weights_back(
        1, (mixed_keep, hat_one, hidden_keep), (gains, offsets), parts[:3]
    )
    qkv = product(tn, halves(carried[...]), parts[3])
    blocks = [qkv[:, at * WIDTH : (at + 1) * WIDTH] for at in range(3)] + [out]
    others[...] = jnp.concatenate(blocks, axis=0).reshape(others.shape)
    for k, quarter in enumerate(quarters):
        quarter_rows(quarter, ffn_index(ffns) ^ k, sum_up, sum_down, others)


def first_ffn_back_kernel(grad_rows, edge, out_rows, small_second, *refs, ffns):
    weights, keeps = refs[:8], refs[8:14]
    joined_keep, mixed_keep, pillars = refs[14:17]
    quarters = refs[17 : 17 + ffns]
    grad, small, sum_up, sum_down, sum_out, others, semaphores = refs[17 + ffns :]
    copies = Copies(semaphores)
    copies.start(edge.at[:, WIDTH:], pillars.at[:HALF])
    copies.start(out_rows.at[HALF:], pillars.at[HALF:])
    small[...] = jnp.zeros(small.shape, F32)
    grad[HALF:] = grad_rows[HALF:]
    grad[:HALF] = edge[:, :WIDTH]
    for step in range(grad.shape[0] // STEP):
        rows = slice(step * STEP, (step + 1) * STEP)
        saved = step_of(keeps, step)
        joined_keep[rows], mixed_keep[rows], parts = ffn_rows_back(0, grad[rows], saved, weights, small)
        made = ffn_weights_back(0, (saved[0], saved[1], saved[2]), weights[6:8], parts)
        for held, part in zip((sum_out, sum_up, sum_down), made):
            held[...] = held[...] + part if step else part
    part, few = WIDTH // ffns, 2 * small.shape[0] // ffns
    smalls = jnp.concatenate([small[...], small_second[...]], axis=0)
    others[...] = jnp.zeros(others.shape, F32)
    for number in range(ffns):
        others[number, :part] = sum_out[number * part : (number + 1) * part]
        others[number, part : part + few] = smalls[number * few : (number + 1) * few]
    for k, quarter in enumerate(quarters):
        quarter_rows(quarter, ffn_index(ffns) ^ k, sum_up, sum_down, others)
    for copy in copies.started:
        copy.wait()


def first_attention_back_kernel(*refs):
    stats, occupied_ref, lifted_ref, feats_ref, joined_keep, mixed_keep = refs[:6]
    qkv_weights, arrays = refs[6:8], refs[8:13]
    grad_affine, sum_qkv, sum_feats, small = refs[13:]
    live = live_column(occupied_ref)
    small[...] = jnp.zeros(small.shape, F32)
    for step in range(live.shape[0] // STEP):
        rows = slice(step * STEP, (step + 1) * STEP)
        vfe_slope, carried, *saved = step_of(arrays, step)
        grad, grad_packed = attention_rows_back(0, live[rows], joined_keep[rows], mixed_keep[rows], saved, qkv_weights)
        grad = grad * vfe_slope[...]
        grad_affine[rows] = grad
        small[0:1] += column_sum(grad * (lifted_ref[rows] - stats[1:2]) * stats[2:3])
        small[1:2] += column_sum(grad)
        for held, part in (
            (sum_qkv, product(tn, halves(carried[...]), grad_packed)),
            (sum_feats, product(tn, halves(feats_ref[rows]), halves(grad))),
        ):
            held[...] = held[...] + part if step else part


def share_kernel(sum_qkv, sum_feats, small, *refs, ffns, cuts):
    shared = refs[2 * ffns]
    devices = shared.shape[0]
    shared[...] = jnp.zeros(shared.shape, F32)
    row = 0
    for layer, counts in enumerate(cuts):
        quarters = refs[layer * ffns : (layer + 1) * ffns]
        total = quarters[0][...]
        for other in quarters[1:]:
            total = total + other[...]
        begin = 0
        for count in counts:
            row = share_rows(shared, row, total[begin : begin + count], devices)
            begin += count
    for block in range(3):
        row = share_rows(shared, row, sum_qkv[:, block * WIDTH : (block + 1) * WIDTH], devices)
    row = share_rows(shared, row, sum_feats[...], devices)
    shared[:, row : row + 2] = jnp.broadcast_to(small[0:2][None], (devices, 2, WIDTH))


def relay_kernel(
    arrived,
    hat_product,
    stats,
    bn_gain,
    affine,
    lifted_ref,
    occupied_ref,
    weight_ref,
    returned,
    vfe_grads,
    grad_feats,
    *,
    ffns,
    counts,
):
    unit_rows, second_rows, out_rows, small_rows, part = counts
    devices = arrived.shape[0]
    cuts = [0]
    for count in (unit_rows, second_rows, unit_rows, out_rows, small_rows):
        cuts.append(cuts[-1] + count)
    later = cuts[-1]
    total = jnp.sum(arrived[:, later:], axis=0)
    first_qkv, tail = total[: 3 * part], total[3 * part :]
    blocks = []
    for f in range(ffns):
        block = arrived[f, :later]
        for device in range(f + ffns, devices, ffns):
            block = block + arrived[device, :later]
        blocks.append(block)
    gain, shift = tail[part : part + 1], tail[part + 1 : part + 2]
    lanes = lax.broadcasted_iota(jnp.int32, (part, WIDTH), 1)
    mine = lax.axis_index(AXES) * part + lax.broadcasted_iota(jnp.int32, (part, WIDTH), 0)
    live_sum = jnp.sum(jnp.where(lanes == mine, stats[3:4], 0.0), axis=1, keepdims=True)
    grad_w_vfe = stats[2:3] * bn_gain[0:1] * (
        tail[:part] - (hat_product[:part] * gain + live_sum * shift) / stats[0:1]
    )
    rows = jnp.concatenate(
        [block[cuts[at] : cuts[at + 1]] for at in (1, 3, 4) for block in blocks] + [first_qkv, grad_w_vfe],
        axis=0,
    )
    room = returned.shape[1] - 4 * unit_rows
    if rows.shape[0] < room:
        rows = jnp.concatenate([rows, jnp.zeros((room - rows.shape[0], WIDTH), F32)], axis=0)
    returned[:, 4 * unit_rows :] = jnp.broadcast_to(rows[None], (devices // 2,) + rows.shape)
    for chip in range(devices // 2):
        f = 2 * chip % ffns
        for at, block in enumerate((blocks[f], blocks[f + 1])):
            returned[chip, at * unit_rows : (at + 1) * unit_rows] = block[: cuts[1]]
            returned[chip, (2 + at) * unit_rows : (3 + at) * unit_rows] = block[cuts[2] : cuts[3]]
    vfe_grads[...] = jnp.concatenate([gain, shift, jnp.zeros((6, WIDTH), F32)], axis=0)
    hat = (lifted_ref[...] - stats[1:2]) * stats[2:3]
    grad = affine[...] - live_column(occupied_ref) * (hat * gain + shift) / stats[0:1]
    grad = stats[2:3] * bn_gain[0:1] * grad
    grad_feats[...] = product(nt, halves(grad), halves(weight_ref[...]))


def last_kernel(
    returned,
    vfe_grads,
    neck,
    grad_w_vfe,
    grad_bn_gain,
    grad_bn_shift,
    grad_w_qkv,
    grad_w_out,
    grad_w_in,
    grad_b_in,
    grad_w_back,
    grad_b_back,
    grad_ln_gain,
    grad_ln_shift,
    *,
    ffns,
):
    devices = 2 * returned.shape[1]
    units = grad_w_in.shape[1]
    at = 0

    def take(count):
        nonlocal at
        rows = joined_rows(returned, at, count)
        at += share_of(count, devices)
        return rows

    mine = ffn_index(ffns)
    core = lax.rem(mine, 2)
    blocks = []
    for layer in range(2):
        pair = take(2 * units), take(2 * units)
        blocks.append(jnp.where(core == 0, *pair))

    def take_blocks(count):
        return jnp.concatenate([take(count) for f in range(ffns)], axis=0)

    for layer in (1, 0):
        grad_w_in[layer] = blocks[1 - layer][:units]
        grad_w_back[layer] = blocks[1 - layer][units:]
    rows = take_blocks(4 * WIDTH // ffns)
    for block in range(3):
        grad_w_qkv[1, :, block * WIDTH : (block + 1) * WIDTH] = rows[block * WIDTH : (block + 1) * WIDTH]
    grad_w_out[1] = rows[3 * WIDTH :]
    grad_w_out[0] = take_blocks(WIDTH // ffns)
    smalls = take_blocks(16 // ffns)
    for block in range(3):
        grad_w_qkv[0, :, block * WIDTH : (block + 1) * WIDTH] = take(WIDTH)
    for layer in range(2):
        small = smalls[layer * 8 : (layer + 1) * 8]
        grad_b_back[layer : layer + 1] = small[0:1]
        grad_ln_gain[2 * layer : 2 * layer + 1] = small[1:2]
        grad_ln_shift[2 * layer : 2 * layer + 1] = small[2:3]
        grad_ln_gain[2 * layer + 1 : 2 * layer + 2] = small[3:4]
        grad_ln_shift[2 * layer + 1 : 2 * layer + 2] = small[4:5]
        held = jnp.zeros((1, units), F32)
        for f in range(ffns):
            row, lane = divmod(f * units, WIDTH)
            held = jnp.where(mine == f, small[5 + row : 6 + row, lane : lane + units], held)
        grad_b_in[layer : layer + 1] = held
    grad_w_vfe[...] = take(WIDTH)
    grad_bn_gain[0:1] = vfe_grads[0:1]
    grad_bn_gain[1:2] = neck[0:1]
    grad_bn_shift[0:1] = vfe_grads[1:2]
    grad_bn_shift[1:2] = neck[1:2]


def spread_rows(pieces, axes):
    return lax.all_to_all(pieces, axes, 0, 0)


def same_core(devices):
    return [list(range(core, devices, 2)) for core in range(2)]


def between_cores(rows, ffns):
    pairs = [[at, at + 1] for at in range(0, ffns, 2)]
    return lax.all_gather(rows, "ffn", axis=0, tiled=False, axis_index_groups=pairs)


def partner(rows, k):
    return lax.ppermute(rows, "ffn", [(i, i ^ k) for i in range(lax.axis_size("ffn"))])


def passed_along(rows, by):
    peers = lax.axis_size(AXES)
    return lax.ppermute(rows, AXES, [(i, (i + by) % peers) for i in range(peers)])


def on_device(
    pillar_feats,
    occupied,
    shifted_source_rows,
    w_vfe,
    bn_gain,
    bn_shift,
    query_key_value_weight,
    attention_output_weight,
    up_weight_matrix,
    up_bias_rows,
    down_weight_matrix,
    down_bias_rows,
    layernorm_gains,
    layernorm_offsets,
    cotangent,
):
    row_count = pillar_feats.shape[0]
    spread = row_count + -(-HALF // 16) * 16
    ffns = lax.axis_size("ffn")
    devices = lax.axis_size(AXES)
    units = up_weight_matrix.shape[2]
    hidden = units * ffns
    windows = row_count // CELLS
    part = share_of(WIDTH, devices)
    piece = share_of(2 * units, devices)
    stats_rows = -(-(4 + part) // 8) * 8
    out_part, small_part = WIDTH // ffns, 16 // ffns
    second_cuts = (2 * units, 4 * WIDTH // ffns)
    first_cuts = (2 * units, out_part, small_part)
    shares = [share_of(count, devices) for count in second_cuts + first_cuts]
    shared_rows = -(-(sum(shares) + 4 * part + 2) // 8) * 8
    returned_rows = -(-(4 * piece + ffns * (shares[1] + shares[3] + shares[4]) + 4 * part) // 8) * 8
    rows_shape = shape(row_count, WIDTH)
    weights_kept = kept(windows, CELLS, HEADS * CELLS, dtype=BF16)
    rows_kept, hidden_kept = kept(row_count, WIDTH), kept(row_count, hidden)
    keeps = [
        rows_kept,
        kept(row_count, 3 * WIDTH),
        weights_kept,
        weights_kept,
        rows_kept,
        rows_kept,
        hidden_kept,
        hidden_kept,
        rows_kept,
        rows_kept,
    ]

    lifted, sent, packed = run(
        vfe_kernel,
        "vfe",
        (rows_shape, shape(devices, stats_rows, WIDTH), shape(4 * units + 8, WIDTH)),
        (
            pillar_feats,
            w_vfe,
            occupied,
            up_weight_matrix.transpose(0, 2, 1),
            down_weight_matrix,
            up_bias_rows,
        ),
    )
    seen = spread_rows(sent, AXES)
    packed = lax.all_gather(packed, "ffn", axis=0, tiled=False)
    weight_dims = (
        [(2, hidden, WIDTH, BF16)] * 4
        + [(2, hidden, F32)]
        + [(2, WIDTH, 3 * WIDTH, BF16)] * 2
        + [(2, WIDTH, WIDTH, BF16)] * 2
        + [(2, WIDTH, 3 * WIDTH, BF16)]
    )
    norms = pinned((down_bias_rows, layernorm_gains, layernorm_offsets))
    bn_pair = pinned((bn_gain, bn_shift))
    first_arrays = [rows_kept, rows_kept] + keeps
    outs = run(
        functools.partial(first_kernel, head=True),
        "first",
        [kept(*dims[:-1], dtype=dims[-1]) for dims in weight_dims]
        + [kept(8, WIDTH), kept(8, WIDTH), kept(HALF, 3 * WIDTH)]
        + first_arrays,
        (
            lifted,
            occupied,
            bn_gain,
            bn_shift,
            down_bias_rows,
            layernorm_gains,
            layernorm_offsets,
            Pinned(seen),
            packed,
            query_key_value_weight,
            attention_output_weight,
            Far(cotangent),
        ),
        scratch=[pltpu.VMEM((HALF, WIDTH), F32)],
        copies=1,
        flops=1e9,
    )
    weights, (stats, hat_product, edge) = outs[:10], outs[10:13]
    layer_weights = pinned(weights) + norms
    back_weights = pinned(weights[:4] + weights[5:9]) + norms[1:]
    edge = passed_along(edge, -1)
    first_out, *first_keep = run(
        functools.partial(first_kernel, head=False),
        "first_rest",
        first_arrays,
        (
            Pinned(lifted),
            Pinned(occupied),
            *bn_pair,
            *norms,
            Pinned(stats),
            *pinned(weights),
            *pinned(outs[13:]),
        ),
        aliases={18 + at: at for at in range(len(first_arrays))},
        flops=1e9,
    )
    sent, *second_keep = run(
        second_kernel,
        "second",
        [kept(devices, 8, WIDTH), rows_kept, kept(row_count, 1), rows_kept] + keeps,
        (
            Pinned(first_out),
            Pinned(cotangent),
            Pinned(occupied),
            Pinned(edge),
            Pinned(shifted_source_rows),
            *layer_weights,
        ),
        scratch=[pltpu.VMEM((spread, 5 * WIDTH), BF16), pltpu.VMEM((8, WIDTH), F32)],
        flops=2e9,
    )
    seen = spread_rows(sent, AXES)
    second_carried, second_mixed, second_hat, second_hidden = (second_keep[at] for at in (3, 7, 8, 9))
    edge, grad_rows, out_rows, neck, small, *parts = run(
        second_back_kernel,
        "second_back",
        [kept(HALF, 2 * WIDTH), rows_kept, rows_kept, kept(8, WIDTH), kept(8, WIDTH)]
        + [kept(row_count, width, dtype=BF16) for width in (2 * WIDTH, 2 * hidden, 2 * WIDTH, 6 * WIDTH)],
        (Pinned(seen), *bn_pair, Pinned(shifted_source_rows), *back_weights, *pinned(second_keep)),
        flops=4e9,
    )
    edge = passed_along(edge, 1)
    sums = [pltpu.VMEM((hidden, WIDTH), F32)] * 2

    def over_ffn(quarters):
        return [quarters[0]] + [partner(quarters[k], k) for k in range(1, ffns)]

    second_quarters = run(
        functools.partial(second_sums_kernel, ffns=ffns),
        "second_sums",
        [kept(sum(second_cuts), WIDTH)] * ffns,
        (*norms[1:], *pinned((second_carried, second_mixed, second_hat, second_hidden, *parts))),
        scratch=sums + [pltpu.VMEM((ffns, second_cuts[1], WIDTH), F32)],
        flops=1e9,
    )
    second_quarters = over_ffn(second_quarters)
    first_others = -(-(out_part + small_part) // 8) * 8
    grad_joined, grad_mixed, pillars_out, *first_quarters = run(
        functools.partial(first_ffn_back_kernel, ffns=ffns),
        "first_ffn_back",
        [rows_kept, rows_kept, Far(rows_shape)] + [kept(2 * units + first_others, WIDTH)] * ffns,
        (*pinned((grad_rows, edge, out_rows, small)), *back_weights[:4], *back_weights[6:], *pinned(first_keep[5:])),
        scratch=[pltpu.VMEM((row_count, WIDTH), F32), pltpu.VMEM((8, WIDTH), F32)]
        + sums
        + [pltpu.VMEM((WIDTH, WIDTH), F32), pltpu.VMEM((ffns, first_others, WIDTH), F32)],
        copies=2,
        flops=2e9,
    )
    first_quarters = over_ffn(first_quarters)
    grad_affine, *late_sums = run(
        first_attention_back_kernel,
        "first_attention_back",
        [rows_kept, kept(WIDTH, 3 * WIDTH), kept(WIDTH, WIDTH), kept(8, WIDTH)],
        pinned(
            (stats, occupied, lifted, pillar_feats, grad_joined, grad_mixed, *weights[5:7], *first_keep[:5])
        ),
        flops=4e9,
    )
    (shared,) = run(
        functools.partial(share_kernel, ffns=ffns, cuts=(second_cuts, first_cuts)),
        "share",
        [kept(devices, shared_rows, WIDTH)],
        pinned((*late_sums, *second_quarters, *first_quarters)),
    )
    arrived = spread_rows(shared, AXES)
    returned, vfe_grads, grad_feats = run(
        functools.partial(relay_kernel, ffns=ffns, counts=(*shares[:2], *shares[3:], part)),
        "relay",
        (kept(devices // 2, returned_rows, WIDTH), kept(8, WIDTH), rows_shape),
        pinned((arrived, hat_product, stats, bn_gain, grad_affine, lifted, occupied, w_vfe)),
    )
    returned = lax.all_to_all(returned, AXES, 0, 0, axis_index_groups=same_core(devices))
    returned = between_cores(returned, ffns)
    grads = list(run(
        functools.partial(last_kernel, ffns=ffns),
        "last",
        (
            shape(WIDTH, WIDTH),
            shape(2, WIDTH),
            shape(2, WIDTH),
            shape(2, WIDTH, 3 * WIDTH),
            shape(2, WIDTH, WIDTH),
            shape(2, units, WIDTH),
            shape(2, units),
            shape(2, units, WIDTH),
            shape(2, WIDTH),
            shape(4, WIDTH),
            shape(4, WIDTH),
        ),
        pinned((returned, vfe_grads, neck)),
    ))
    grads[5] = grads[5].transpose(0, 2, 1)
    return (pillars_out, grad_feats, *grads)


def solution(mesh):
    return jax.shard_map(
        on_device,
        mesh=mesh,
        in_specs=(
            P(("win", "ffn"), None),
            P(("win", "ffn")),
            P(("win", "ffn")),
            P(),
            P(),
            P(),
            P(),
            P(),
            P(None, None, "ffn"),
            P(None, "ffn"),
            P(None, "ffn", None),
            P(),
            P(),
            P(),
            P(("win", "ffn"), None),
        ),
        out_specs=(
            P(("win", "ffn"), None),
            P(("win", "ffn"), None),
            P(),
            P(),
            P(),
            P(),
            P(),
            P(None, None, "ffn"),
            P(None, "ffn"),
            P(None, "ffn", None),
            P(),
            P(),
            P(),
        ),
        check_vma=False,
    )
```
